128 devices in a mesh: batch: 4 (over y_lo, core), dap: 32 (over z, x, y_hi).
Axes of the slice: x: 4, y: 4 (y_hi: 2, y_lo: 2; y = y_hi * 2 + y_lo), z: 4, core: 2. Of those that a mesh axis runs over, the one named last changes fastest.
Arguments:
- alignment: bfloat16 [1024, 512, 256], P(('batch', 'dap')), parts along dimension 0, may hold values from -6 to 6
- pair_state: bfloat16 [2048, 512, 128], P(('batch', 'dap')), parts along dimension 0, may hold values from -6 to 6
- row_norm_gain: float32 [256], replicated, may hold values from 0.5 to 1.5
- row_norm_bias: float32 [256], replicated, may hold values from -3 to 3
- pair_norm_gain: float32 [128], replicated, may hold values from 0.25 to 1.75
- pair_weight: bfloat16 [128, 8], replicated, may hold values from -0.5 to 0.5
- row_query: bfloat16 [256, 256], replicated, may hold values from -23 to 23, as said below
- row_key: bfloat16 [256, 256], replicated, may hold values from -0.375 to 0.375, as said below
- row_value: bfloat16 [256, 256], replicated, may hold values from -0.375 to 0.375
- row_gate: bfloat16 [256, 256], replicated, may hold values from -0.375 to 0.375
- row_gate_bias: float32 [256], replicated, may hold values from -4 to 4
- row_output: bfloat16 [256, 256], replicated, may hold values from -0.375 to 0.375
- row_output_bias: float32 [256], replicated, may hold values from -3 to 3
- column_norm_gain: float32 [256], replicated, may hold values from 0.5 to 1.5
- column_norm_bias: float32 [256], replicated, may hold values from -3 to 3
- column_query: bfloat16 [256, 256], replicated, may hold values from -23 to 23, as said below
- column_key: bfloat16 [256, 256], replicated, may hold values from -0.375 to 0.375, as said below
- column_value: bfloat16 [256, 256], replicated, may hold values from -0.375 to 0.375
- column_gate: bfloat16 [256, 256], replicated, may hold values from -0.375 to 0.375
- column_gate_bias: float32 [256], replicated, may hold values from -4 to 4
- column_output: bfloat16 [256, 256], replicated, may hold values from -0.375 to 0.375
- column_output_bias: float32 [256], replicated, may hold values from -3 to 3
Outputs:
- updated: bfloat16 [1024, 512, 256], P(('batch', 'dap')), parts along dimension 0
The draws below stay inside these ranges and needn't reach their ends.
There are 4 independent parts, one for each index of `batch`. The reference program is written for one: setup_inputs(seed, part) draws one part's arguments, and reference() takes and returns one part's arrays. A program takes and returns all parts, laid end to end along the dimension named above; an argument that names none is the same for every part. Nothing has to cross between parts.
Inputs may be any that keep to these rules, and one draw needn't show every extreme that they name: `row_query`: a projection's entries. `row_key`: a projection's entries. `column_query`: a projection's entries. `column_key`: a projection's entries.
All inputs are finite; a program needn't handle non-finite values.
Results may differ from the reference program's by a relative error of at most 0.005.
The reference program's roundings to bfloat16 on the way count: a program that leaves them out, or rounds other values in their place, can miss the bound.
Values may be sent and summed in bfloat16 or wider, within the bound.
No kernel may reach another device: no remote copies, remote signals or barrier semaphores. Data moves between devices by JAX's collectives and lax.ppermute only.
A program may use at most 192 MiB of HBM per device.

```python
import jax
import jax.numpy as jnp
from jax import lax

CM = 256
CZ = 128
H = 8
HEAD = 32
S = 256
R = 512


def shared_weight(key, salt):
    folded = jax.random.fold_in(key, salt)
    normal_values = jax.random.normal(folded, (CM, CM), jnp.float32) / jnp.sqrt(jnp.float32(CM))
    return jnp.clip(normal_values, -0.375, 0.375)


def draw_row_key(key, part):
    return shared_weight(key, 11).astype(jnp.bfloat16)


def draw_row_query(key, part):
    key = jax.random.fold_in(key, 2)
    own = shared_weight(key, 3)
    return own.astype(jnp.bfloat16)


def draw_column_key(key, part):
    return shared_weight(key, 23).astype(jnp.bfloat16)


def draw_column_query(key, part):
    key = jax.random.fold_in(key, 5)
    own = shared_weight(key, 3)
    return own.astype(jnp.bfloat16)


def steps_of(own_key, shape, pieces, low, largest):
    factor_of, own = 1.0, jax.random.fold_in(own_key, 6)
    for dim, shards_of in pieces:
        heights = jnp.exp(jax.random.uniform(jax.random.fold_in(own, dim), (shards_of,), jnp.float32, low / len(pieces), largest / len(pieces)))
        factor_of = factor_of * jnp.repeat(heights, shape[dim] // shards_of).reshape([-1 if axis == dim else 1 for axis in range(len(shape))])
    return factor_of


def gaussian(key, extent, scale, limit, shards=(), held_as=jnp.bfloat16):
    factor_of = steps_of(key, extent, shards, -0.22, 0.18) if shards else 1.0
    result = jax.random.normal(key, extent, jnp.float32) * scale * factor_of
    return jnp.minimum(jnp.maximum(result, -limit), limit).astype(held_as)


def setup_inputs(seed: int = 0, part: int = 0) -> dict:
    arg_keys = jax.random.split(jax.random.key(seed), 23)
    part_splits = jax.random.split(jax.random.fold_in(arg_keys[22], part), 23)
    return {
        "alignment": gaussian(part_splits[0], (S, R, CM), 1.0, 6.0, ((0, 32),)),
        "pair_state": gaussian(part_splits[1], (R, R, CZ), 1.0, 6.0, ((0, 32),)),
        "row_norm_gain": jnp.clip(1.0 + 0.1 * jax.random.normal(arg_keys[2], (CM,), jnp.float32), 0.5, 1.5),
        "row_norm_bias": gaussian(arg_keys[3], (CM,), 0.5, 3.0, (), jnp.float32),
        "pair_norm_gain": jnp.clip(1.0 + 0.15 * jax.random.normal(arg_keys[4], (CZ,), jnp.float32), 0.25, 1.75),
        "pair_weight": gaussian(arg_keys[5], (CZ, H), CZ ** -0.5, 0.5),
        "row_query": draw_row_query(jax.random.fold_in(arg_keys[22], 71), part),
        "row_key": draw_row_key(jax.random.fold_in(arg_keys[22], 71), part),
        "row_value": gaussian(arg_keys[8], (CM, CM), CM ** -0.5, 0.375),
        "row_gate": gaussian(arg_keys[9], (CM, CM), CM ** -0.5, 0.375),
        "row_gate_bias": gaussian(arg_keys[10], (CM,), 1.0, 4.0, (), jnp.float32),
        "row_output": gaussian(arg_keys[11], (CM, CM), CM ** -0.5, 0.375),
        "row_output_bias": gaussian(arg_keys[12], (CM,), 0.5, 3.0, (), jnp.float32),
        "column_norm_gain": jnp.clip(1.0 + 0.1 * jax.random.normal(arg_keys[13], (CM,), jnp.float32), 0.5, 1.5),
        "column_norm_bias": gaussian(arg_keys[14], (CM,), 0.5, 3.0, (), jnp.float32),
        "column_query": draw_column_query(jax.random.fold_in(arg_keys[22], 71), part),
        "column_key": draw_column_key(jax.random.fold_in(arg_keys[22], 71), part),
        "column_value": gaussian(arg_keys[17], (CM, CM), CM ** -0.5, 0.375),
        "column_gate": gaussian(arg_keys[18], (CM, CM), CM ** -0.5, 0.375),
        "column_gate_bias": gaussian(arg_keys[19], (CM,), 1.0, 4.0, (), jnp.float32),
        "column_output": gaussian(arg_keys[20], (CM, CM), CM ** -0.5, 0.375),
        "column_output_bias": gaussian(arg_keys[21], (CM,), 0.5, 3.0, (), jnp.float32),
    }


epsilon = 1e-05

def layer_norm(values, norm_gain, norm_bias):
    values = values.astype(jnp.float32)
    center = lax.optimization_barrier(jnp.mean(values, axis=-1, keepdims=True))
    spread = lax.optimization_barrier(jnp.mean(jnp.square(values - center), axis=-1, keepdims=True))
    return ((values - center) * lax.rsqrt(spread + epsilon) * norm_gain + norm_bias).astype(jnp.bfloat16)

def widen(values):
    return lax.optimization_barrier(values).astype(jnp.float32)

def project_all(normed, query_weight, key_weight, value_weight, gate_weight, gate_bias):
    feature_width = query_weight.shape[1]
    stacked = jnp.concatenate([query_weight, key_weight, value_weight, gate_weight], axis=1)
    flattened = normed.reshape(-1, normed.shape[-1])
    projected = jnp.dot(flattened, stacked, preferred_element_type=jnp.float32)
    lead_shape = normed.shape[:-1] + (feature_width,)
    queries = (projected[:, :feature_width] * HEAD ** (-0.5)).astype(jnp.bfloat16).reshape(lead_shape)
    key_proj = projected[:, feature_width:2 * feature_width].astype(jnp.bfloat16).reshape(lead_shape)
    value_proj = projected[:, 2 * feature_width:3 * feature_width].astype(jnp.bfloat16).reshape(lead_shape)
    gate_proj = jax.nn.sigmoid(projected[:, 3 * feature_width:] + gate_bias).reshape(lead_shape)
    return (queries, key_proj, value_proj, gate_proj)

def head_scores(query_rows, key_rows):
    query_heads = widen(query_rows).reshape(query_rows.shape[0], H, HEAD)
    key_heads = widen(key_rows).reshape(key_rows.shape[0], H, HEAD)
    return jnp.einsum('qhd,khd->hqk', query_heads, key_heads)

def head_average(scores, value_rows):
    weights = widen(jax.nn.softmax(scores, axis=-1).astype(jnp.bfloat16))
    value_heads = widen(value_rows).reshape(value_rows.shape[0], H, HEAD)
    averaged = jnp.einsum('hqk,khd->qhd', weights, value_heads)
    return averaged.reshape(scores.shape[1], H * HEAD)

def output_layer(gated, residual, out_weight, out_bias):
    update = jnp.dot(gated, out_weight, preferred_element_type=jnp.float32) + out_bias
    return (residual.astype(jnp.float32) + update).astype(jnp.bfloat16)

def reference(alignment, pair_state, row_norm_gain, row_norm_bias, pair_norm_gain, pair_weight, row_query, row_key, row_value, row_gate, row_gate_bias, row_output, row_output_bias, column_norm_gain, column_norm_bias, column_query, column_key, column_value, column_gate, column_gate_bias, column_output, column_output_bias):
    pair_normed = layer_norm(pair_state, pair_norm_gain, jnp.zeros_like(pair_norm_gain))
    pair_bias = jnp.einsum('irc,ch->hir', widen(pair_normed), pair_weight.astype(jnp.float32)).astype(jnp.bfloat16)
    bias_wide = widen(pair_bias)
    normed = layer_norm(alignment, row_norm_gain, row_norm_bias)
    queries, key_proj, value_proj, gate_proj = project_all(normed, row_query, row_key, row_value, row_gate, row_gate_bias)

    def one_sequence(parts):
        seq_query, seq_key, seq_value, seq_gate, seq_residual = parts
        scores = head_scores(seq_query, seq_key) + bias_wide
        gated = (seq_gate * head_average(scores, seq_value)).astype(jnp.bfloat16)
        return output_layer(gated, seq_residual, row_output, row_output_bias)
    after_rows = lax.map(one_sequence, (queries, key_proj, value_proj, gate_proj, alignment))
    by_residue = jnp.transpose(after_rows, (1, 0, 2))
    column_normed = layer_norm(by_residue, column_norm_gain, column_norm_bias)
    col_parts = project_all(column_normed, column_query, column_key, column_value, column_gate, column_gate_bias)

    def one_residue(parts):
        res_query, res_key, res_value, res_gate, res_residual = parts
        scores = head_scores(res_query, res_key)
        gated = (res_gate * head_average(scores, res_value)).astype(jnp.bfloat16)
        return output_layer(gated, res_residual, column_output, column_output_bias)
    after_columns = lax.map(one_residue, (col_parts[0], col_parts[1], col_parts[2], col_parts[3], by_residue))
    return jnp.transpose(after_columns, (1, 0, 2))
```

```python
import functools

import jax
import jax.numpy as jnp
from jax import lax
from jax.experimental import pallas as pl
from jax.experimental.pallas import tpu as pltpu
from jax.sharding import PartitionSpec as P

H = 8
HEAD = 32
C = 256
LANES = 128
GROUP = LANES // HEAD
EPS = 1e-05
BLOCK = 32
VMEM = 56 * 1024 * 1024
NZ, NX, NY = 4, 4, 2
DAP = NZ * NX * NY
NT = (((1,), (1,)), ((), ()))


def norm(x, gain, bias):
    center = jnp.mean(x, axis=-1, keepdims=True)
    moved = x - center
    spread = jnp.mean(moved * moved, axis=-1, keepdims=True)
    return (moved * lax.rsqrt(spread + EPS) * gain + bias).astype(jnp.bfloat16)


def lanes_of(part):
    return slice(part * LANES, (part + 1) * LANES)


def dot(a, b):
    return jnp.dot(a, b, preferred_element_type=jnp.float32)


def softmax_rounded(scores):
    top = jnp.max(scores, axis=-1, keepdims=True)
    e = jnp.exp(scores - top)
    total = jnp.sum(e, axis=-1, keepdims=True)
    return (e * (1.0 / total)).astype(jnp.bfloat16)


def head_of_lane():
    return lax.broadcasted_iota(jnp.int32, (1, LANES), 1) // HEAD


def stacked(q):
    head = head_of_lane()
    masks = [(head == i).astype(jnp.float32).astype(jnp.bfloat16) for i in range(GROUP)]
    return jnp.concatenate([q * mask for mask in masks], axis=0)


def own_lanes(mixed):
    head = head_of_lane()
    rows = mixed.shape[0] // GROUP
    total = mixed[:rows]
    for i in range(1, GROUP):
        total = jnp.where(head == i, mixed[i * rows : (i + 1) * rows], total)
    return total


def pipelined(count, score, soften, average):
    scores, weights = {0: score(0)}, {}
    for n in range(count + 1):
        if n + 1 < count:
            scores[n + 1] = score(n + 1)
        if n < count:
            weights[n] = soften(n, scores.pop(n))
        if n >= 1:
            average(n - 1, weights.pop(n - 1))


def project(normed, q_w, k_w, v_w, g_w, g_b):
    q = (dot(normed, q_w[...]) * HEAD ** (-0.5)).astype(jnp.bfloat16)
    k_t = dot(normed, k_w[...]).T.astype(jnp.bfloat16)
    v = dot(normed, v_w[...]).astype(jnp.bfloat16)
    g = jax.nn.sigmoid(dot(normed, g_w[...]) + g_b[...])
    return q, k_t, v, g


def pair_kernel(x_ref, gain_ref, w_ref, out_ref, held):
    step = pl.program_id(0)
    rows = x_ref.shape[0]
    heads, count, _ = out_ref.shape
    for i in range(rows):
        normed = norm(x_ref[i].astype(jnp.float32), gain_ref[...], 0.0)
        bias = lax.dot_general(w_ref[...], normed, NT, preferred_element_type=jnp.float32)
        for part in range(held.shape[0]):
            held[part, pl.ds(step * rows + i, H, stride=count), :] = bias[:, lanes_of(part)]

    @pl.when(step == pl.num_programs(0) - 1)
    def _():
        for part in range(held.shape[0]):
            out_ref[:, :, lanes_of(part)] = (
                held[part].astype(jnp.bfloat16).reshape(heads, count, LANES)
            )


def pair_bias(pair_state, gain, weight):
    count, res, cz = pair_state.shape
    rows = 4
    return pl.pallas_call(
        pair_kernel,
        grid=(count // rows,),
        out_shape=jax.ShapeDtypeStruct((H, count, res), jnp.bfloat16),
        in_specs=[
            pl.BlockSpec((rows, res, cz), lambda i: (i, 0, 0)),
            pl.BlockSpec((1, cz), lambda i: (0, 0)),
            pl.BlockSpec((H, cz), lambda i: (0, 0)),
        ],
        out_specs=pl.BlockSpec((H, count, res), lambda i: (0, 0, 0)),
        scratch_shapes=[pltpu.VMEM((res // LANES, H * count, LANES), jnp.float32)],
        compiler_params=pltpu.CompilerParams(vmem_limit_bytes=VMEM),
        name="pair_bias",
    )(pair_state, gain.reshape(1, cz), weight.T)


def project_kernel(x_ref, gain, bias, q_w, k_w, v_w, g_w, g_b, *refs):
    q_ref, k_ref, v_ref, g_ref = refs[-4:]
    count, res, width = x_ref.shape
    x = x_ref[...].reshape(count * res, width).astype(jnp.float32)
    normed = norm(x, gain[...], bias[...])
    q, k_t, v, g = project(normed, q_w, k_w, v_w, g_w, g_b)
    for out_ref, value in ((q_ref, q), (v_ref, v), (g_ref, g)):
        out_ref[...] = value.reshape(count, res, width)
    for n in range(count):
        k_ref[n] = k_t[:, n * res : (n + 1) * res]


def row_project(first, count, held, x, gain, bias, q_w, k_w, v_w, g_w, g_b):
    seqs, res, width = x.shape
    once = 2
    block = pl.BlockSpec((once, res, width), lambda s: (first // once + s, 0, 0))
    turned = pl.BlockSpec((once, width, res), lambda s: (first // once + s, 0, 0))
    vector = pl.BlockSpec((1, width), lambda s: (0, 0))
    weight = pl.BlockSpec((width, width), lambda s: (0, 0))
    shape = jax.ShapeDtypeStruct
    return pl.pallas_call(
        project_kernel,
        grid=(count // once,),
        out_shape=[
            shape((seqs, res, width), jnp.bfloat16),
            shape((seqs, width, res), jnp.bfloat16),
            shape((seqs, res, width), jnp.bfloat16),
            shape((seqs, res, width), jnp.float32),
        ],
        in_specs=[block, vector, vector]
        + [weight] * 4
        + [vector]
        + [pl.BlockSpec(memory_space=pl.ANY)] * len(held),
        out_specs=[block, turned, block, block],
        input_output_aliases={8 + n: n for n in range(len(held))},
        compiler_params=pltpu.CompilerParams(vmem_limit_bytes=VMEM),
        cost_estimate=pl.CostEstimate(
            flops=2 * count * res * width * width * 4,
            bytes_accessed=count * res * width * 12,
            transcendentals=count * res * width * 2,
        ),
        name="row_project",
    )(x, gain.reshape(1, -1), bias.reshape(1, -1), q_w, k_w, v_w, g_w, g_b.reshape(1, -1), *held)


def row_kernel(layout, tile, here_ref, q_ref, k_ref, v_ref, g_ref, x_ref, o_w, o_b, *rest):
    pieces, (out_ref, whole, held, weights, sems) = rest[: len(layout)], rest[len(layout) :]
    res = q_ref.shape[1]
    own = res // DAP

    @pl.when(pl.program_id(0) == 0)
    def _():
        copies = []
        z, x, y = here_ref[0], here_ref[1], here_ref[2]
        for n, (piece, (first_head, slots)) in enumerate(zip(pieces, layout)):
            heads = piece.shape[1]
            for m, (zo, xo, yo) in enumerate(slots):
                owner = (
                    lax.rem(z + zo, NZ) * (NX * NY) + lax.rem(x + xo, NX) * NY + lax.rem(y + yo, NY)
                )
                rows = pl.ds(pl.multiple_of(owner * own, own), own)
                copies.append(
                    pltpu.make_async_copy(
                        piece.at[m], whole.at[pl.ds(first_head, heads), rows, :], sems.at[n, m]
                    )
                )
        for copy in copies:
            copy.start()
        for copy in copies:
            copy.wait()

    def place(n):
        t, group = divmod(n, H // GROUP)
        return slice(t * tile, (t + 1) * tile), lanes_of(group), group

    def score(n):
        rows, lanes, _ = place(n)
        held[n % 2] = dot(stacked(q_ref[0, rows, lanes]), k_ref[0, lanes, :])

    def soften(n, _):
        rows, _, group = place(n)
        for i in range(GROUP):
            for low in range(0, tile, BLOCK):
                here = slice(i * tile + low, i * tile + low + BLOCK)
                bias = whole[group * GROUP + i, rows.start + low : rows.start + low + BLOCK, :]
                weights[n % 2, here] = softmax_rounded(held[n % 2, here] + bias.astype(jnp.float32))

    gated = {}

    def average(n, _):
        rows, lanes, group = place(n)
        mixed = own_lanes(dot(weights[n % 2], v_ref[0, :, lanes]))
        gated[group] = (mixed * g_ref[0, rows, lanes]).astype(jnp.bfloat16)
        if len(gated) == H // GROUP:
            both = jnp.concatenate([gated.pop(part) for part in range(H // GROUP)], axis=1)
            after = x_ref[0, rows, :].astype(jnp.float32) + (dot(both, o_w[...]) + o_b[...])
            out_ref[rows.start // own : rows.stop // own, 0] = after.astype(jnp.bfloat16).reshape(
                tile // own, own, C
            )

    pipelined(res // tile * (H // GROUP), score, soften, average)


def row_attention(here, q, k, v, g, x, o_w, o_b, pieces, layout):
    seqs, res, width = x.shape
    own = res // DAP
    block = pl.BlockSpec((1, res, width), lambda s, *_: (s, 0, 0))
    turned = pl.BlockSpec((1, width, res), lambda s, *_: (s, 0, 0))
    most = max(len(slots) for _, slots in layout)
    return pl.pallas_call(
        functools.partial(row_kernel, layout, 256),
        out_shape=jax.ShapeDtypeStruct((DAP, seqs, own, width), jnp.bfloat16),
        grid_spec=pltpu.PrefetchScalarGridSpec(
            num_scalar_prefetch=1,
            grid=(seqs,),
            in_specs=[block, turned, block, block, block]
            + [
                pl.BlockSpec((width, width), lambda s, *_: (0, 0)),
                pl.BlockSpec((1, width), lambda s, *_: (0, 0)),
            ]
            + [pl.BlockSpec(memory_space=pl.ANY)] * len(pieces),
            out_specs=pl.BlockSpec((DAP, 1, own, width), lambda s, *_: (0, s, 0, 0)),
            scratch_shapes=[
                pltpu.VMEM((H, res, res), jnp.bfloat16),
                pltpu.VMEM((2, GROUP * 256, res), jnp.float32),
                pltpu.VMEM((2, GROUP * 256, res), jnp.bfloat16),
                pltpu.SemaphoreType.DMA((len(layout), most)),
            ],
        ),
        compiler_params=pltpu.CompilerParams(vmem_limit_bytes=VMEM),
        name="row_attention",
    )(here, q, k, v, g, x, o_w, o_b.reshape(1, -1), *pieces)


def column_kernel(at_once, x_ref, gain, bias, q_w, k_w, v_w, g_w, g_b, o_w, o_b, out_ref, held):
    step = pl.program_id(0)
    seqs, items, width = x_ref.shape
    parts = width // LANES

    @pl.when(step == 0)
    def _():
        for part in range(parts):
            held[part] = (
                x_ref[:, :, lanes_of(part)].astype(jnp.float32).reshape(seqs * items, LANES)
            )

    mine = [pl.ds(step * at_once + n, seqs, stride=items) for n in range(at_once)]
    x = jnp.concatenate(
        [jnp.concatenate([held[part, rows, :] for rows in mine], axis=0) for part in range(parts)], axis=1
    )
    normed = norm(x, gain[...], bias[...])
    q, k_t, v, g = project(normed, q_w, k_w, v_w, g_w, g_b)
    gated = {}

    def place(n):
        return slice(n // parts * seqs, (n // parts + 1) * seqs), lanes_of(n % parts)

    def score(n):
        rows, lanes = place(n)
        return dot(stacked(q[rows, lanes]), k_t[lanes, rows])

    def average(n, weights):
        rows, lanes = place(n)
        mixed = own_lanes(dot(weights, v[rows, lanes]))
        gated[n] = (mixed * g[rows, lanes]).astype(jnp.bfloat16)

    pipelined(at_once * parts, score, lambda n, scores: softmax_rounded(scores), average)
    gated = [
        jnp.concatenate([gated[n * parts + part] for part in range(parts)], axis=1)
        for n in range(at_once)
    ]
    after = x + (dot(jnp.concatenate(gated, axis=0), o_w[...]) + o_b[...])
    for n, rows in enumerate(mine):
        for part in range(parts):
            held[part, rows, :] = after[n * seqs : (n + 1) * seqs, lanes_of(part)]

    @pl.when(step == pl.num_programs(0) - 1)
    def _():
        for part in range(parts):
            out_ref[:, :, lanes_of(part)] = (
                held[part].astype(jnp.bfloat16).reshape(seqs, items, LANES)
            )


def column_attention(x, gain, bias, q_w, k_w, v_w, g_w, g_b, o_w, o_b):
    seqs, items, width = x.shape
    at_once = 2
    whole = pl.BlockSpec(x.shape, lambda r: (0, 0, 0))
    vector = pl.BlockSpec((1, width), lambda r: (0, 0))
    weight = pl.BlockSpec((width, width), lambda r: (0, 0))
    return pl.pallas_call(
        functools.partial(column_kernel, at_once),
        grid=(items // at_once,),
        out_shape=jax.ShapeDtypeStruct(x.shape, jnp.bfloat16),
        in_specs=[whole, vector, vector] + [weight] * 4 + [vector, weight, vector],
        out_specs=whole,
        scratch_shapes=[pltpu.VMEM((width // LANES, seqs * items, LANES), jnp.float32)],
        compiler_params=pltpu.CompilerParams(vmem_limit_bytes=VMEM),
        name="column_attention",
    )(
        x, gain.reshape(1, -1), bias.reshape(1, -1), q_w, k_w, v_w, g_w, g_b.reshape(1, -1),
        o_w, o_b.reshape(1, -1),
    )


def fetch(value, z=0, x=0, y=0):
    pairs = []
    for dz in range(NZ):
        for dx in range(NX):
            for dy in range(NY):
                src = ((dz + z) % NZ * NX + (dx + x) % NX) * NY + (dy + y) % NY
                pairs.append((src, (dz * NX + dx) * NY + dy))
    return lax.ppermute(value, "dap", pairs)


def shift(values, axis):
    return [(v, fetch(v, **{a: 1}), fetch(v, **{a: 3})) for v, a in zip(values, axis)]


def relay(rings, axis):
    out = []
    for (value, ahead, behind), a in zip(rings, axis):
        half = value.shape[0] // 2
        out.append([value, ahead, fetch(ahead[:half], **{a: 1}), fetch(behind[half:], **{a: 3}), behind])
    return out


def gather_bias(local, work):
    other = fetch(local, y=1)
    order, turned = ("x", "z"), ("z", "x")
    pairs = [
        jnp.stack([local[part * GROUP : (part + 1) * GROUP], other[part * GROUP : (part + 1) * GROUP]])
        for part in range(2)
    ]
    planes = [
        jnp.concatenate([fetch(pair, **{a: step}) if step else pair for step in range(4)])
        for pair, a in zip(pairs, order)
    ]
    rings = shift(planes, turned)
    rings, result = lax.optimization_barrier((rings, work[0]()))
    rings = relay(rings, turned)
    result = work[1](result)
    pieces, layout = [], []
    for part in range(2):
        first, second = order[part], turned[part]
        slots = [{first: a, second: 0, "y": b} for a in range(4) for b in range(NY)]
        half = len(slots) // 2
        for piece, kept, step in zip(
            rings[part], (slots, slots, slots[:half], slots[half:], slots), (0, 1, 2, 2, 3)
        ):
            pieces.append(piece)
            layout.append(
                (part * GROUP, [(s["z"], s["x"], s["y"]) for s in (dict(k, **{second: step}) for k in kept)])
            )
    return pieces, layout, result


def per_device(
    alignment,
    pair_state,
    row_norm_gain,
    row_norm_bias,
    pair_norm_gain,
    pair_weight,
    row_query,
    row_key,
    row_value,
    row_gate,
    row_gate_bias,
    row_output,
    row_output_bias,
    column_norm_gain,
    column_norm_bias,
    column_query,
    column_key,
    column_value,
    column_gate,
    column_gate_bias,
    column_output,
    column_output_bias,
):
    seqs, res, width = alignment.shape
    own = res // DAP
    me = lax.axis_index("dap")
    here = jnp.stack([me // (NX * NY), me // NY % NX, me % NY]).astype(jnp.int32)
    row = (
        alignment, row_norm_gain, row_norm_bias, row_query, row_key, row_value, row_gate, row_gate_bias
    )
    pieces, layout, (q, k, v, g) = gather_bias(
        pair_bias(pair_state, pair_norm_gain, pair_weight),
        (
            lambda: row_project(0, seqs // 2, (), *row),
            lambda held: row_project(seqs // 2, seqs // 2, held, *row),
        ),
    )
    after = row_attention(
        here, q, k, v, g, alignment, row_output, row_output_bias, pieces, layout
    )
    received = lax.all_to_all(after, "dap", split_axis=0, concat_axis=0, tiled=True)
    columns = column_attention(
        received.reshape(DAP * seqs, own, width),
        column_norm_gain,
        column_norm_bias,
        column_query,
        column_key,
        column_value,
        column_gate,
        column_gate_bias,
        column_output,
        column_output_bias,
    )
    back = lax.all_to_all(
        columns.reshape(DAP, seqs, own, width), "dap", split_axis=0, concat_axis=0, tiled=True
    )
    return back.transpose(1, 0, 2, 3).reshape(alignment.shape)


def solution(mesh):
    split = P(("batch", "dap"), None, None)
    return jax.shard_map(
        per_device,
        mesh=mesh,
        in_specs=(split, split) + (P(),) * 20,
        out_specs=split,
        check_vma=False,
    )
```

```python
import functools

import jax
import jax.numpy as jnp
from jax import lax
from jax.experimental import pallas as pl
from jax.experimental.pallas import tpu as pltpu
from jax.sharding import PartitionSpec as P

H = 8
HEAD = 32
C = 256
LANES = 128
GROUP = LANES // HEAD
EPS = 1e-05
VMEM = 40 * 1024 * 1024
NZ, NX, NY = 4, 4, 2
DAP = NZ * NX * NY
NT = (((1,), (1,)), ((), ()))


def norm(x, gain, bias):
    center = jnp.mean(x, axis=-1, keepdims=True)
    moved = x - center
    spread = jnp.mean(moved * moved, axis=-1, keepdims=True)
    return (moved * lax.rsqrt(spread + EPS) * gain + bias).astype(jnp.bfloat16)


def lanes_of(part):
    return slice(part * LANES, (part + 1) * LANES)


def dot(a, b):
    return jnp.dot(a, b, preferred_element_type=jnp.float32)


def softmax_rounded(scores):
    top = jnp.max(scores, axis=-1, keepdims=True)
    e = jnp.exp(scores - top)
    total = jnp.sum(e, axis=-1, keepdims=True)
    return (e * (1.0 / total)).astype(jnp.bfloat16)


def head_of_lane():
    return lax.broadcasted_iota(jnp.int32, (1, LANES), 1) // HEAD


def stacked(q):
    head = head_of_lane()
    masks = [(head == i).astype(jnp.float32).astype(jnp.bfloat16) for i in range(GROUP)]
    return jnp.concatenate([q * mask for mask in masks], axis=0)


def own_lanes(mixed):
    head = head_of_lane()
    rows = mixed.shape[0] // GROUP
    total = mixed[:rows]
    for i in range(1, GROUP):
        total = jnp.where(head == i, mixed[i * rows : (i + 1) * rows], total)
    return total


def pipelined(count, score, soften, average):
    scores, weights = {0: score(0)}, {}
    for n in range(count + 1):
        if n + 1 < count:
            scores[n + 1] = score(n + 1)
        if n < count:
            weights[n] = soften(n, scores.pop(n))
        if n >= 1:
            average(n - 1, weights.pop(n - 1))


def project(normed, q_w, k_w, v_w, g_w, g_b):
    q = (dot(normed, q_w[...]) * HEAD ** (-0.5)).astype(jnp.bfloat16)
    k_t = dot(normed, k_w[...]).T.astype(jnp.bfloat16)
    v = dot(normed, v_w[...]).astype(jnp.bfloat16)
    g = jax.nn.sigmoid(dot(normed, g_w[...]) + g_b[...])
    return q, k_t, v, g


def pair_kernel(x_ref, gain_ref, w_ref, out_ref, held):
    step = pl.program_id(0)
    rows = x_ref.shape[0]
    heads, count, _ = out_ref.shape
    for i in range(rows):
        normed = norm(x_ref[i].astype(jnp.float32), gain_ref[...], 0.0)
        bias = lax.dot_general(w_ref[...], normed, NT, preferred_element_type=jnp.float32)
        for part in range(held.shape[0]):
            held[part, pl.ds(step * rows + i, H, stride=count), :] = bias[:, lanes_of(part)]

    @pl.when(step == pl.num_programs(0) - 1)
    def _():
        for part in range(held.shape[0]):
            out_ref[:, :, lanes_of(part)] = (
                held[part].astype(jnp.bfloat16).reshape(heads, count, LANES)
            )


def pair_bias(pair_state, gain, weight):
    count, res, cz = pair_state.shape
    rows = 4
    return pl.pallas_call(
        pair_kernel,
        grid=(count // rows,),
        out_shape=jax.ShapeDtypeStruct((H, count, res), jnp.bfloat16),
        in_specs=[
            pl.BlockSpec((rows, res, cz), lambda i: (i, 0, 0)),
            pl.BlockSpec((1, cz), lambda i: (0, 0)),
            pl.BlockSpec((H, cz), lambda i: (0, 0)),
        ],
        out_specs=pl.BlockSpec((H, count, res), lambda i: (0, 0, 0)),
        scratch_shapes=[pltpu.VMEM((res // LANES, H * count, LANES), jnp.float32)],
        compiler_params=pltpu.CompilerParams(vmem_limit_bytes=VMEM),
        name="pair_bias",
    )(pair_state, gain.reshape(1, cz), weight.T)


def project_kernel(x_ref, gain, bias, q_w, k_w, v_w, g_w, g_b, q_ref, k_ref, v_ref, g_ref):
    count, res, width = x_ref.shape
    x = x_ref[...].reshape(count * res, width).astype(jnp.float32)
    normed = norm(x, gain[...], bias[...])
    q, k_t, v, g = project(normed, q_w, k_w, v_w, g_w, g_b)
    for out_ref, value in ((q_ref, q), (v_ref, v), (g_ref, g)):
        out_ref[...] = value.reshape(count, res, width)
    for n in range(count):
        k_ref[n] = k_t[:, n * res : (n + 1) * res]


def row_project(x, gain, bias, q_w, k_w, v_w, g_w, g_b):
    seqs, res, width = x.shape
    count = 2
    block = pl.BlockSpec((count, res, width), lambda s: (s, 0, 0))
    turned = pl.BlockSpec((count, width, res), lambda s: (s, 0, 0))
    vector = pl.BlockSpec((1, width), lambda s: (0, 0))
    weight = pl.BlockSpec((width, width), lambda s: (0, 0))
    shape = jax.ShapeDtypeStruct
    return pl.pallas_call(
        project_kernel,
        grid=(seqs // count,),
        out_shape=[
            shape((seqs, res, width), jnp.bfloat16),
            shape((seqs, width, res), jnp.bfloat16),
            shape((seqs, res, width), jnp.bfloat16),
            shape((seqs, res, width), jnp.float32),
        ],
        in_specs=[block, vector, vector] + [weight] * 4 + [vector],
        out_specs=[block, turned, block, block],
        compiler_params=pltpu.CompilerParams(vmem_limit_bytes=VMEM),
        cost_estimate=pl.CostEstimate(
            flops=2 * seqs * res * width * width * 4,
            bytes_accessed=x.size * 12,
            transcendentals=x.size * 2,
        ),
        name="row_project",
    )(x, gain.reshape(1, -1), bias.reshape(1, -1), q_w, k_w, v_w, g_w, g_b.reshape(1, -1))


def row_kernel(here_ref, q_ref, k_ref, v_ref, g_ref, x_ref, bias_ref, o_w, o_b, *rest):
    out_ref, held, weights = rest[-3:]
    seqs, tile, width = q_ref.shape
    own = out_ref.shape[2]
    groups = H // GROUP

    def place(n):
        return n // groups, n % groups, lanes_of(n % groups)

    def score(n):
        seq, _, lanes = place(n)
        held[n % 2] = dot(stacked(q_ref[seq, :, lanes]), k_ref[seq, lanes, :])

    def slot(x, y):
        return lax.rem(x - here_ref[1] + NX, NX) * NY + lax.rem(y - here_ref[2] + NY, NY)

    def soften(n, _):
        _, group, _ = place(n)
        for i in range(GROUP):
            for x in range(NX):
                rows = slice(i * tile + x * NY * own, i * tile + (x + 1) * NY * own)
                bias = [bias_ref[slot(x, y), group * GROUP + i] for y in range(NY)]
                bias = jnp.concatenate(bias, axis=0).astype(jnp.float32)
                weights[n % 2, rows] = softmax_rounded(held[n % 2, rows] + bias)

    gated = {}

    def average(n, _):
        seq, group, lanes = place(n)
        mixed = own_lanes(dot(weights[n % 2], v_ref[seq, :, lanes]))
        gated[group] = (mixed * g_ref[seq, :, lanes]).astype(jnp.bfloat16)
        if len(gated) == groups:
            both = jnp.concatenate([gated.pop(part) for part in range(groups)], axis=1)
            after = x_ref[seq].astype(jnp.float32) + (dot(both, o_w[...]) + o_b[...])
            out_ref[:, seq] = after.astype(jnp.bfloat16).reshape(out_ref.shape[0], own, width)

    pipelined(seqs * groups, score, soften, average)


def row_attention(plane, here, q, k, v, g, x, bias, o_w, o_b, held):
    seqs, res, width = x.shape
    own = res // DAP
    tile = res // NZ
    once = 4

    def which(here):
        return lax.rem(here[0] + plane, NZ)

    queries = pl.BlockSpec((once, tile, width), lambda s, here: (s, which(here), 0))
    args = [q, k, v, g, x, bias, o_w, o_b.reshape(1, -1), *held]
    return pl.pallas_call(
        row_kernel,
        out_shape=jax.ShapeDtypeStruct((DAP, seqs, own, width), jnp.bfloat16),
        grid_spec=pltpu.PrefetchScalarGridSpec(
            num_scalar_prefetch=1,
            grid=(seqs // once,),
            in_specs=[
                queries,
                pl.BlockSpec((once, width, res), lambda s, here: (s, 0, 0)),
                pl.BlockSpec((once, res, width), lambda s, here: (s, 0, 0)),
                queries,
                queries,
                pl.BlockSpec(bias.shape, lambda s, here: (0, 0, 0, 0)),
                pl.BlockSpec((width, width), lambda s, here: (0, 0)),
                pl.BlockSpec((1, width), lambda s, here: (0, 0)),
            ]
            + [pl.BlockSpec(memory_space=pl.ANY)] * len(held),
            out_specs=pl.BlockSpec(
                (DAP // NZ, once, own, width), lambda s, here: (which(here), s, 0, 0)
            ),
            scratch_shapes=[
                pltpu.VMEM((2, GROUP * tile, res), jnp.float32),
                pltpu.VMEM((2, GROUP * tile, res), jnp.bfloat16),
            ],
        ),
        input_output_aliases={len(args): 0} if held else {},
        compiler_params=pltpu.CompilerParams(vmem_limit_bytes=VMEM),
        cost_estimate=pl.CostEstimate(
            flops=seqs * H * tile * res * 256 * 16,
            bytes_accessed=8 * 1024 * 1024,
            transcendentals=seqs * H * tile * res,
        ),
        name="row_attention",
    )(here, *args)


def column_kernel(at_once, x_ref, gain, bias, q_w, k_w, v_w, g_w, g_b, o_w, o_b, out_ref, held, scores, weights):
    step = pl.program_id(0)
    seqs, items, width = x_ref.shape
    parts = width // LANES

    @pl.when(step == 0)
    def _():
        for part in range(parts):
            held[part] = (
                x_ref[:, :, lanes_of(part)].astype(jnp.float32).reshape(seqs * items, LANES)
            )

    mine = [pl.ds(step * at_once + n, seqs, stride=items) for n in range(at_once)]
    x = jnp.concatenate(
        [jnp.concatenate([held[part, rows, :] for rows in mine], axis=0) for part in range(parts)], axis=1
    )
    normed = norm(x, gain[...], bias[...])
    q, k_t, v, g = project(normed, q_w, k_w, v_w, g_w, g_b)
    gated = {}

    def place(n):
        return slice(n // parts * seqs, (n // parts + 1) * seqs), lanes_of(n % parts)

    def score(n):
        rows, lanes = place(n)
        scores[n % 2] = dot(stacked(q[rows, lanes]), k_t[lanes, rows])

    def soften(n, _):
        for low in range(0, GROUP * seqs, 64):
            weights[n % 2, low : low + 64] = softmax_rounded(scores[n % 2, low : low + 64])

    def average(n, _):
        rows, lanes = place(n)
        mixed = own_lanes(dot(weights[n % 2], v[rows, lanes]))
        gated[n] = (mixed * g[rows, lanes]).astype(jnp.bfloat16)

    pipelined(at_once * parts, score, soften, average)
    gated = [
        jnp.concatenate([gated[n * parts + part] for part in range(parts)], axis=1)
        for n in range(at_once)
    ]
    after = x + (dot(jnp.concatenate(gated, axis=0), o_w[...]) + o_b[...])
    for n, rows in enumerate(mine):
        for part in range(parts):
            held[part, rows, :] = after[n * seqs : (n + 1) * seqs, lanes_of(part)]

    @pl.when(step == pl.num_programs(0) - 1)
    def _():
        for part in range(parts):
            out_ref[:, :, lanes_of(part)] = (
                held[part].astype(jnp.bfloat16).reshape(seqs, items, LANES)
            )


def column_attention(x, gain, bias, q_w, k_w, v_w, g_w, g_b, o_w, o_b):
    seqs, items, width = x.shape
    at_once = 4
    whole = pl.BlockSpec(x.shape, lambda r: (0, 0, 0))
    vector = pl.BlockSpec((1, width), lambda r: (0, 0))
    weight = pl.BlockSpec((width, width), lambda r: (0, 0))
    return pl.pallas_call(
        functools.partial(column_kernel, at_once),
        grid=(items // at_once,),
        out_shape=jax.ShapeDtypeStruct(x.shape, jnp.bfloat16),
        in_specs=[whole, vector, vector] + [weight] * 4 + [vector, weight, vector],
        out_specs=whole,
        scratch_shapes=[
            pltpu.VMEM((width // LANES, seqs * items, LANES), jnp.float32),
            pltpu.VMEM((2, GROUP * seqs, seqs), jnp.float32),
            pltpu.VMEM((2, GROUP * seqs, seqs), jnp.bfloat16),
        ],
        compiler_params=pltpu.CompilerParams(vmem_limit_bytes=VMEM),
        name="column_attention",
    )(
        x, gain.reshape(1, -1), bias.reshape(1, -1), q_w, k_w, v_w, g_w, g_b.reshape(1, -1),
        o_w, o_b.reshape(1, -1),
    )


def fetch(value, z=0, x=0, y=0):
    pairs = []
    for dz in range(NZ):
        for dx in range(NX):
            for dy in range(NY):
                src = ((dz + z) % NZ * NX + (dx + x) % NX) * NY + (dy + y) % NY
                pairs.append((src, (dz * NX + dx) * NY + dy))
    return lax.ppermute(value, "dap", pairs)


def plane_bias(local):
    near = {(x, y): fetch(local, x=x, y=y) for y in range(NY) for x in (1, 3, 2, 0) if x or y}
    near[0, 0] = local
    return jnp.stack([near[x, y] for x in range(NX) for y in range(NY)])


def per_device(
    alignment,
    pair_state,
    row_norm_gain,
    row_norm_bias,
    pair_norm_gain,
    pair_weight,
    row_query,
    row_key,
    row_value,
    row_gate,
    row_gate_bias,
    row_output,
    row_output_bias,
    column_norm_gain,
    column_norm_bias,
    column_query,
    column_key,
    column_value,
    column_gate,
    column_gate_bias,
    column_output,
    column_output_bias,
):
    seqs, res, width = alignment.shape
    own = res // DAP
    me = lax.axis_index("dap")
    here = jnp.stack([me // (NX * NY), me // NY % NX, me % NY]).astype(jnp.int32)
    bias = plane_bias(pair_bias(pair_state, pair_norm_gain, pair_weight))
    bias, inputs = lax.optimization_barrier((bias, alignment))
    ahead, behind = fetch(bias, z=1), fetch(bias, z=3)
    projected = row_project(
        inputs, row_norm_gain, row_norm_bias, row_query, row_key, row_value, row_gate, row_gate_bias
    )

    def attend(plane, bias, *held):
        return row_attention(
            plane, here, *projected, alignment, bias, row_output, row_output_bias, held
        )

    after = attend(0, bias)
    ahead, behind, after = lax.optimization_barrier((ahead, behind, after))
    far = fetch(ahead, z=1)
    after = attend(3, behind, attend(1, ahead, after))
    after = attend(2, far, after)
    received = lax.all_to_all(after, "dap", split_axis=0, concat_axis=0, tiled=True)
    columns = column_attention(
        received.reshape(DAP * seqs, own, width),
        column_norm_gain,
        column_norm_bias,
        column_query,
        column_key,
        column_value,
        column_gate,
        column_gate_bias,
        column_output,
        column_output_bias,
    )
    back = lax.all_to_all(
        columns.reshape(DAP, seqs, own, width), "dap", split_axis=0, concat_axis=0, tiled=True
    )
    return back.transpose(1, 0, 2, 3).reshape(alignment.shape)


def solution(mesh):
    split = P(("batch", "dap"), None, None)
    return jax.shard_map(
        per_device,
        mesh=mesh,
        in_specs=(split, split) + (P(),) * 20,
        out_specs=split,
        check_vma=False,
    )
```

```python
import functools

import jax
import jax.numpy as jnp
from jax import lax
from jax.experimental import pallas as pl
from jax.experimental.pallas import tpu as pltpu
from jax.sharding import PartitionSpec as P

H = 8
HEAD = 32
C = 256
LANES = 128
GROUP = LANES // HEAD
EPS = 1e-05
MIB = 1024 * 1024
HALVES = 2
HALF_ROWS = 8
NZ, NX, NY = 4, 4, 2
DAP = NZ * NX * NY
NT = (((1,), (1,)), ((), ()))


def norm(x, gain, bias):
    center = jnp.mean(x, axis=-1, keepdims=True)
    moved = x - center
    spread = jnp.mean(moved * moved, axis=-1, keepdims=True)
    return moved * lax.rsqrt(spread + EPS) * gain + bias


def lanes_of(part):
    return slice(part * LANES, (part + 1) * LANES)


def dot(a, b):
    return jnp.dot(a, b, preferred_element_type=jnp.float32)


def softmax_rounded(scores):
    top = jnp.max(scores, axis=-1, keepdims=True)
    e = jnp.exp(scores - top)
    total = jnp.sum(e, axis=-1, keepdims=True)
    return (e * (1.0 / total)).astype(jnp.bfloat16)


def head_of_lane():
    return lax.broadcasted_iota(jnp.int32, (1, LANES), 1) // HEAD


def stacked(q):
    head = head_of_lane()
    masks = [(head == i).astype(jnp.float32).astype(jnp.bfloat16) for i in range(GROUP)]
    return jnp.concatenate([q * mask for mask in masks], axis=0)


def own_lanes(mixed):
    head = head_of_lane()
    rows = mixed.shape[0] // GROUP
    total = mixed[:rows]
    for i in range(1, GROUP):
        total = jnp.where(head == i, mixed[i * rows : (i + 1) * rows], total)
    return total


def pipelined(count, score, soften, average):
    scores, weights = {0: score(0)}, {}
    for n in range(count + 1):
        if n + 1 < count:
            scores[n + 1] = score(n + 1)
        if n < count:
            weights[n] = soften(n, scores.pop(n))
        if n >= 1:
            average(n - 1, weights.pop(n - 1))


def project(normed, at_queries, q_w, k_w, v_w, g_w, g_b):
    q = (dot(at_queries, q_w[...]) * HEAD ** (-0.5)).astype(jnp.bfloat16)
    k_t = dot(normed, k_w[...]).T.astype(jnp.bfloat16)
    v = dot(normed, v_w[...]).astype(jnp.bfloat16)
    g = jax.nn.sigmoid(dot(at_queries, g_w[...]) + g_b[...])
    return q, k_t, v, g


def pair_kernel(x_ref, gain_ref, w_ref, out_ref, held):
    step = pl.program_id(0)
    rows = x_ref.shape[0]
    for i in range(rows):
        normed = norm(x_ref[i].astype(jnp.float32), gain_ref[...], 0.0).astype(jnp.bfloat16)
        bias = lax.dot_general(w_ref[...], normed, NT, preferred_element_type=jnp.float32)
        for part in range(held.shape[0]):
            low = step * rows // HALF_ROWS * (H * HALF_ROWS) + lax.rem(step * rows, HALF_ROWS) + i
            held[part, pl.ds(low, H, stride=HALF_ROWS), :] = bias[:, lanes_of(part)]

    @pl.when(step == pl.num_programs(0) - 1)
    def _():
        for part in range(held.shape[0]):
            out_ref[:, :, lanes_of(part)] = (
                held[part].astype(jnp.bfloat16).reshape(out_ref.shape[:2] + (LANES,))
            )


def pair_bias(pair_state, gain, weight):
    count, res, cz = pair_state.shape
    rows = 4
    return pl.pallas_call(
        pair_kernel,
        grid=(count // rows,),
        out_shape=jax.ShapeDtypeStruct((H, count, res), jnp.bfloat16),
        in_specs=[
            pl.BlockSpec((rows, res, cz), lambda i: (i, 0, 0)),
            pl.BlockSpec((1, cz), lambda i: (0, 0)),
            pl.BlockSpec((H, cz), lambda i: (0, 0)),
        ],
        out_specs=pl.BlockSpec((H, count, res), lambda i: (0, 0, 0)),
        scratch_shapes=[pltpu.VMEM((res // LANES, H * count, LANES), jnp.float32)],
        compiler_params=pltpu.CompilerParams(vmem_limit_bytes=56 * MIB),
        name="pair_bias",
    )(pair_state, gain.reshape(1, cz), weight.T)


def project_kernel(x_ref, gain, bias, q_w, k_w, v_w, g_w, g_b, q_ref, k_ref, v_ref, g_ref):
    count, res, width = x_ref.shape
    x = x_ref[...].reshape(count * res, width).astype(jnp.float32)
    normed = norm(x, gain[...], bias[...])
    split = normed.reshape(count, DAP, HALVES, HALF_ROWS, width)
    halves = [split[:, :, half].reshape(count, res // HALVES, width) for half in range(HALVES)]
    at_queries = jnp.concatenate(halves, axis=1).reshape(count * res, width)
    q, k_t, v, g = project(
        normed.astype(jnp.bfloat16), at_queries.astype(jnp.bfloat16), q_w, k_w, v_w, g_w, g_b
    )
    for out_ref, value in ((q_ref, q), (v_ref, v), (g_ref, g)):
        out_ref[...] = value.reshape(count, res, width)
    for n in range(count):
        k_ref[n] = k_t[:, n * res : (n + 1) * res]


def row_project(x, gain, bias, q_w, k_w, v_w, g_w, g_b):
    seqs, res, width = x.shape
    count = 2
    block = pl.BlockSpec((count, res, width), lambda s: (s, 0, 0))
    turned = pl.BlockSpec((count, width, res), lambda s: (s, 0, 0))
    vector = pl.BlockSpec((1, width), lambda s: (0, 0))
    weight = pl.BlockSpec((width, width), lambda s: (0, 0))
    shape = jax.ShapeDtypeStruct
    return pl.pallas_call(
        project_kernel,
        grid=(seqs // count,),
        out_shape=[
            shape((seqs, res, width), jnp.bfloat16),
            shape((seqs, width, res), jnp.bfloat16),
            shape((seqs, res, width), jnp.bfloat16),
            shape((seqs, res, width), jnp.float32),
        ],
        in_specs=[block, vector, vector] + [weight] * 4 + [vector],
        out_specs=[block, turned, block, block],
        compiler_params=pltpu.CompilerParams(vmem_limit_bytes=24 * MIB),
        cost_estimate=pl.CostEstimate(
            flops=2 * seqs * res * width * width * 4,
            bytes_accessed=x.size * 12,
            transcendentals=x.size * 2,
        ),
        name="row_project",
    )(x, gain.reshape(1, -1), bias.reshape(1, -1), q_w, k_w, v_w, g_w, g_b.reshape(1, -1))


def row_kernel(blocks, here_ref, *refs):
    count = len(blocks)
    planes = 1 + max(which for _, _, which in blocks)
    q_refs, g_refs, x_refs, (k_ref, v_ref) = refs[:2], refs[2:4], refs[4:6], refs[6:8]
    bias_refs, (o_w, o_b) = refs[8 : 8 + planes], refs[8 + planes : 10 + planes]
    held, weights, ready, sems = refs[-4:]
    halves = sorted({half for _, half, _ in blocks})
    outs = dict(zip(halves, refs[-4 - len(halves) : -4]))
    step, last = pl.program_id(0), pl.num_programs(0) - 1
    seqs, part_rows, width = q_refs[0].shape
    tile = count * part_rows
    owners = part_rows // HALF_ROWS
    groups = H // GROUP

    def place(n):
        return n // groups, n % groups, lanes_of(n % groups)

    def both(pick):
        return jnp.concatenate([pick(n) for n in range(count)], axis=0)

    def score(n):
        seq, _, lanes = place(n)
        q = both(lambda b: q_refs[b][seq, :, lanes])
        held[n % 2] = dot(stacked(q), k_ref[seq, lanes, :])

    def slot(x, y):
        return lax.rem(x - here_ref[1] + NX, NX) * NY + lax.rem(y - here_ref[2] + NY, NY)

    slots = [slot(x, y) for x in range(NX) for y in range(NY)]
    taken = 4

    def soften(n, _):
        _, group, _ = place(n)
        for b, (_, half, which) in enumerate(blocks):
            for two in range(0, GROUP, 2):
                for first in range(0, owners, taken):
                    piece = (half * H + group * GROUP + two) // 2
                    bias = [
                        bias_refs[which][slots[o], piece].astype(jnp.float32)
                        for o in range(first, first + taken)
                    ]
                    for i in range(2):
                        low = (two + i) * tile + b * part_rows + first * HALF_ROWS
                        rows = slice(low, low + taken * HALF_ROWS)
                        mine = [value[i * HALF_ROWS : (i + 1) * HALF_ROWS] for value in bias]
                        weights[n % 2, rows] = softmax_rounded(
                            held[n % 2, rows] + jnp.concatenate(mine, axis=0)
                        )

    gated, done = {}, []

    def average(n, _):
        seq, group, lanes = place(n)
        mixed = own_lanes(dot(weights[n % 2], v_ref[seq, :, lanes]))
        gated[group] = (mixed * both(lambda b: g_refs[b][seq, :, lanes])).astype(jnp.bfloat16)
        if len(gated) == groups:
            whole = jnp.concatenate([gated.pop(part) for part in range(groups)], axis=1)
            update = dot(whole, o_w[...]) + o_b[...]
            after = []
            for b, (_, half, _) in enumerate(blocks):
                x = x_refs[b][seq].astype(jnp.float32).reshape(owners, HALVES, HALF_ROWS, width)
                own = update[b * part_rows : (b + 1) * part_rows].reshape(owners, HALF_ROWS, width)
                after.append(x[:, half] + own)
            done.append(after)
            if len(done) == 2:
                low = (seq - 1) * HALF_ROWS
                for b in range(count):
                    rows = jnp.concatenate([value[b] for value in done], axis=1)
                    ready[step, b, :, low : low + 2 * HALF_ROWS] = rows.astype(jnp.bfloat16)
                done.clear()

    pipelined(seqs * groups, score, soften, average)

    def copies(step):
        for b, (plane, half, _) in enumerate(blocks):
            first = pl.multiple_of(lax.rem(here_ref[0] + plane, NZ) * owners, owners)
            rows = pl.ds(pl.multiple_of(step * seqs * HALF_ROWS, seqs * HALF_ROWS), seqs * HALF_ROWS)
            yield pltpu.make_async_copy(
                ready.at[step, b], outs[half].at[pl.ds(first, owners), rows], sems.at[step, b]
            )

    for copy in copies(step):
        copy.start()

    @pl.when(step == last)
    def _():
        for n in range(ready.shape[0]):
            for copy in copies(n):
                copy.wait()


def row_attention(blocks, here, q, k, v, g, x, biases, o_w, o_b, held):
    seqs, res, width = x.shape
    own = res // DAP
    part_rows = DAP // NZ * HALF_ROWS
    once = 4
    halves = sorted({half for _, half, _ in blocks})

    def which(here, plane):
        return lax.rem(here[0] + plane, NZ)

    queries = [
        pl.BlockSpec(
            (once, part_rows, width),
            lambda s, here, plane=plane, half=half: (s, half * NZ + which(here, plane), 0),
        )
        for plane, half, _ in blocks
    ]
    residual = [
        pl.BlockSpec((once, res // NZ, width), lambda s, here, plane=plane: (s, which(here, plane), 0))
        for plane, _, _ in blocks
    ]
    args = [q, q, g, g, x, x, k, v, *biases, o_w, o_b.reshape(1, -1), *held]
    return pl.pallas_call(
        functools.partial(row_kernel, blocks),
        out_shape=[jax.ShapeDtypeStruct((DAP, seqs * HALF_ROWS, width), jnp.bfloat16)] * len(halves),
        grid_spec=pltpu.PrefetchScalarGridSpec(
            num_scalar_prefetch=1,
            grid=(seqs // once,),
            in_specs=queries
            + queries
            + residual
            + [
                pl.BlockSpec((once, width, res), lambda s, here: (s, 0, 0)),
                pl.BlockSpec((once, res, width), lambda s, here: (s, 0, 0)),
            ]
            + [pl.BlockSpec(bias.shape, lambda s, here: (0, 0, 0, 0)) for bias in biases]
            + [
                pl.BlockSpec((width, width), lambda s, here: (0, 0)),
                pl.BlockSpec((1, width), lambda s, here: (0, 0)),
            ]
            + [pl.BlockSpec(memory_space=pl.ANY)] * len(held),
            out_specs=[pl.BlockSpec(memory_space=pl.ANY)] * len(halves),
            scratch_shapes=[
                pltpu.VMEM((2, GROUP * part_rows * len(blocks), res), jnp.float32),
                pltpu.VMEM((2, GROUP * part_rows * len(blocks), res), jnp.bfloat16),
                pltpu.VMEM(
                    (seqs // once, len(blocks), DAP // NZ, once * HALF_ROWS, width), jnp.bfloat16
                ),
                pltpu.SemaphoreType.DMA((seqs // once, len(blocks))),
            ],
        ),
        input_output_aliases={len(args) + 1 - len(held) + n: n for n in range(len(held))},
        compiler_params=pltpu.CompilerParams(vmem_limit_bytes=24 * MIB),
        cost_estimate=pl.CostEstimate(
            flops=seqs * H * part_rows * len(blocks) * res * 256 * 16,
            bytes_accessed=8 * 1024 * 1024,
            transcendentals=seqs * H * part_rows * len(blocks) * res,
        ),
        name="row_attention",
    )(here, *args)


def column_kernel(at_once, x_ref, gain, bias, q_w, k_w, v_w, g_w, g_b, o_w, o_b, *refs):
    out_ref, held, scores, weights = refs[-4:]
    step = pl.program_id(0)
    owners, per, width = x_ref.shape
    items = pl.num_programs(0) * at_once
    seqs = owners * per // items
    parts = width // LANES

    @pl.when(step == 0)
    def _():
        for part in range(parts):
            held[part] = x_ref[:, :, lanes_of(part)].astype(jnp.float32).reshape(-1, LANES)

    mine = [pl.ds(step * at_once + n, seqs, stride=items) for n in range(at_once)]
    x = jnp.concatenate(
        [jnp.concatenate([held[part, rows, :] for rows in mine], axis=0) for part in range(parts)], axis=1
    )
    normed = norm(x, gain[...], bias[...]).astype(jnp.bfloat16)
    q, k_t, v, g = project(normed, normed, q_w, k_w, v_w, g_w, g_b)
    gated = {}

    def place(n):
        return slice(n // parts * seqs, (n // parts + 1) * seqs), lanes_of(n % parts)

    def score(n):
        rows, lanes = place(n)
        scores[n % 2] = dot(stacked(q[rows, lanes]), k_t[lanes, rows])

    def soften(n, _):
        for low in range(0, GROUP * seqs, 64):
            weights[n % 2, low : low + 64] = softmax_rounded(scores[n % 2, low : low + 64])

    def average(n, _):
        rows, lanes = place(n)
        mixed = own_lanes(dot(weights[n % 2], v[rows, lanes]))
        gated[n] = (mixed * g[rows, lanes]).astype(jnp.bfloat16)

    pipelined(at_once * parts, score, soften, average)
    gated = [
        jnp.concatenate([gated[n * parts + part] for part in range(parts)], axis=1)
        for n in range(at_once)
    ]
    after = x + (dot(jnp.concatenate(gated, axis=0), o_w[...]) + o_b[...])
    for n, rows in enumerate(mine):
        for part in range(parts):
            held[part, rows, :] = after[n * seqs : (n + 1) * seqs, lanes_of(part)]

    @pl.when(step == pl.num_programs(0) - 1)
    def _():
        for part in range(parts):
            out_ref[:, :, lanes_of(part)] = (
                held[part].reshape(owners, per, LANES).astype(jnp.bfloat16)
            )


def column_attention(items, half, before, x, gain, bias, q_w, k_w, v_w, g_w, g_b, o_w, o_b):
    width = x.shape[2]
    seqs = x.size // (items * width)
    at_once = 4
    whole = pl.BlockSpec(x.shape, lambda r: (0, 0, 0))
    vector = pl.BlockSpec((1, width), lambda r: (0, 0))
    weight = pl.BlockSpec((width, width), lambda r: (0, 0))
    return pl.pallas_call(
        functools.partial(column_kernel, at_once),
        grid=(items // at_once,),
        out_shape=[jax.ShapeDtypeStruct((DAP, HALVES * x.shape[1], width), jnp.bfloat16)],
        in_specs=[whole, vector, vector]
        + [weight] * 4
        + [vector, weight, vector]
        + [pl.BlockSpec(memory_space=pl.ANY)] * len(before),
        out_specs=[pl.BlockSpec(x.shape, lambda r: (0, half, 0))],
        input_output_aliases={10: 0} if before else {},
        scratch_shapes=[
            pltpu.VMEM((width // LANES, seqs * items, LANES), jnp.float32),
            pltpu.VMEM((2, GROUP * seqs, seqs), jnp.float32),
            pltpu.VMEM((2, GROUP * seqs, seqs), jnp.bfloat16),
        ],
        compiler_params=pltpu.CompilerParams(vmem_limit_bytes=24 * MIB),
        name="column_attention",
    )(
        x, gain.reshape(1, -1), bias.reshape(1, -1), q_w, k_w, v_w, g_w, g_b.reshape(1, -1),
        o_w, o_b.reshape(1, -1), *before,
    )


def fetch(value, z=0, x=0, y=0):
    pairs = []
    for dz in range(NZ):
        for dx in range(NX):
            for dy in range(NY):
                src = ((dz + z) % NZ * NX + (dx + x) % NX) * NY + (dy + y) % NY
                pairs.append((src, (dz * NX + dx) * NY + dy))
    return lax.ppermute(value, "dap", pairs)


def join_kernel(*refs):
    count = len(refs) - 2
    parts, out_ref, sems = refs[:count], refs[count], refs[count + 1]
    place, copies = 0, []
    for n, part in enumerate(parts):
        size = part.shape[0]
        copies.append(pltpu.make_async_copy(part, out_ref.at[pl.ds(place, size)], sems.at[n]))
        place += size
    for copy in copies:
        copy.start()
    for copy in copies:
        copy.wait()


def join(*parts):
    total = sum(part.shape[0] for part in parts)
    return pl.pallas_call(
        join_kernel,
        out_shape=jax.ShapeDtypeStruct((total,) + parts[0].shape[1:], parts[0].dtype),
        in_specs=[pl.BlockSpec(memory_space=pl.ANY)] * len(parts),
        out_specs=pl.BlockSpec(memory_space=pl.ANY),
        scratch_shapes=[pltpu.SemaphoreType.DMA((len(parts),))],
        compiler_params=pltpu.CompilerParams(vmem_limit_bytes=8 * MIB),
        name="join",
    )(*parts)


def exchange(value):
    return lax.all_to_all(value, "dap", split_axis=0, concat_axis=0, tiled=True)


def per_device(
    alignment,
    pair_state,
    row_norm_gain,
    row_norm_bias,
    pair_norm_gain,
    pair_weight,
    row_query,
    row_key,
    row_value,
    row_gate,
    row_gate_bias,
    row_output,
    row_output_bias,
    column_norm_gain,
    column_norm_bias,
    column_query,
    column_key,
    column_value,
    column_gate,
    column_gate_bias,
    column_output,
    column_output_bias,
):
    seqs, res, width = alignment.shape
    own = res // DAP
    me = lax.axis_index("dap")
    here = jnp.stack([me // (NX * NY), me // NY % NX, me % NY]).astype(jnp.int32)
    local = pair_bias(pair_state, pair_norm_gain, pair_weight)[None]
    pair = join(local, fetch(local, y=1))
    own_plane = join(pair, *(fetch(pair, x=step) for step in (1, 2, 3)))
    far_pair = fetch(pair, z=2)
    own_plane, far_pair, inputs = lax.optimization_barrier((own_plane, far_pair, alignment))
    ahead, behind = fetch(own_plane, z=1), fetch(own_plane, z=3)
    far_plane = join(far_pair, *(fetch(far_pair, x=step) for step in (1, 2, 3)))
    projected = row_project(
        inputs, row_norm_gain, row_norm_bias, row_query, row_key, row_value, row_gate, row_gate_bias
    )

    def attend(blocks, biases, *held):
        return row_attention(
            blocks, here, *projected, alignment, biases, row_output, row_output_bias, held
        )

    after = attend(((0, 0, 0), (0, 1, 0)), [own_plane])
    after = attend(((2, 0, 0), (2, 1, 0)), [far_plane], *after)
    first = attend(((1, 0, 0), (3, 0, 1)), [ahead, behind], after[0])[0]
    second = attend(((1, 1, 0), (3, 1, 1)), [ahead, behind], after[1])[0]
    first, second = lax.optimization_barrier((exchange(first), second))
    items = own // HALVES
    columns = ()
    for half, part in enumerate((first, exchange(second))):
        columns = column_attention(
            items,
            half,
            columns,
            part,
            column_norm_gain,
            column_norm_bias,
            column_query,
            column_key,
            column_value,
            column_gate,
            column_gate_bias,
            column_output,
            column_output_bias,
        )
    back = exchange(columns[0]).reshape(DAP, HALVES, seqs, items, width)
    return back.transpose(2, 0, 1, 3, 4).reshape(alignment.shape)


def solution(mesh):
    split = P(("batch", "dap"), None, None)
    return jax.shard_map(
        per_device,
        mesh=mesh,
        in_specs=(split, split) + (P(),) * 20,
        out_specs=split,
        check_vma=False,
    )
```

```python
import functools

import jax
import jax.numpy as jnp
from jax import lax
from jax.experimental import pallas as pl
from jax.experimental.pallas import tpu as pltpu
from jax.sharding import PartitionSpec as P

H = 8
HEAD = 32
C = 256
LANES = 128
GROUP = LANES // HEAD
EPS = 1e-05
MIB = 1024 * 1024
HALVES = 2
HALF_ROWS = 8
NZ, NX, NY = 4, 4, 2
DAP = NZ * NX * NY
NT = (((1,), (1,)), ((), ()))


def norm(x, gain, bias, center=None):
    if center is None:
        center = jnp.mean(x, axis=-1, keepdims=True)
    moved = x - center
    spread = jnp.mean(moved * moved, axis=-1, keepdims=True)
    return moved * lax.rsqrt(spread + EPS) * gain + bias


def lanes_of(part):
    return slice(part * LANES, (part + 1) * LANES)


def dot(a, b):
    return jnp.dot(a, b, preferred_element_type=jnp.float32)


def softmax_rounded(scores):
    top = jnp.max(scores, axis=-1, keepdims=True)
    e = jnp.exp(scores - top)
    total = jnp.sum(e, axis=-1, keepdims=True)
    return (e * (1.0 / total)).astype(jnp.bfloat16)


def head_of_lane():
    return lax.broadcasted_iota(jnp.int32, (1, LANES), 1) // HEAD


def stacked(q):
    head = head_of_lane()
    masks = [(head == i).astype(jnp.float32).astype(jnp.bfloat16) for i in range(GROUP)]
    return jnp.concatenate([q * mask for mask in masks], axis=0)


def own_lanes(mixed):
    head = head_of_lane()
    rows = mixed.shape[0] // GROUP
    total = mixed[:rows]
    for i in range(1, GROUP):
        total = jnp.where(head == i, mixed[i * rows : (i + 1) * rows], total)
    return total


def pipelined(count, score, soften, average):
    scores, weights = {0: score(0)}, {}
    for n in range(count + 1):
        if n + 1 < count:
            scores[n + 1] = score(n + 1)
        if n < count:
            weights[n] = soften(n, scores.pop(n))
        if n >= 1:
            average(n - 1, weights.pop(n - 1))


def project(normed, at_queries, q_w, k_w, v_w, g_w, g_b):
    q = (dot(at_queries, q_w[...]) * HEAD ** (-0.5)).astype(jnp.bfloat16)
    k_t = dot(normed, k_w[...]).T.astype(jnp.bfloat16)
    v = dot(normed, v_w[...]).astype(jnp.bfloat16)
    g = jax.nn.sigmoid(dot(at_queries, g_w[...]) + g_b[...])
    return q, k_t, v, g


def pair_kernel(x_ref, gain_ref, w_ref, out_ref, held):
    step = pl.program_id(0)
    rows, _, cz = x_ref.shape
    mean = jnp.full((cz, cz), 1.0 / cz, jnp.bfloat16)
    for i in range(rows):
        x = x_ref[i]
        normed = norm(x.astype(jnp.float32), gain_ref[...], 0.0, dot(x, mean)).astype(jnp.bfloat16)
        bias = lax.dot_general(w_ref[...], normed, NT, preferred_element_type=jnp.float32)
        for part in range(held.shape[0]):
            low = step * rows // HALF_ROWS * (H * HALF_ROWS) + lax.rem(step * rows, HALF_ROWS) + i
            held[part, pl.ds(low, H, stride=HALF_ROWS), :] = bias[:, lanes_of(part)]

    @pl.when(step == pl.num_programs(0) - 1)
    def _():
        for part in range(held.shape[0]):
            out_ref[:, :, lanes_of(part)] = (
                held[part].astype(jnp.bfloat16).reshape(out_ref.shape[:2] + (LANES,))
            )


def pair_bias(pair_state, gain, weight):
    count, res, cz = pair_state.shape
    rows = 4
    return pl.pallas_call(
        pair_kernel,
        grid=(count // rows,),
        out_shape=jax.ShapeDtypeStruct((H, count, res), jnp.bfloat16),
        in_specs=[
            pl.BlockSpec((rows, res, cz), lambda i: (i, 0, 0)),
            pl.BlockSpec((1, cz), lambda i: (0, 0)),
            pl.BlockSpec((H, cz), lambda i: (0, 0)),
        ],
        out_specs=pl.BlockSpec((H, count, res), lambda i: (0, 0, 0)),
        scratch_shapes=[pltpu.VMEM((res // LANES, H * count, LANES), jnp.float32)],
        compiler_params=pltpu.CompilerParams(vmem_limit_bytes=56 * MIB),
        name="pair_bias",
    )(pair_state, gain.reshape(1, cz), weight.T)


def project_kernel(x_ref, gain, bias, q_w, k_w, v_w, g_w, g_b, q_ref, k_ref, v_ref, g_ref):
    count, res, width = x_ref.shape
    x = x_ref[...].reshape(count * res, width).astype(jnp.float32)
    normed = norm(x, gain[...], bias[...])
    split = normed.reshape(count, DAP, HALVES, HALF_ROWS, width)
    halves = [split[:, :, half].reshape(count, res // HALVES, width) for half in range(HALVES)]
    at_queries = jnp.concatenate(halves, axis=1).reshape(count * res, width)
    q, k_t, v, g = project(
        normed.astype(jnp.bfloat16), at_queries.astype(jnp.bfloat16), q_w, k_w, v_w, g_w, g_b
    )
    for out_ref, value in ((q_ref, q), (v_ref, v), (g_ref, g)):
        out_ref[...] = value.reshape(count, res, width)
    for n in range(count):
        k_ref[n] = k_t[:, n * res : (n + 1) * res]


def row_project(x, gain, bias, q_w, k_w, v_w, g_w, g_b):
    seqs, res, width = x.shape
    count = 2
    block = pl.BlockSpec((count, res, width), lambda s: (s, 0, 0))
    turned = pl.BlockSpec((count, width, res), lambda s: (s, 0, 0))
    vector = pl.BlockSpec((1, width), lambda s: (0, 0))
    weight = pl.BlockSpec((width, width), lambda s: (0, 0))
    shape = jax.ShapeDtypeStruct
    return pl.pallas_call(
        project_kernel,
        grid=(seqs // count,),
        out_shape=[
            shape((seqs, res, width), jnp.bfloat16),
            shape((seqs, width, res), jnp.bfloat16),
            shape((seqs, res, width), jnp.bfloat16),
            shape((seqs, res, width), jnp.float32),
        ],
        in_specs=[block, vector, vector] + [weight] * 4 + [vector],
        out_specs=[block, turned, block, block],
        compiler_params=pltpu.CompilerParams(vmem_limit_bytes=56 * MIB),
        cost_estimate=pl.CostEstimate(
            flops=2 * seqs * res * width * width * 4,
            bytes_accessed=x.size * 12,
            transcendentals=x.size * 2,
        ),
        name="row_project",
    )(x, gain.reshape(1, -1), bias.reshape(1, -1), q_w, k_w, v_w, g_w, g_b.reshape(1, -1))


def row_kernel(blocks, here_ref, *refs):
    count = len(blocks)
    planes = 1 + max(which for _, _, which in blocks)
    q_refs, g_refs, x_refs, (k_ref, v_ref) = refs[:2], refs[2:4], refs[4:6], refs[6:8]
    bias_refs, (o_w, o_b) = refs[8 : 8 + planes], refs[8 + planes : 10 + planes]
    held, weights, ready, sems = refs[-4:]
    halves = sorted({half for _, half, _ in blocks})
    outs = dict(zip(halves, refs[-4 - len(halves) : -4]))
    step, last = pl.program_id(0), pl.num_programs(0) - 1
    seqs, part_rows, width = q_refs[0].shape
    tile = count * part_rows
    owners = part_rows // HALF_ROWS
    groups = H // GROUP

    def place(n):
        return n // groups, n % groups, lanes_of(n % groups)

    def both(pick):
        return jnp.concatenate([pick(n) for n in range(count)], axis=0)

    def score(n):
        seq, _, lanes = place(n)
        q = both(lambda b: q_refs[b][seq, :, lanes])
        held[n % 2] = dot(stacked(q), k_ref[seq, lanes, :])

    def slot(x, y):
        return lax.rem(x - here_ref[1] + NX, NX) * NY + lax.rem(y - here_ref[2] + NY, NY)

    slots = [slot(x, y) for x in range(NX) for y in range(NY)]
    taken = 4

    def soften(n, _):
        _, group, _ = place(n)
        for b, (_, half, which) in enumerate(blocks):
            for two in range(0, GROUP, 2):
                for first in range(0, owners, taken):
                    piece = (half * H + group * GROUP + two) // 2
                    bias = [
                        bias_refs[which][slots[o], piece].astype(jnp.float32)
                        for o in range(first, first + taken)
                    ]
                    for i in range(2):
                        low = (two + i) * tile + b * part_rows + first * HALF_ROWS
                        rows = slice(low, low + taken * HALF_ROWS)
                        mine = [value[i * HALF_ROWS : (i + 1) * HALF_ROWS] for value in bias]
                        weights[n % 2, rows] = softmax_rounded(
                            held[n % 2, rows] + jnp.concatenate(mine, axis=0)
                        )

    gated, done = {}, []

    def average(n, _):
        seq, group, lanes = place(n)
        mixed = own_lanes(dot(weights[n % 2], v_ref[seq, :, lanes]))
        gated[group] = (mixed * both(lambda b: g_refs[b][seq, :, lanes])).astype(jnp.bfloat16)
        if len(gated) == groups:
            whole = jnp.concatenate([gated.pop(part) for part in range(groups)], axis=1)
            update = dot(whole, o_w[...]) + o_b[...]
            after = []
            for b, (_, half, _) in enumerate(blocks):
                x = x_refs[b][seq].astype(jnp.float32).reshape(owners, HALVES, HALF_ROWS, width)
                own = update[b * part_rows : (b + 1) * part_rows].reshape(owners, HALF_ROWS, width)
                after.append(x[:, half] + own)
            done.append(after)
            if len(done) == 2:
                low = (seq - 1) * HALF_ROWS
                for b in range(count):
                    rows = jnp.concatenate([value[b] for value in done], axis=1)
                    ready[step, b, :, low : low + 2 * HALF_ROWS] = rows.astype(jnp.bfloat16)
                done.clear()

    pipelined(seqs * groups, score, soften, average)

    def copies(step):
        for b, (plane, half, _) in enumerate(blocks):
            first = pl.multiple_of(lax.rem(here_ref[0] + plane, NZ) * owners, owners)
            rows = pl.ds(pl.multiple_of(step * seqs * HALF_ROWS, seqs * HALF_ROWS), seqs * HALF_ROWS)
            yield pltpu.make_async_copy(
                ready.at[step, b], outs[half].at[pl.ds(first, owners), rows], sems.at[step, b]
            )

    for copy in copies(step):
        copy.start()

    @pl.when(step == last)
    def _():
        for n in range(ready.shape[0]):
            for copy in copies(n):
                copy.wait()


def row_attention(blocks, here, q, k, v, g, x, biases, o_w, o_b, held):
    seqs, res, width = x.shape
    own = res // DAP
    part_rows = DAP // NZ * HALF_ROWS
    once = 4
    halves = sorted({half for _, half, _ in blocks})

    def which(here, plane):
        return lax.rem(here[0] + plane, NZ)

    queries = [
        pl.BlockSpec(
            (once, part_rows, width),
            lambda s, here, plane=plane, half=half: (s, half * NZ + which(here, plane), 0),
        )
        for plane, half, _ in blocks
    ]
    residual = [
        pl.BlockSpec((once, res // NZ, width), lambda s, here, plane=plane: (s, which(here, plane), 0))
        for plane, _, _ in blocks
    ]
    args = [q, q, g, g, x, x, k, v, *biases, o_w, o_b.reshape(1, -1), *held]
    return pl.pallas_call(
        functools.partial(row_kernel, blocks),
        out_shape=[jax.ShapeDtypeStruct((DAP, seqs * HALF_ROWS, width), jnp.bfloat16)] * len(halves),
        grid_spec=pltpu.PrefetchScalarGridSpec(
            num_scalar_prefetch=1,
            grid=(seqs // once,),
            in_specs=queries
            + queries
            + residual
            + [
                pl.BlockSpec((once, width, res), lambda s, here: (s, 0, 0)),
                pl.BlockSpec((once, res, width), lambda s, here: (s, 0, 0)),
            ]
            + [pl.BlockSpec(bias.shape, lambda s, here: (0, 0, 0, 0)) for bias in biases]
            + [
                pl.BlockSpec((width, width), lambda s, here: (0, 0)),
                pl.BlockSpec((1, width), lambda s, here: (0, 0)),
            ]
            + [pl.BlockSpec(memory_space=pl.ANY)] * len(held),
            out_specs=[pl.BlockSpec(memory_space=pl.ANY)] * len(halves),
            scratch_shapes=[
                pltpu.VMEM((2, GROUP * part_rows * len(blocks), res), jnp.float32),
                pltpu.VMEM((2, GROUP * part_rows * len(blocks), res), jnp.bfloat16),
                pltpu.VMEM(
                    (seqs // once, len(blocks), DAP // NZ, once * HALF_ROWS, width), jnp.bfloat16
                ),
                pltpu.SemaphoreType.DMA((seqs // once, len(blocks))),
            ],
        ),
        input_output_aliases={len(args) + 1 - len(held) + n: n for n in range(len(held))},
        compiler_params=pltpu.CompilerParams(vmem_limit_bytes=56 * MIB),
        cost_estimate=pl.CostEstimate(
            flops=seqs * H * part_rows * len(blocks) * res * 256 * 16,
            bytes_accessed=8 * 1024 * 1024,
            transcendentals=seqs * H * part_rows * len(blocks) * res,
        ),
        name="row_attention",
    )(here, *args)


def column_kernel(at_once, x_ref, gain, bias, q_w, k_w, v_w, g_w, g_b, o_w, o_b, *refs):
    out_ref, held, scores, weights = refs[-4:]
    step = pl.program_id(0)
    owners, per, width = x_ref.shape
    items = pl.num_programs(0) * at_once
    seqs = owners * per // items
    parts = width // LANES

    @pl.when(step == 0)
    def _():
        for part in range(parts):
            held[part] = x_ref[:, :, lanes_of(part)].astype(jnp.float32).reshape(-1, LANES)

    mine = [pl.ds(step * at_once + n, seqs, stride=items) for n in range(at_once)]
    x = jnp.concatenate(
        [jnp.concatenate([held[part, rows, :] for rows in mine], axis=0) for part in range(parts)], axis=1
    )
    normed = norm(x, gain[...], bias[...]).astype(jnp.bfloat16)
    q, k_t, v, g = project(normed, normed, q_w, k_w, v_w, g_w, g_b)
    gated = {}

    def place(n):
        return slice(n // parts * seqs, (n // parts + 1) * seqs), lanes_of(n % parts)

    def score(n):
        rows, lanes = place(n)
        scores[n % 2] = dot(stacked(q[rows, lanes]), k_t[lanes, rows])

    def soften(n, _):
        for low in range(0, GROUP * seqs, 64):
            weights[n % 2, low : low + 64] = softmax_rounded(scores[n % 2, low : low + 64])

    def average(n, _):
        rows, lanes = place(n)
        mixed = own_lanes(dot(weights[n % 2], v[rows, lanes]))
        gated[n] = (mixed * g[rows, lanes]).astype(jnp.bfloat16)

    pipelined(at_once * parts, score, soften, average)
    gated = [
        jnp.concatenate([gated[n * parts + part] for part in range(parts)], axis=1)
        for n in range(at_once)
    ]
    after = x + (dot(jnp.concatenate(gated, axis=0), o_w[...]) + o_b[...])
    for n, rows in enumerate(mine):
        for part in range(parts):
            held[part, rows, :] = after[n * seqs : (n + 1) * seqs, lanes_of(part)]

    @pl.when(step == pl.num_programs(0) - 1)
    def _():
        for part in range(parts):
            out_ref[:, :, lanes_of(part)] = (
                held[part].reshape(owners, per, LANES).astype(jnp.bfloat16)
            )


def column_attention(items, half, before, x, gain, bias, q_w, k_w, v_w, g_w, g_b, o_w, o_b):
    width = x.shape[2]
    seqs = x.size // (items * width)
    at_once = 4
    whole = pl.BlockSpec(x.shape, lambda r: (0, 0, 0))
    vector = pl.BlockSpec((1, width), lambda r: (0, 0))
    weight = pl.BlockSpec((width, width), lambda r: (0, 0))
    return pl.pallas_call(
        functools.partial(column_kernel, at_once),
        grid=(items // at_once,),
        out_shape=[jax.ShapeDtypeStruct((DAP, HALVES * x.shape[1], width), jnp.bfloat16)],
        in_specs=[whole, vector, vector]
        + [weight] * 4
        + [vector, weight, vector]
        + [pl.BlockSpec(memory_space=pl.ANY)] * len(before),
        out_specs=[pl.BlockSpec(x.shape, lambda r: (0, half, 0))],
        input_output_aliases={10: 0} if before else {},
        scratch_shapes=[
            pltpu.VMEM((width // LANES, seqs * items, LANES), jnp.float32),
            pltpu.VMEM((2, GROUP * seqs, seqs), jnp.float32),
            pltpu.VMEM((2, GROUP * seqs, seqs), jnp.bfloat16),
        ],
        compiler_params=pltpu.CompilerParams(vmem_limit_bytes=56 * MIB),
        name="column_attention",
    )(
        x, gain.reshape(1, -1), bias.reshape(1, -1), q_w, k_w, v_w, g_w, g_b.reshape(1, -1),
        o_w, o_b.reshape(1, -1), *before,
    )


def fetch(value, z=0, x=0, y=0):
    pairs = []
    for dz in range(NZ):
        for dx in range(NX):
            for dy in range(NY):
                src = ((dz + z) % NZ * NX + (dx + x) % NX) * NY + (dy + y) % NY
                pairs.append((src, (dz * NX + dx) * NY + dy))
    return lax.ppermute(value, "dap", pairs)


def join_kernel(*refs):
    count = len(refs) - 2
    parts, out_ref, sems = refs[:count], refs[count], refs[count + 1]
    place, copies = 0, []
    for n, part in enumerate(parts):
        size = part.shape[0]
        copies.append(pltpu.make_async_copy(part, out_ref.at[pl.ds(place, size)], sems.at[n]))
        place += size
    for copy in copies:
        copy.start()
    for copy in copies:
        copy.wait()


def join(*parts):
    total = sum(part.shape[0] for part in parts)
    return pl.pallas_call(
        join_kernel,
        out_shape=jax.ShapeDtypeStruct((total,) + parts[0].shape[1:], parts[0].dtype),
        in_specs=[pl.BlockSpec(memory_space=pl.ANY)] * len(parts),
        out_specs=pl.BlockSpec(memory_space=pl.ANY),
        scratch_shapes=[pltpu.SemaphoreType.DMA((len(parts),))],
        compiler_params=pltpu.CompilerParams(vmem_limit_bytes=4 * MIB),
        name="join",
    )(*parts)


def exchange(value):
    return lax.all_to_all(value, "dap", split_axis=0, concat_axis=0, tiled=True)


def per_device(
    alignment,
    pair_state,
    row_norm_gain,
    row_norm_bias,
    pair_norm_gain,
    pair_weight,
    row_query,
    row_key,
    row_value,
    row_gate,
    row_gate_bias,
    row_output,
    row_output_bias,
    column_norm_gain,
    column_norm_bias,
    column_query,
    column_key,
    column_value,
    column_gate,
    column_gate_bias,
    column_output,
    column_output_bias,
):
    seqs, res, width = alignment.shape
    own = res // DAP
    me = lax.axis_index("dap")
    here = jnp.stack([me // (NX * NY), me // NY % NX, me % NY]).astype(jnp.int32)
    local = pair_bias(pair_state, pair_norm_gain, pair_weight)[None]
    pair = join(local, fetch(local, y=1))
    near = [fetch(pair, x=step) for step in (1, 2, 3)]
    far_pair = fetch(pair, z=2)
    pair, inputs = lax.optimization_barrier((pair, alignment))
    projected = row_project(
        inputs, row_norm_gain, row_norm_bias, row_query, row_key, row_value, row_gate, row_gate_bias
    )
    near, projected = lax.optimization_barrier((near, projected))
    own_plane = join(pair, *near)
    far_pair, own_plane = lax.optimization_barrier((far_pair, own_plane))
    ahead, behind = fetch(own_plane, z=1), fetch(own_plane, z=3)
    far_plane = join(far_pair, *(fetch(far_pair, x=step) for step in (1, 2, 3)))

    def attend(blocks, biases, *held):
        return row_attention(
            blocks, here, *projected, alignment, biases, row_output, row_output_bias, held
        )

    after = attend(((0, 0, 0), (0, 1, 0)), [own_plane])
    after = attend(((2, 0, 0), (2, 1, 0)), [far_plane], *after)
    first = attend(((1, 0, 0), (3, 0, 1)), [ahead, behind], after[0])[0]
    second = attend(((1, 1, 0), (3, 1, 1)), [ahead, behind], after[1])[0]
    first, second = lax.optimization_barrier((exchange(first), second))
    items = own // HALVES
    columns = ()
    for half, part in enumerate((first, exchange(second))):
        columns = column_attention(
            items,
            half,
            columns,
            part,
            column_norm_gain,
            column_norm_bias,
            column_query,
            column_key,
            column_value,
            column_gate,
            column_gate_bias,
            column_output,
            column_output_bias,
        )
    back = exchange(columns[0]).reshape(DAP, HALVES, seqs, items, width)
    return back.transpose(2, 0, 1, 3, 4).reshape(alignment.shape)


def solution(mesh):
    split = P(("batch", "dap"), None, None)
    return jax.shard_map(
        per_device,
        mesh=mesh,
        in_specs=(split, split) + (P(),) * 20,
        out_specs=split,
        check_vma=False,
    )
```

```python
import functools

import jax
import jax.numpy as jnp
from jax import lax
from jax.experimental import pallas as pl
from jax.experimental.pallas import tpu as pltpu
from jax.sharding import PartitionSpec as P

H = 8
HEAD = 32
C = 256
LANES = 128
GROUP = LANES // HEAD
EPS = 1e-05
MIB = 1024 * 1024
HALVES = 2
HALF_ROWS = 8
NZ, NX, NY = 4, 4, 2
DAP = NZ * NX * NY
NT = (((1,), (1,)), ((), ()))


def norm(x, gain, bias, center=None):
    if center is None:
        center = jnp.mean(x, axis=-1, keepdims=True)
    moved = x - center
    spread = jnp.mean(moved * moved, axis=-1, keepdims=True)
    return moved * lax.rsqrt(spread + EPS) * gain + bias


def lanes_of(part):
    return slice(part * LANES, (part + 1) * LANES)


def dot(a, b):
    return jnp.dot(a, b, preferred_element_type=jnp.float32)


def softmax_rounded(scores):
    top = jnp.max(scores, axis=-1, keepdims=True)
    e = jnp.exp(scores - top)
    total = jnp.sum(e, axis=-1, keepdims=True)
    guess = pl.reciprocal(total, approx=True)
    return (e * (guess * (2.0 - total * guess))).astype(jnp.bfloat16)


def head_of_lane():
    return lax.broadcasted_iota(jnp.int32, (1, LANES), 1) // HEAD


def stacked(q):
    head = head_of_lane()
    masks = [(head == i).astype(jnp.float32).astype(jnp.bfloat16) for i in range(GROUP)]
    return jnp.concatenate([q * mask for mask in masks], axis=0)


def own_lanes(mixed):
    head = head_of_lane()
    rows = mixed.shape[0] // GROUP
    total = mixed[:rows]
    for i in range(1, GROUP):
        total = jnp.where(head == i, mixed[i * rows : (i + 1) * rows], total)
    return total


def pipelined(count, score, soften, average):
    scores, weights = {0: score(0)}, {}
    for n in range(count + 1):
        if n + 1 < count:
            scores[n + 1] = score(n + 1)
        if n < count:
            weights[n] = soften(n, scores.pop(n))
        if n >= 1:
            average(n - 1, weights.pop(n - 1))


def project(normed, at_queries, q_w, k_w, v_w, g_w, g_b):
    q = (dot(at_queries, q_w[...]) * HEAD ** (-0.5)).astype(jnp.bfloat16)
    k_t = dot(normed, k_w[...]).T.astype(jnp.bfloat16)
    v = dot(normed, v_w[...]).astype(jnp.bfloat16)
    g = 0.5 * jnp.tanh(0.5 * (dot(at_queries, g_w[...]) + g_b[...])) + 0.5
    return q, k_t, v, g


def pair_kernel(x_ref, gain_ref, w_ref, out_ref, held):
    step = pl.program_id(0)
    rows, _, cz = x_ref.shape
    mean = jnp.full((cz, cz), 1.0 / cz, jnp.bfloat16)
    for i in range(rows):
        x = x_ref[i]
        normed = norm(x.astype(jnp.float32), gain_ref[...], 0.0, dot(x, mean)).astype(jnp.bfloat16)
        bias = lax.dot_general(w_ref[...], normed, NT, preferred_element_type=jnp.float32)
        for part in range(held.shape[0]):
            low = step * rows // HALF_ROWS * (H * HALF_ROWS) + lax.rem(step * rows, HALF_ROWS) + i
            held[part, pl.ds(low, H, stride=HALF_ROWS), :] = bias[:, lanes_of(part)]

    @pl.when(step == pl.num_programs(0) - 1)
    def _():
        for part in range(held.shape[0]):
            out_ref[:, :, lanes_of(part)] = (
                held[part].astype(jnp.bfloat16).reshape(out_ref.shape[:2] + (LANES,))
            )


def pair_bias(pair_state, gain, weight):
    count, res, cz = pair_state.shape
    rows = 4
    return pl.pallas_call(
        pair_kernel,
        grid=(count // rows,),
        out_shape=jax.ShapeDtypeStruct((H, count, res), jnp.bfloat16),
        in_specs=[
            pl.BlockSpec((rows, res, cz), lambda i: (i, 0, 0)),
            pl.BlockSpec((1, cz), lambda i: (0, 0)),
            pl.BlockSpec((H, cz), lambda i: (0, 0)),
        ],
        out_specs=pl.BlockSpec((H, count, res), lambda i: (0, 0, 0)),
        scratch_shapes=[pltpu.VMEM((res // LANES, H * count, LANES), jnp.float32)],
        compiler_params=pltpu.CompilerParams(vmem_limit_bytes=56 * MIB),
        name="pair_bias",
    )(pair_state, gain.reshape(1, cz), weight.T)


def project_kernel(x_ref, gain, bias, q_w, k_w, v_w, g_w, g_b, q_ref, k_ref, v_ref, g_ref):
    count, res, width = x_ref.shape
    x = x_ref[...].reshape(count * res, width).astype(jnp.float32)
    normed = norm(x, gain[...], bias[...])
    split = normed.reshape(count, DAP, HALVES, HALF_ROWS, width)
    halves = [split[:, :, half].reshape(count, res // HALVES, width) for half in range(HALVES)]
    at_queries = jnp.concatenate(halves, axis=1).reshape(count * res, width)
    q, k_t, v, g = project(
        normed.astype(jnp.bfloat16), at_queries.astype(jnp.bfloat16), q_w, k_w, v_w, g_w, g_b
    )
    for out_ref, value in ((q_ref, q), (v_ref, v), (g_ref, g)):
        out_ref[...] = value.reshape(count, res, width)
    for n in range(count):
        k_ref[n] = k_t[:, n * res : (n + 1) * res]


def row_project(x, gain, bias, q_w, k_w, v_w, g_w, g_b):
    seqs, res, width = x.shape
    count = 2
    block = pl.BlockSpec((count, res, width), lambda s: (s, 0, 0))
    turned = pl.BlockSpec((count, width, res), lambda s: (s, 0, 0))
    vector = pl.BlockSpec((1, width), lambda s: (0, 0))
    weight = pl.BlockSpec((width, width), lambda s: (0, 0))
    shape = jax.ShapeDtypeStruct
    return pl.pallas_call(
        project_kernel,
        grid=(seqs // count,),
        out_shape=[
            shape((seqs, res, width), jnp.bfloat16),
            shape((seqs, width, res), jnp.bfloat16),
            shape((seqs, res, width), jnp.bfloat16),
            shape((seqs, res, width), jnp.float32),
        ],
        in_specs=[block, vector, vector] + [weight] * 4 + [vector],
        out_specs=[block, turned, block, block],
        compiler_params=pltpu.CompilerParams(vmem_limit_bytes=56 * MIB),
        cost_estimate=pl.CostEstimate(
            flops=2 * seqs * res * width * width * 4,
            bytes_accessed=x.size * 12,
            transcendentals=x.size * 2,
        ),
        name="row_project",
    )(x, gain.reshape(1, -1), bias.reshape(1, -1), q_w, k_w, v_w, g_w, g_b.reshape(1, -1))


def row_kernel(blocks, here_ref, *refs):
    count = len(blocks)
    planes = 1 + max(which for _, _, which in blocks)
    q_refs, g_refs, x_refs, (k_ref, v_ref) = refs[:2], refs[2:4], refs[4:6], refs[6:8]
    bias_refs, (o_w, o_b) = refs[8 : 8 + planes], refs[8 + planes : 10 + planes]
    held, weights, ready, sems = refs[-4:]
    halves = sorted({half for _, half, _ in blocks})
    outs = dict(zip(halves, refs[-4 - len(halves) : -4]))
    step, last = pl.program_id(0), pl.num_programs(0) - 1
    seqs, part_rows, width = q_refs[0].shape
    tile = count * part_rows
    owners = part_rows // HALF_ROWS
    groups = H // GROUP

    def place(n):
        return n // groups, n % groups, lanes_of(n % groups)

    def both(pick):
        return jnp.concatenate([pick(n) for n in range(count)], axis=0)

    def score(n):
        seq, _, lanes = place(n)
        q = both(lambda b: q_refs[b][seq, :, lanes])
        held[n % 2] = dot(stacked(q), k_ref[seq, lanes, :])

    def slot(x, y):
        return lax.rem(x - here_ref[1] + NX, NX) * NY + lax.rem(y - here_ref[2] + NY, NY)

    slots = [slot(x, y) for x in range(NX) for y in range(NY)]
    taken = 4

    def soften(n, _):
        _, group, _ = place(n)
        for b, (_, half, which) in enumerate(blocks):
            for two in range(0, GROUP, 2):
                for first in range(0, owners, taken):
                    piece = (half * H + group * GROUP + two) // 2
                    bias = [
                        bias_refs[which][slots[o], piece].astype(jnp.float32)
                        for o in range(first, first + taken)
                    ]
                    for i in range(2):
                        low = (two + i) * tile + b * part_rows + first * HALF_ROWS
                        rows = slice(low, low + taken * HALF_ROWS)
                        mine = [value[i * HALF_ROWS : (i + 1) * HALF_ROWS] for value in bias]
                        weights[n % 2, rows] = softmax_rounded(
                            held[n % 2, rows] + jnp.concatenate(mine, axis=0)
                        )

    gated, done = {}, []

    def average(n, _):
        seq, group, lanes = place(n)
        mixed = own_lanes(dot(weights[n % 2], v_ref[seq, :, lanes]))
        gated[group] = (mixed * both(lambda b: g_refs[b][seq, :, lanes])).astype(jnp.bfloat16)
        if len(gated) == groups:
            whole = jnp.concatenate([gated.pop(part) for part in range(groups)], axis=1)
            update = dot(whole, o_w[...]) + o_b[...]
            after = []
            for b, (_, half, _) in enumerate(blocks):
                x = x_refs[b][seq].astype(jnp.float32).reshape(owners, HALVES, HALF_ROWS, width)
                own = update[b * part_rows : (b + 1) * part_rows].reshape(owners, HALF_ROWS, width)
                after.append(x[:, half] + own)
            done.append(after)
            if len(done) == 2:
                low = (seq - 1) * HALF_ROWS
                for b in range(count):
                    rows = jnp.concatenate([value[b] for value in done], axis=1)
                    ready[step, b, :, low : low + 2 * HALF_ROWS] = rows.astype(jnp.bfloat16)
                done.clear()

    pipelined(seqs * groups, score, soften, average)

    def copies(step):
        for b, (plane, half, _) in enumerate(blocks):
            first = pl.multiple_of(lax.rem(here_ref[0] + plane, NZ) * owners, owners)
            rows = pl.ds(pl.multiple_of(step * seqs * HALF_ROWS, seqs * HALF_ROWS), seqs * HALF_ROWS)
            yield pltpu.make_async_copy(
                ready.at[step, b], outs[half].at[pl.ds(first, owners), rows], sems.at[step, b]
            )

    for copy in copies(step):
        copy.start()

    @pl.when(step == last)
    def _():
        for n in range(ready.shape[0]):
            for copy in copies(n):
                copy.wait()


def row_attention(blocks, here, q, k, v, g, x, biases, o_w, o_b, held):
    seqs, res, width = x.shape
    own = res // DAP
    part_rows = DAP // NZ * HALF_ROWS
    once = 4
    halves = sorted({half for _, half, _ in blocks})

    def which(here, plane):
        return lax.rem(here[0] + plane, NZ)

    queries = [
        pl.BlockSpec(
            (once, part_rows, width),
            lambda s, here, plane=plane, half=half: (s, half * NZ + which(here, plane), 0),
        )
        for plane, half, _ in blocks
    ]
    residual = [
        pl.BlockSpec((once, res // NZ, width), lambda s, here, plane=plane: (s, which(here, plane), 0))
        for plane, _, _ in blocks
    ]
    args = [q, q, g, g, x, x, k, v, *biases, o_w, o_b.reshape(1, -1), *held]
    return pl.pallas_call(
        functools.partial(row_kernel, blocks),
        out_shape=[jax.ShapeDtypeStruct((DAP, seqs * HALF_ROWS, width), jnp.bfloat16)] * len(halves),
        grid_spec=pltpu.PrefetchScalarGridSpec(
            num_scalar_prefetch=1,
            grid=(seqs // once,),
            in_specs=queries
            + queries
            + residual
            + [
                pl.BlockSpec((once, width, res), lambda s, here: (s, 0, 0)),
                pl.BlockSpec((once, res, width), lambda s, here: (s, 0, 0)),
            ]
            + [pl.BlockSpec(bias.shape, lambda s, here: (0, 0, 0, 0)) for bias in biases]
            + [
                pl.BlockSpec((width, width), lambda s, here: (0, 0)),
                pl.BlockSpec((1, width), lambda s, here: (0, 0)),
            ]
            + [pl.BlockSpec(memory_space=pl.ANY)] * len(held),
            out_specs=[pl.BlockSpec(memory_space=pl.ANY)] * len(halves),
            scratch_shapes=[
                pltpu.VMEM((2, GROUP * part_rows * len(blocks), res), jnp.float32),
                pltpu.VMEM((2, GROUP * part_rows * len(blocks), res), jnp.bfloat16),
                pltpu.VMEM(
                    (seqs // once, len(blocks), DAP // NZ, once * HALF_ROWS, width), jnp.bfloat16
                ),
                pltpu.SemaphoreType.DMA((seqs // once, len(blocks))),
            ],
        ),
        input_output_aliases={len(args) + 1 - len(held) + n: n for n in range(len(held))},
        compiler_params=pltpu.CompilerParams(vmem_limit_bytes=56 * MIB),
        cost_estimate=pl.CostEstimate(
            flops=seqs * H * part_rows * len(blocks) * res * 256 * 16,
            bytes_accessed=8 * 1024 * 1024,
            transcendentals=seqs * H * part_rows * len(blocks) * res,
        ),
        name="row_attention",
    )(here, *args)


def column_kernel(at_once, x_ref, gain, bias, q_w, k_w, v_w, g_w, g_b, o_w, o_b, *refs):
    out_ref, held, scores, weights = refs[-4:]
    step = pl.program_id(0)
    owners, per, width = x_ref.shape
    items = pl.num_programs(0) * at_once
    seqs = owners * per // items
    parts = width // LANES

    @pl.when(step == 0)
    def _():
        for part in range(parts):
            held[part] = x_ref[:, :, lanes_of(part)].astype(jnp.float32).reshape(-1, LANES)

    mine = [pl.ds(step * at_once + n, seqs, stride=items) for n in range(at_once)]
    x = jnp.concatenate(
        [jnp.concatenate([held[part, rows, :] for rows in mine], axis=0) for part in range(parts)], axis=1
    )
    normed = norm(x, gain[...], bias[...]).astype(jnp.bfloat16)
    q, k_t, v, g = project(normed, normed, q_w, k_w, v_w, g_w, g_b)
    gated = {}

    def place(n):
        return slice(n // parts * seqs, (n // parts + 1) * seqs), lanes_of(n % parts)

    def score(n):
        rows, lanes = place(n)
        scores[n % 2] = dot(stacked(q[rows, lanes]), k_t[lanes, rows])

    def soften(n, _):
        for low in range(0, GROUP * seqs, 64):
            weights[n % 2, low : low + 64] = softmax_rounded(scores[n % 2, low : low + 64])

    def average(n, _):
        rows, lanes = place(n)
        mixed = own_lanes(dot(weights[n % 2], v[rows, lanes]))
        gated[n] = (mixed * g[rows, lanes]).astype(jnp.bfloat16)

    pipelined(at_once * parts, score, soften, average)
    gated = [
        jnp.concatenate([gated[n * parts + part] for part in range(parts)], axis=1)
        for n in range(at_once)
    ]
    after = x + (dot(jnp.concatenate(gated, axis=0), o_w[...]) + o_b[...])
    for n, rows in enumerate(mine):
        for part in range(parts):
            held[part, rows, :] = after[n * seqs : (n + 1) * seqs, lanes_of(part)]

    @pl.when(step == pl.num_programs(0) - 1)
    def _():
        for part in range(parts):
            out_ref[:, :, lanes_of(part)] = (
                held[part].reshape(owners, per, LANES).astype(jnp.bfloat16)
            )


def column_attention(items, half, before, x, gain, bias, q_w, k_w, v_w, g_w, g_b, o_w, o_b):
    width = x.shape[2]
    seqs = x.size // (items * width)
    at_once = 4
    whole = pl.BlockSpec(x.shape, lambda r: (0, 0, 0))
    vector = pl.BlockSpec((1, width), lambda r: (0, 0))
    weight = pl.BlockSpec((width, width), lambda r: (0, 0))
    return pl.pallas_call(
        functools.partial(column_kernel, at_once),
        grid=(items // at_once,),
        out_shape=[jax.ShapeDtypeStruct((DAP, HALVES * x.shape[1], width), jnp.bfloat16)],
        in_specs=[whole, vector, vector]
        + [weight] * 4
        + [vector, weight, vector]
        + [pl.BlockSpec(memory_space=pl.ANY)] * len(before),
        out_specs=[pl.BlockSpec(x.shape, lambda r: (0, half, 0))],
        input_output_aliases={10: 0} if before else {},
        scratch_shapes=[
            pltpu.VMEM((width // LANES, seqs * items, LANES), jnp.float32),
            pltpu.VMEM((2, GROUP * seqs, seqs), jnp.float32),
            pltpu.VMEM((2, GROUP * seqs, seqs), jnp.bfloat16),
        ],
        compiler_params=pltpu.CompilerParams(vmem_limit_bytes=56 * MIB),
        name="column_attention",
    )(
        x, gain.reshape(1, -1), bias.reshape(1, -1), q_w, k_w, v_w, g_w, g_b.reshape(1, -1),
        o_w, o_b.reshape(1, -1), *before,
    )


def fetch(value, z=0, x=0, y=0):
    pairs = []
    for dz in range(NZ):
        for dx in range(NX):
            for dy in range(NY):
                src = ((dz + z) % NZ * NX + (dx + x) % NX) * NY + (dy + y) % NY
                pairs.append((src, (dz * NX + dx) * NY + dy))
    return lax.ppermute(value, "dap", pairs)


def join_kernel(*refs):
    count = len(refs) - 2
    parts, out_ref, sems = refs[:count], refs[count], refs[count + 1]
    place, copies = 0, []
    for n, part in enumerate(parts):
        size = part.shape[0]
        copies.append(pltpu.make_async_copy(part, out_ref.at[pl.ds(place, size)], sems.at[n]))
        place += size
    for copy in copies:
        copy.start()
    for copy in copies:
        copy.wait()


def join(*parts):
    total = sum(part.shape[0] for part in parts)
    return pl.pallas_call(
        join_kernel,
        out_shape=jax.ShapeDtypeStruct((total,) + parts[0].shape[1:], parts[0].dtype),
        in_specs=[pl.BlockSpec(memory_space=pl.ANY)] * len(parts),
        out_specs=pl.BlockSpec(memory_space=pl.ANY),
        scratch_shapes=[pltpu.SemaphoreType.DMA((len(parts),))],
        compiler_params=pltpu.CompilerParams(vmem_limit_bytes=4 * MIB),
        name="join",
    )(*parts)


def exchange(value):
    return lax.all_to_all(value, "dap", split_axis=0, concat_axis=0, tiled=True)


def per_device(
    alignment,
    pair_state,
    row_norm_gain,
    row_norm_bias,
    pair_norm_gain,
    pair_weight,
    row_query,
    row_key,
    row_value,
    row_gate,
    row_gate_bias,
    row_output,
    row_output_bias,
    column_norm_gain,
    column_norm_bias,
    column_query,
    column_key,
    column_value,
    column_gate,
    column_gate_bias,
    column_output,
    column_output_bias,
):
    seqs, res, width = alignment.shape
    own = res // DAP
    me = lax.axis_index("dap")
    here = jnp.stack([me // (NX * NY), me // NY % NX, me % NY]).astype(jnp.int32)
    local = pair_bias(pair_state, pair_norm_gain, pair_weight)[None]
    pair = join(local, fetch(local, y=1))
    near = [fetch(pair, x=step) for step in (1, 2, 3)]
    far_pair = fetch(pair, z=2)
    pair, inputs = lax.optimization_barrier((pair, alignment))
    projected = row_project(
        inputs, row_norm_gain, row_norm_bias, row_query, row_key, row_value, row_gate, row_gate_bias
    )
    near, projected = lax.optimization_barrier((near, projected))
    own_plane = join(pair, *near)
    far_pair, own_plane = lax.optimization_barrier((far_pair, own_plane))
    ahead, behind = fetch(own_plane, z=1), fetch(own_plane, z=3)
    far_plane = join(far_pair, *(fetch(far_pair, x=step) for step in (1, 2, 3)))

    def attend(blocks, biases, *held):
        return row_attention(
            blocks, here, *projected, alignment, biases, row_output, row_output_bias, held
        )

    after = attend(((0, 0, 0), (0, 1, 0)), [own_plane])
    after = attend(((2, 0, 0), (2, 1, 0)), [far_plane], *after)
    first = attend(((1, 0, 0), (3, 0, 1)), [ahead, behind], after[0])[0]
    second = attend(((1, 1, 0), (3, 1, 1)), [ahead, behind], after[1])[0]
    first, second = lax.optimization_barrier((exchange(first), second))
    items = own // HALVES
    columns = ()
    for half, part in enumerate((first, exchange(second))):
        columns = column_attention(
            items,
            half,
            columns,
            part,
            column_norm_gain,
            column_norm_bias,
            column_query,
            column_key,
            column_value,
            column_gate,
            column_gate_bias,
            column_output,
            column_output_bias,
        )
    back = exchange(columns[0]).reshape(DAP, HALVES, seqs, items, width)
    return back.transpose(2, 0, 1, 3, 4).reshape(alignment.shape)


def solution(mesh):
    split = P(("batch", "dap"), None, None)
    return jax.shard_map(
        per_device,
        mesh=mesh,
        in_specs=(split, split) + (P(),) * 20,
        out_specs=split,
        check_vma=False,
    )
```

```python
import functools

import jax
import jax.numpy as jnp
from jax import lax
from jax.experimental import pallas as pl
from jax.experimental.pallas import tpu as pltpu
from jax.sharding import PartitionSpec as P

H = 8
HEAD = 32
C = 256
LANES = 128
GROUP = LANES // HEAD
EPS = 1e-05
MIB = 1024 * 1024
HALVES = 2
HALF_ROWS = 8
NZ, NX, NY = 4, 4, 2
PLANE = NX * NY
DAP = NZ * PLANE
NT = (((1,), (1,)), ((), ()))


def norm(x, gain, bias, center=None):
    if center is None:
        center = jnp.mean(x, axis=-1, keepdims=True)
    moved = x - center
    spread = jnp.mean(moved * moved, axis=-1, keepdims=True)
    return moved * lax.rsqrt(spread + EPS) * gain + bias


def lanes_of(part):
    return slice(part * LANES, (part + 1) * LANES)


def dot(a, b):
    return jnp.dot(a, b, preferred_element_type=jnp.float32)


def softmax_rounded(scores):
    top = jnp.max(scores, axis=-1, keepdims=True)
    e = jnp.exp(scores - top)
    total = jnp.sum(e, axis=-1, keepdims=True)
    return (e * (1.0 / total)).astype(jnp.bfloat16)


def head_of_lane():
    return lax.broadcasted_iota(jnp.int32, (1, LANES), 1) // HEAD


def stacked(q):
    head = head_of_lane()
    masks = [(head == i).astype(jnp.float32).astype(jnp.bfloat16) for i in range(GROUP)]
    return jnp.concatenate([q * mask for mask in masks], axis=0)


def own_lanes(mixed):
    head = head_of_lane()
    rows = mixed.shape[0] // GROUP
    total = mixed[:rows]
    for i in range(1, GROUP):
        total = jnp.where(head == i, mixed[i * rows : (i + 1) * rows], total)
    return total


def pipelined(count, score, soften, average):
    scores, weights = {0: score(0)}, {}
    for n in range(count + 1):
        if n + 1 < count:
            scores[n + 1] = score(n + 1)
        if n < count:
            weights[n] = soften(n, scores.pop(n))
        if n >= 1:
            average(n - 1, weights.pop(n - 1))


def project(normed, at_queries, q_w, k_w, v_w, g_w, g_b):
    q = (dot(at_queries, q_w[...]) * HEAD ** (-0.5)).astype(jnp.bfloat16)
    k_t = dot(normed, k_w[...]).T.astype(jnp.bfloat16)
    v = dot(normed, v_w[...]).astype(jnp.bfloat16)
    g = jax.nn.sigmoid(dot(at_queries, g_w[...]) + g_b[...])
    return q, k_t, v, g


def pair_kernel(x_ref, gain_ref, w_ref, out_ref, copies_ref, held):
    step = pl.program_id(0)
    rows, _, cz = x_ref.shape
    mean = jnp.full((cz, cz), 1.0 / cz, jnp.bfloat16)
    for i in range(rows):
        x = x_ref[i]
        normed = norm(x.astype(jnp.float32), gain_ref[...], 0.0, dot(x, mean)).astype(jnp.bfloat16)
        bias = lax.dot_general(w_ref[...], normed, NT, preferred_element_type=jnp.float32)
        for part in range(held.shape[0]):
            low = step * rows // HALF_ROWS * (H * HALF_ROWS) + lax.rem(step * rows, HALF_ROWS) + i
            held[part, pl.ds(low, H, stride=HALF_ROWS), :] = bias[:, lanes_of(part)]

    @pl.when(step == pl.num_programs(0) - 1)
    def _():
        for part in range(held.shape[0]):
            value = held[part].astype(jnp.bfloat16).reshape(out_ref.shape[:2] + (LANES,))
            out_ref[:, :, lanes_of(part)] = value
            for n in range(PLANE):
                copies_ref[n, :, :, lanes_of(part)] = value


def pair_bias(pair_state, gain, weight):
    count, res, cz = pair_state.shape
    rows = 4
    return pl.pallas_call(
        pair_kernel,
        grid=(count // rows,),
        out_shape=[
            jax.ShapeDtypeStruct((H, count, res), jnp.bfloat16),
            jax.ShapeDtypeStruct((PLANE, H, count, res), jnp.bfloat16),
        ],
        in_specs=[
            pl.BlockSpec((rows, res, cz), lambda i: (i, 0, 0)),
            pl.BlockSpec((1, cz), lambda i: (0, 0)),
            pl.BlockSpec((H, cz), lambda i: (0, 0)),
        ],
        out_specs=[
            pl.BlockSpec((H, count, res), lambda i: (0, 0, 0)),
            pl.BlockSpec((PLANE, H, count, res), lambda i: (0, 0, 0, 0)),
        ],
        scratch_shapes=[pltpu.VMEM((res // LANES, H * count, LANES), jnp.float32)],
        compiler_params=pltpu.CompilerParams(vmem_limit_bytes=56 * MIB),
        name="pair_bias",
    )(pair_state, gain.reshape(1, cz), weight.T)


def project_kernel(x_ref, gain, bias, q_w, k_w, v_w, g_w, g_b, q_ref, k_ref, v_ref, g_ref):
    count, res, width = x_ref.shape
    x = x_ref[...].reshape(count * res, width).astype(jnp.float32)
    normed = norm(x, gain[...], bias[...])
    split = normed.reshape(count, DAP, HALVES, HALF_ROWS, width)
    halves = [split[:, :, half].reshape(count, res // HALVES, width) for half in range(HALVES)]
    at_queries = jnp.concatenate(halves, axis=1).reshape(count * res, width)
    q, k_t, v, g = project(
        normed.astype(jnp.bfloat16), at_queries.astype(jnp.bfloat16), q_w, k_w, v_w, g_w, g_b
    )
    for out_ref, value in ((q_ref, q), (v_ref, v), (g_ref, g)):
        out_ref[...] = value.reshape(count, res, width)
    for n in range(count):
        k_ref[n] = k_t[:, n * res : (n + 1) * res]


def row_project(x, gain, bias, q_w, k_w, v_w, g_w, g_b):
    seqs, res, width = x.shape
    count = 2
    block = pl.BlockSpec((count, res, width), lambda s: (s, 0, 0))
    turned = pl.BlockSpec((count, width, res), lambda s: (s, 0, 0))
    vector = pl.BlockSpec((1, width), lambda s: (0, 0))
    weight = pl.BlockSpec((width, width), lambda s: (0, 0))
    shape = jax.ShapeDtypeStruct
    return pl.pallas_call(
        project_kernel,
        grid=(seqs // count,),
        out_shape=[
            shape((seqs, res, width), jnp.bfloat16),
            shape((seqs, width, res), jnp.bfloat16),
            shape((seqs, res, width), jnp.bfloat16),
            shape((seqs, res, width), jnp.float32),
        ],
        in_specs=[block, vector, vector] + [weight] * 4 + [vector],
        out_specs=[block, turned, block, block],
        compiler_params=pltpu.CompilerParams(vmem_limit_bytes=56 * MIB),
        cost_estimate=pl.CostEstimate(
            flops=2 * seqs * res * width * width * 4,
            bytes_accessed=x.size * 12,
            transcendentals=x.size * 2,
        ),
        name="row_project",
    )(x, gain.reshape(1, -1), bias.reshape(1, -1), q_w, k_w, v_w, g_w, g_b.reshape(1, -1))


def row_kernel(blocks, here_ref, *refs):
    count = len(blocks)
    planes = 1 + max(which for _, _, which in blocks)
    q_refs, g_refs, x_refs, (k_ref, v_ref) = refs[:2], refs[2:4], refs[4:6], refs[6:8]
    bias_refs, (o_w, o_b) = refs[8 : 8 + planes], refs[8 + planes : 10 + planes]
    held, weights, ready, sems = refs[-4:]
    halves = sorted({half for _, half, _ in blocks})
    outs = dict(zip(halves, refs[-4 - len(halves) : -4]))
    step, last = pl.program_id(0), pl.num_programs(0) - 1
    seqs, part_rows, width = q_refs[0].shape
    tile = count * part_rows
    owners = part_rows // HALF_ROWS
    groups = H // GROUP

    def place(n):
        return n // groups, n % groups, lanes_of(n % groups)

    def both(pick):
        return jnp.concatenate([pick(n) for n in range(count)], axis=0)

    def score(n):
        seq, _, lanes = place(n)
        q = both(lambda b: q_refs[b][seq, :, lanes])
        held[n % 2] = dot(stacked(q), k_ref[seq, lanes, :])

    taken = 4

    def soften(n, _):
        _, group, _ = place(n)
        for b, (_, half, which) in enumerate(blocks):
            for two in range(0, GROUP, 2):
                for first in range(0, owners, taken):
                    piece = (half * H + group * GROUP + two) // 2
                    bias = [
                        bias_refs[which][o, piece].astype(jnp.float32)
                        for o in range(first, first + taken)
                    ]
                    for i in range(2):
                        low = (two + i) * tile + b * part_rows + first * HALF_ROWS
                        rows = slice(low, low + taken * HALF_ROWS)
                        mine = [value[i * HALF_ROWS : (i + 1) * HALF_ROWS] for value in bias]
                        weights[n % 2, rows] = softmax_rounded(
                            held[n % 2, rows] + jnp.concatenate(mine, axis=0)
                        )

    gated, done = {}, []

    def average(n, _):
        seq, group, lanes = place(n)
        mixed = own_lanes(dot(weights[n % 2], v_ref[seq, :, lanes]))
        gated[group] = (mixed * both(lambda b: g_refs[b][seq, :, lanes])).astype(jnp.bfloat16)
        if len(gated) == groups:
            whole = jnp.concatenate([gated.pop(part) for part in range(groups)], axis=1)
            update = dot(whole, o_w[...]) + o_b[...]
            after = []
            for b, (_, half, _) in enumerate(blocks):
                x = x_refs[b][seq].astype(jnp.float32).reshape(owners, HALVES, HALF_ROWS, width)
                own = update[b * part_rows : (b + 1) * part_rows].reshape(owners, HALF_ROWS, width)
                after.append(x[:, half] + own)
            done.append(after)
            if len(done) == 2:
                low = (seq - 1) * HALF_ROWS
                for b in range(count):
                    rows = jnp.concatenate([value[b] for value in done], axis=1)
                    ready[step, b, :, low : low + 2 * HALF_ROWS] = rows.astype(jnp.bfloat16)
                done.clear()

    pipelined(seqs * groups, score, soften, average)

    def copies(step):
        for b, (plane, half, _) in enumerate(blocks):
            first = pl.multiple_of(lax.rem(here_ref[0] + plane, NZ) * owners, owners)
            rows = pl.ds(pl.multiple_of(step * seqs * HALF_ROWS, seqs * HALF_ROWS), seqs * HALF_ROWS)
            yield pltpu.make_async_copy(
                ready.at[step, b], outs[half].at[pl.ds(first, owners), rows], sems.at[step, b]
            )

    for copy in copies(step):
        copy.start()

    @pl.when(step == last)
    def _():
        for n in range(ready.shape[0]):
            for copy in copies(n):
                copy.wait()


def row_attention(blocks, here, q, k, v, g, x, biases, o_w, o_b, held):
    seqs, res, width = x.shape
    own = res // DAP
    part_rows = DAP // NZ * HALF_ROWS
    once = 4
    halves = sorted({half for _, half, _ in blocks})

    def which(here, plane):
        return lax.rem(here[0] + plane, NZ)

    queries = [
        pl.BlockSpec(
            (once, part_rows, width),
            lambda s, here, plane=plane, half=half: (s, half * NZ + which(here, plane), 0),
        )
        for plane, half, _ in blocks
    ]
    residual = [
        pl.BlockSpec((once, res // NZ, width), lambda s, here, plane=plane: (s, which(here, plane), 0))
        for plane, _, _ in blocks
    ]
    args = [q, q, g, g, x, x, k, v, *biases, o_w, o_b.reshape(1, -1), *held]
    return pl.pallas_call(
        functools.partial(row_kernel, blocks),
        out_shape=[jax.ShapeDtypeStruct((DAP, seqs * HALF_ROWS, width), jnp.bfloat16)] * len(halves),
        grid_spec=pltpu.PrefetchScalarGridSpec(
            num_scalar_prefetch=1,
            grid=(seqs // once,),
            in_specs=queries
            + queries
            + residual
            + [
                pl.BlockSpec((once, width, res), lambda s, here: (s, 0, 0)),
                pl.BlockSpec((once, res, width), lambda s, here: (s, 0, 0)),
            ]
            + [pl.BlockSpec(bias.shape, lambda s, here: (0, 0, 0, 0)) for bias in biases]
            + [
                pl.BlockSpec((width, width), lambda s, here: (0, 0)),
                pl.BlockSpec((1, width), lambda s, here: (0, 0)),
            ]
            + [pl.BlockSpec(memory_space=pl.ANY)] * len(held),
            out_specs=[pl.BlockSpec(memory_space=pl.ANY)] * len(halves),
            scratch_shapes=[
                pltpu.VMEM((2, GROUP * part_rows * len(blocks), res), jnp.float32),
                pltpu.VMEM((2, GROUP * part_rows * len(blocks), res), jnp.bfloat16),
                pltpu.VMEM(
                    (seqs // once, len(blocks), DAP // NZ, once * HALF_ROWS, width), jnp.bfloat16
                ),
                pltpu.SemaphoreType.DMA((seqs // once, len(blocks))),
            ],
        ),
        input_output_aliases={len(args) + 1 - len(held) + n: n for n in range(len(held))},
        compiler_params=pltpu.CompilerParams(vmem_limit_bytes=56 * MIB),
        cost_estimate=pl.CostEstimate(
            flops=seqs * H * part_rows * len(blocks) * res * 256 * 16,
            bytes_accessed=8 * 1024 * 1024,
            transcendentals=seqs * H * part_rows * len(blocks) * res,
        ),
        name="row_attention",
    )(here, *args)


def column_kernel(at_once, x_ref, gain, bias, q_w, k_w, v_w, g_w, g_b, o_w, o_b, *refs):
    out_ref, held, scores, weights = refs[-4:]
    step = pl.program_id(0)
    owners, per, width = x_ref.shape
    items = pl.num_programs(0) * at_once
    seqs = owners * per // items
    parts = width // LANES

    @pl.when(step == 0)
    def _():
        for part in range(parts):
            held[part] = x_ref[:, :, lanes_of(part)].astype(jnp.float32).reshape(-1, LANES)

    mine = [pl.ds(step * at_once + n, seqs, stride=items) for n in range(at_once)]
    x = jnp.concatenate(
        [jnp.concatenate([held[part, rows, :] for rows in mine], axis=0) for part in range(parts)], axis=1
    )
    normed = norm(x, gain[...], bias[...]).astype(jnp.bfloat16)
    q, k_t, v, g = project(normed, normed, q_w, k_w, v_w, g_w, g_b)
    gated = {}

    def place(n):
        return slice(n // parts * seqs, (n // parts + 1) * seqs), lanes_of(n % parts)

    def score(n):
        rows, lanes = place(n)
        scores[n % 2] = dot(stacked(q[rows, lanes]), k_t[lanes, rows])

    def soften(n, _):
        for low in range(0, GROUP * seqs, 64):
            weights[n % 2, low : low + 64] = softmax_rounded(scores[n % 2, low : low + 64])

    def average(n, _):
        rows, lanes = place(n)
        mixed = own_lanes(dot(weights[n % 2], v[rows, lanes]))
        gated[n] = (mixed * g[rows, lanes]).astype(jnp.bfloat16)

    pipelined(at_once * parts, score, soften, average)
    gated = [
        jnp.concatenate([gated[n * parts + part] for part in range(parts)], axis=1)
        for n in range(at_once)
    ]
    after = x + (dot(jnp.concatenate(gated, axis=0), o_w[...]) + o_b[...])
    for n, rows in enumerate(mine):
        for part in range(parts):
            held[part, rows, :] = after[n * seqs : (n + 1) * seqs, lanes_of(part)]

    @pl.when(step == pl.num_programs(0) - 1)
    def _():
        for part in range(parts):
            out_ref[:, :, lanes_of(part)] = (
                held[part].reshape(owners, per, LANES).astype(jnp.bfloat16)
            )


def column_attention(items, half, before, x, gain, bias, q_w, k_w, v_w, g_w, g_b, o_w, o_b):
    width = x.shape[2]
    seqs = x.size // (items * width)
    at_once = 4
    whole = pl.BlockSpec(x.shape, lambda r: (0, 0, 0))
    vector = pl.BlockSpec((1, width), lambda r: (0, 0))
    weight = pl.BlockSpec((width, width), lambda r: (0, 0))
    return pl.pallas_call(
        functools.partial(column_kernel, at_once),
        grid=(items // at_once,),
        out_shape=[jax.ShapeDtypeStruct((DAP, HALVES * x.shape[1], width), jnp.bfloat16)],
        in_specs=[whole, vector, vector]
        + [weight] * 4
        + [vector, weight, vector]
        + [pl.BlockSpec(memory_space=pl.ANY)] * len(before),
        out_specs=[pl.BlockSpec(x.shape, lambda r: (0, half, 0))],
        input_output_aliases={10: 0} if before else {},
        scratch_shapes=[
            pltpu.VMEM((width // LANES, seqs * items, LANES), jnp.float32),
            pltpu.VMEM((2, GROUP * seqs, seqs), jnp.float32),
            pltpu.VMEM((2, GROUP * seqs, seqs), jnp.bfloat16),
        ],
        compiler_params=pltpu.CompilerParams(vmem_limit_bytes=56 * MIB),
        name="column_attention",
    )(
        x, gain.reshape(1, -1), bias.reshape(1, -1), q_w, k_w, v_w, g_w, g_b.reshape(1, -1),
        o_w, o_b.reshape(1, -1), *before,
    )


def fetch(value, z):
    pairs = [((n + z * PLANE) % DAP, n) for n in range(DAP)]
    return lax.ppermute(value, "dap", pairs)


def gather_plane(copies):
    groups = [[z * PLANE + n for n in range(PLANE)] for z in range(NZ)]
    return lax.all_to_all(
        copies, "dap", split_axis=0, concat_axis=0, axis_index_groups=groups, tiled=True
    )


def exchange(value):
    return lax.all_to_all(value, "dap", split_axis=0, concat_axis=0, tiled=True)


def per_device(
    alignment,
    pair_state,
    row_norm_gain,
    row_norm_bias,
    pair_norm_gain,
    pair_weight,
    row_query,
    row_key,
    row_value,
    row_gate,
    row_gate_bias,
    row_output,
    row_output_bias,
    column_norm_gain,
    column_norm_bias,
    column_query,
    column_key,
    column_value,
    column_gate,
    column_gate_bias,
    column_output,
    column_output_bias,
):
    seqs, res, width = alignment.shape
    own = res // DAP
    me = lax.axis_index("dap")
    here = (me // PLANE).astype(jnp.int32).reshape(1)
    local, copies = pair_bias(pair_state, pair_norm_gain, pair_weight)
    far_rows = fetch(local, 2)
    own_plane = gather_plane(copies)
    projected = row_project(
        alignment, row_norm_gain, row_norm_bias, row_query, row_key, row_value, row_gate, row_gate_bias
    )
    own_plane, far_rows, projected = lax.optimization_barrier((own_plane, far_rows, projected))
    ahead, behind = fetch(own_plane, 1), fetch(own_plane, 3)
    far_plane = gather_plane(jnp.broadcast_to(far_rows, (PLANE,) + far_rows.shape))

    def attend(blocks, biases, *held):
        return row_attention(
            blocks, here, *projected, alignment, biases, row_output, row_output_bias, held
        )

    after = attend(((0, 0, 0), (0, 1, 0)), [own_plane])
    after = attend(((2, 0, 0), (2, 1, 0)), [far_plane], *after)
    first = attend(((1, 0, 0), (3, 0, 1)), [ahead, behind], after[0])[0]
    second = attend(((1, 1, 0), (3, 1, 1)), [ahead, behind], after[1])[0]
    first, second = lax.optimization_barrier((exchange(first), second))
    items = own // HALVES
    columns = ()
    for half, part in enumerate((first, exchange(second))):
        columns = column_attention(
            items,
            half,
            columns,
            part,
            column_norm_gain,
            column_norm_bias,
            column_query,
            column_key,
            column_value,
            column_gate,
            column_gate_bias,
            column_output,
            column_output_bias,
        )
    back = exchange(columns[0]).reshape(DAP, HALVES, seqs, items, width)
    return back.transpose(2, 0, 1, 3, 4).reshape(alignment.shape)


def solution(mesh):
    split = P(("batch", "dap"), None, None)
    return jax.shard_map(
        per_device,
        mesh=mesh,
        in_specs=(split, split) + (P(),) * 20,
        out_specs=split,
        check_vma=False,
    )
```

```python
import functools

import jax
import jax.numpy as jnp
from jax import lax
from jax.experimental import pallas as pl
from jax.experimental.pallas import tpu as pltpu
from jax.sharding import PartitionSpec as P

H = 8
HEAD = 32
C = 256
LANES = 128
GROUP = LANES // HEAD
EPS = 1e-05
MIB = 1024 * 1024
HALVES = 2
HALF_ROWS = 8
NZ, NX, NY = 4, 4, 2
DAP = NZ * NX * NY
NT = (((1,), (1,)), ((), ()))


def norm(x, gain, bias, center=None):
    if center is None:
        center = jnp.mean(x, axis=-1, keepdims=True)
    moved = x - center
    spread = jnp.mean(moved * moved, axis=-1, keepdims=True)
    return moved * lax.rsqrt(spread + EPS) * gain + bias


def lanes_of(part):
    return slice(part * LANES, (part + 1) * LANES)


def dot(a, b):
    return jnp.dot(a, b, preferred_element_type=jnp.float32)


def softmax_rounded(scores):
    top = jnp.max(scores, axis=-1, keepdims=True)
    e = jnp.exp(scores - top)
    total = jnp.sum(e, axis=-1, keepdims=True)
    return (e * (1.0 / total)).astype(jnp.bfloat16)


def head_of_lane():
    return lax.broadcasted_iota(jnp.int32, (1, LANES), 1) // HEAD


def stacked(q):
    head = head_of_lane()
    masks = [(head == i).astype(jnp.float32).astype(jnp.bfloat16) for i in range(GROUP)]
    return jnp.concatenate([q * mask for mask in masks], axis=0)


def own_lanes(mixed):
    head = head_of_lane()
    rows = mixed.shape[0] // GROUP
    total = mixed[:rows]
    for i in range(1, GROUP):
        total = jnp.where(head == i, mixed[i * rows : (i + 1) * rows], total)
    return total


def pipelined(count, score, soften, average):
    scores, weights = {0: score(0)}, {}
    for n in range(count + 1):
        if n + 1 < count:
            scores[n + 1] = score(n + 1)
        if n < count:
            weights[n] = soften(n, scores.pop(n))
        if n >= 1:
            average(n - 1, weights.pop(n - 1))


def project(normed, at_queries, q_w, k_w, v_w, g_w, g_b):
    q = (dot(at_queries, q_w[...]) * HEAD ** (-0.5)).astype(jnp.bfloat16)
    k_t = dot(normed, k_w[...]).T.astype(jnp.bfloat16)
    v = dot(normed, v_w[...]).astype(jnp.bfloat16)
    g = jax.nn.sigmoid(dot(at_queries, g_w[...]) + g_b[...])
    return q, k_t, v, g


def pair_kernel(x_ref, gain_ref, w_ref, out_ref, held):
    step = pl.program_id(0)
    rows, _, cz = x_ref.shape
    mean = jnp.full((cz, cz), 1.0 / cz, jnp.bfloat16)
    for i in range(rows):
        x = x_ref[i]
        normed = norm(x.astype(jnp.float32), gain_ref[...], 0.0, dot(x, mean)).astype(jnp.bfloat16)
        bias = lax.dot_general(w_ref[...], normed, NT, preferred_element_type=jnp.float32)
        for part in range(held.shape[0]):
            low = step * rows // HALF_ROWS * (H * HALF_ROWS) + lax.rem(step * rows, HALF_ROWS) + i
            held[part, pl.ds(low, H, stride=HALF_ROWS), :] = bias[:, lanes_of(part)]

    @pl.when(step == pl.num_programs(0) - 1)
    def _():
        for part in range(held.shape[0]):
            out_ref[:, :, lanes_of(part)] = (
                held[part].astype(jnp.bfloat16).reshape(out_ref.shape[:2] + (LANES,))
            )


def pair_bias(pair_state, gain, weight):
    count, res, cz = pair_state.shape
    rows = 4
    return pl.pallas_call(
        pair_kernel,
        grid=(count // rows,),
        out_shape=jax.ShapeDtypeStruct((H, count, res), jnp.bfloat16),
        in_specs=[
            pl.BlockSpec((rows, res, cz), lambda i: (i, 0, 0)),
            pl.BlockSpec((1, cz), lambda i: (0, 0)),
            pl.BlockSpec((H, cz), lambda i: (0, 0)),
        ],
        out_specs=pl.BlockSpec((H, count, res), lambda i: (0, 0, 0)),
        scratch_shapes=[pltpu.VMEM((res // LANES, H * count, LANES), jnp.float32)],
        compiler_params=pltpu.CompilerParams(vmem_limit_bytes=56 * MIB),
        name="pair_bias",
    )(pair_state, gain.reshape(1, cz), weight.T)


def project_kernel(x_ref, gain, bias, q_w, k_w, v_w, g_w, g_b, *refs):
    later, (q_ref, k_ref, v_ref, g_ref, stack_ref) = refs[:-5], refs[-5:]

    @pl.when(pl.program_id(0) == 0)
    def _():
        for n, w_ref in enumerate(later):
            stack_ref[n] = w_ref[...]

    count, res, width = x_ref.shape
    x = x_ref[...].reshape(count * res, width).astype(jnp.float32)
    normed = norm(x, gain[...], bias[...])
    split = normed.reshape(count, DAP, HALVES, HALF_ROWS, width)
    halves = [split[:, :, half].reshape(count, res // HALVES, width) for half in range(HALVES)]
    at_queries = jnp.concatenate(halves, axis=1).reshape(count * res, width)
    q, k_t, v, g = project(
        normed.astype(jnp.bfloat16), at_queries.astype(jnp.bfloat16), q_w, k_w, v_w, g_w, g_b
    )
    for out_ref, value in ((q_ref, q), (v_ref, v), (g_ref, g)):
        out_ref[...] = value.reshape(count, res, width)
    for n in range(count):
        k_ref[n] = k_t[:, n * res : (n + 1) * res]


def row_project(x, gain, bias, q_w, k_w, v_w, g_w, g_b, later):
    seqs, res, width = x.shape
    count = 2
    block = pl.BlockSpec((count, res, width), lambda s: (s, 0, 0))
    turned = pl.BlockSpec((count, width, res), lambda s: (s, 0, 0))
    vector = pl.BlockSpec((1, width), lambda s: (0, 0))
    weight = pl.BlockSpec((width, width), lambda s: (0, 0))
    shape = jax.ShapeDtypeStruct
    return pl.pallas_call(
        project_kernel,
        grid=(seqs // count,),
        out_shape=[
            shape((seqs, res, width), jnp.bfloat16),
            shape((seqs, width, res), jnp.bfloat16),
            shape((seqs, res, width), jnp.bfloat16),
            shape((seqs, res, width), jnp.float32),
            shape((len(later), width, width), jnp.bfloat16),
        ],
        in_specs=[block, vector, vector] + [weight] * 4 + [vector] + [weight] * len(later),
        out_specs=[
            block, turned, block, block, pl.BlockSpec((len(later), width, width), lambda s: (0, 0, 0))
        ],
        compiler_params=pltpu.CompilerParams(vmem_limit_bytes=56 * MIB),
        cost_estimate=pl.CostEstimate(
            flops=2 * seqs * res * width * width * 4,
            bytes_accessed=x.size * 12,
            transcendentals=x.size * 2,
        ),
        name="row_project",
    )(x, gain.reshape(1, -1), bias.reshape(1, -1), q_w, k_w, v_w, g_w, g_b.reshape(1, -1), *later)


def row_kernel(blocks, here_ref, *refs):
    count = len(blocks)
    planes = 1 + max(which for _, _, which in blocks)
    q_refs, g_refs, x_refs, (k_ref, v_ref) = refs[:2], refs[2:4], refs[4:6], refs[6:8]
    bias_refs, (o_w, o_b) = refs[8 : 8 + planes], refs[8 + planes : 10 + planes]
    held, weights, ready, sems = refs[-4:]
    halves = sorted({half for _, half, _ in blocks})
    outs = dict(zip(halves, refs[-4 - len(halves) : -4]))
    step, last = pl.program_id(0), pl.num_programs(0) - 1
    seqs, part_rows, width = q_refs[0].shape
    tile = count * part_rows
    owners = part_rows // HALF_ROWS
    groups = H // GROUP

    def place(n):
        return n // groups, n % groups, lanes_of(n % groups)

    def both(pick):
        return jnp.concatenate([pick(n) for n in range(count)], axis=0)

    def score(n):
        seq, _, lanes = place(n)
        q = both(lambda b: q_refs[b][seq, :, lanes])
        held[n % 2] = dot(stacked(q), k_ref[seq, lanes, :])

    taken = 4

    def soften(n, _):
        _, group, _ = place(n)
        for b, (_, half, which) in enumerate(blocks):
            for two in range(0, GROUP, 2):
                for first in range(0, owners, taken):
                    piece = (half * H + group * GROUP + two) // 2
                    bias = [
                        bias_refs[which][o, piece].astype(jnp.float32)
                        for o in range(first, first + taken)
                    ]
                    for i in range(2):
                        low = (two + i) * tile + b * part_rows + first * HALF_ROWS
                        rows = slice(low, low + taken * HALF_ROWS)
                        mine = [value[i * HALF_ROWS : (i + 1) * HALF_ROWS] for value in bias]
                        weights[n % 2, rows] = softmax_rounded(
                            held[n % 2, rows] + jnp.concatenate(mine, axis=0)
                        )

    gated, done = {}, []

    def average(n, _):
        seq, group, lanes = place(n)
        mixed = own_lanes(dot(weights[n % 2], v_ref[seq, :, lanes]))
        gated[group] = (mixed * both(lambda b: g_refs[b][seq, :, lanes])).astype(jnp.bfloat16)
        if len(gated) == groups:
            whole = jnp.concatenate([gated.pop(part) for part in range(groups)], axis=1)
            update = dot(whole, o_w[...]) + o_b[...]
            after = []
            for b, (_, half, _) in enumerate(blocks):
                x = x_refs[b][seq].astype(jnp.float32).reshape(owners, HALVES, HALF_ROWS, width)
                own = update[b * part_rows : (b + 1) * part_rows].reshape(owners, HALF_ROWS, width)
                after.append(x[:, half] + own)
            done.append(after)
            if len(done) == 2:
                low = (seq - 1) * HALF_ROWS
                for b in range(count):
                    rows = jnp.concatenate([value[b] for value in done], axis=1)
                    ready[step, b, :, low : low + 2 * HALF_ROWS] = rows.astype(jnp.bfloat16)
                done.clear()

    pipelined(seqs * groups, score, soften, average)

    def copies(step):
        for b, (plane, half, _) in enumerate(blocks):
            first = pl.multiple_of(lax.rem(here_ref[0] + plane, NZ) * owners, owners)
            rows = pl.ds(pl.multiple_of(step * seqs * HALF_ROWS, seqs * HALF_ROWS), seqs * HALF_ROWS)
            yield pltpu.make_async_copy(
                ready.at[step, b], outs[half].at[pl.ds(first, owners), rows], sems.at[step, b]
            )

    for copy in copies(step):
        copy.start()

    @pl.when(step == last)
    def _():
        for n in range(ready.shape[0]):
            for copy in copies(n):
                copy.wait()


def row_attention(blocks, here, q, k, v, g, x, biases, o_w, o_b, held):
    seqs, res, width = x.shape
    own = res // DAP
    part_rows = DAP // NZ * HALF_ROWS
    once = 4
    halves = sorted({half for _, half, _ in blocks})

    def which(here, plane):
        return lax.rem(here[0] + plane, NZ)

    queries = [
        pl.BlockSpec(
            (once, part_rows, width),
            lambda s, here, plane=plane, half=half: (s, half * NZ + which(here, plane), 0),
        )
        for plane, half, _ in blocks
    ]
    residual = [
        pl.BlockSpec((once, res // NZ, width), lambda s, here, plane=plane: (s, which(here, plane), 0))
        for plane, _, _ in blocks
    ]
    args = [q, q, g, g, x, x, k, v, *biases, o_w, o_b.reshape(1, -1), *held]
    return pl.pallas_call(
        functools.partial(row_kernel, blocks),
        out_shape=[jax.ShapeDtypeStruct((DAP, seqs * HALF_ROWS, width), jnp.bfloat16)] * len(halves),
        grid_spec=pltpu.PrefetchScalarGridSpec(
            num_scalar_prefetch=1,
            grid=(seqs // once,),
            in_specs=queries
            + queries
            + residual
            + [
                pl.BlockSpec((once, width, res), lambda s, here: (s, 0, 0)),
                pl.BlockSpec((once, res, width), lambda s, here: (s, 0, 0)),
            ]
            + [pl.BlockSpec(bias.shape, lambda s, here: (0, 0, 0, 0)) for bias in biases]
            + [
                pl.BlockSpec((width, width), lambda s, here: (0, 0)),
                pl.BlockSpec((1, width), lambda s, here: (0, 0)),
            ]
            + [pl.BlockSpec(memory_space=pl.ANY)] * len(held),
            out_specs=[pl.BlockSpec(memory_space=pl.ANY)] * len(halves),
            scratch_shapes=[
                pltpu.VMEM((2, GROUP * part_rows * len(blocks), res), jnp.float32),
                pltpu.VMEM((2, GROUP * part_rows * len(blocks), res), jnp.bfloat16),
                pltpu.VMEM(
                    (seqs // once, len(blocks), DAP // NZ, once * HALF_ROWS, width), jnp.bfloat16
                ),
                pltpu.SemaphoreType.DMA((seqs // once, len(blocks))),
            ],
        ),
        input_output_aliases={len(args) + 1 - len(held) + n: n for n in range(len(held))},
        compiler_params=pltpu.CompilerParams(vmem_limit_bytes=56 * MIB),
        cost_estimate=pl.CostEstimate(
            flops=seqs * H * part_rows * len(blocks) * res * 256 * 16,
            bytes_accessed=8 * 1024 * 1024,
            transcendentals=seqs * H * part_rows * len(blocks) * res,
        ),
        name="row_attention",
    )(here, *args)


def column_kernel(at_once, x_ref, gain, bias, w_ref, g_b, o_b, *refs):
    q_w, k_w, v_w, g_w, o_w = (w_ref.at[n] for n in range(5))
    out_ref, held, scores, weights = refs[-4:]
    step = pl.program_id(0)
    owners, per, width = x_ref.shape
    items = pl.num_programs(0) * at_once
    seqs = owners * per // items
    parts = width // LANES

    @pl.when(step == 0)
    def _():
        for part in range(parts):
            held[part] = x_ref[:, :, lanes_of(part)].astype(jnp.float32).reshape(-1, LANES)

    mine = [pl.ds(step * at_once + n, seqs, stride=items) for n in range(at_once)]
    x = jnp.concatenate(
        [jnp.concatenate([held[part, rows, :] for rows in mine], axis=0) for part in range(parts)], axis=1
    )
    normed = norm(x, gain[...], bias[...]).astype(jnp.bfloat16)
    q, k_t, v, g = project(normed, normed, q_w, k_w, v_w, g_w, g_b)
    gated = {}

    def place(n):
        return slice(n // parts * seqs, (n // parts + 1) * seqs), lanes_of(n % parts)

    def score(n):
        rows, lanes = place(n)
        scores[n % 2] = dot(stacked(q[rows, lanes]), k_t[lanes, rows])

    def soften(n, _):
        for low in range(0, GROUP * seqs, 64):
            weights[n % 2, low : low + 64] = softmax_rounded(scores[n % 2, low : low + 64])

    def average(n, _):
        rows, lanes = place(n)
        mixed = own_lanes(dot(weights[n % 2], v[rows, lanes]))
        gated[n] = (mixed * g[rows, lanes]).astype(jnp.bfloat16)

    pipelined(at_once * parts, score, soften, average)
    gated = [
        jnp.concatenate([gated[n * parts + part] for part in range(parts)], axis=1)
        for n in range(at_once)
    ]
    after = x + (dot(jnp.concatenate(gated, axis=0), o_w[...]) + o_b[...])
    for n, rows in enumerate(mine):
        for part in range(parts):
            held[part, rows, :] = after[n * seqs : (n + 1) * seqs, lanes_of(part)]

    @pl.when(step == pl.num_programs(0) - 1)
    def _():
        for part in range(parts):
            out_ref[:, :, lanes_of(part)] = (
                held[part].reshape(owners, per, LANES).astype(jnp.bfloat16)
            )


def column_attention(items, half, before, x, gain, bias, weights, g_b, o_b):
    width = x.shape[2]
    seqs = x.size // (items * width)
    at_once = 4
    whole = pl.BlockSpec(x.shape, lambda r: (0, 0, 0))
    vector = pl.BlockSpec((1, width), lambda r: (0, 0))
    weight = pl.BlockSpec((5, width, width), lambda r: (0, 0, 0))
    return pl.pallas_call(
        functools.partial(column_kernel, at_once),
        grid=(items // at_once,),
        out_shape=[jax.ShapeDtypeStruct((DAP, HALVES * x.shape[1], width), jnp.bfloat16)],
        in_specs=[whole, vector, vector, weight, vector, vector]
        + [pl.BlockSpec(memory_space=pl.ANY)] * len(before),
        out_specs=[pl.BlockSpec(x.shape, lambda r: (0, half, 0))],
        input_output_aliases={6: 0} if before else {},
        scratch_shapes=[
            pltpu.VMEM((width // LANES, seqs * items, LANES), jnp.float32),
            pltpu.VMEM((2, GROUP * seqs, seqs), jnp.float32),
            pltpu.VMEM((2, GROUP * seqs, seqs), jnp.bfloat16),
        ],
        compiler_params=pltpu.CompilerParams(vmem_limit_bytes=44 * MIB),
        name="column_attention",
    )(
        x, gain.reshape(1, -1), bias.reshape(1, -1), weights, g_b.reshape(1, -1), o_b.reshape(1, -1), *before
    )


def fetch(value, z=0, x=0, y=0):
    pairs = []
    for dz in range(NZ):
        for dx in range(NX):
            for dy in range(NY):
                src = ((dz + z) % NZ * NX + (dx + x) % NX) * NY + (dy + y) % NY
                pairs.append((src, (dz * NX + dx) * NY + dy))
    return lax.ppermute(value, "dap", pairs)


def join_kernel(axis, here_ref, *refs):
    parts, (out_ref, sems) = refs[:-2], refs[-2:]
    size = parts[0].shape[0]
    copies = []
    for n, part in enumerate(parts):
        place = lax.rem(here_ref[axis] + n, len(parts)) * size
        copies.append(pltpu.make_async_copy(part, out_ref.at[pl.ds(place, size)], sems.at[n]))
    for copy in copies:
        copy.start()
    for copy in copies:
        copy.wait()


def join(here, axis, *parts):
    anywhere = pl.BlockSpec(memory_space=pl.ANY)
    shape = (len(parts) * parts[0].shape[0],) + parts[0].shape[1:]
    return pl.pallas_call(
        functools.partial(join_kernel, axis),
        out_shape=jax.ShapeDtypeStruct(shape, parts[0].dtype),
        in_specs=[pl.BlockSpec(memory_space=pltpu.SMEM)] + [anywhere] * len(parts),
        out_specs=anywhere,
        scratch_shapes=[pltpu.SemaphoreType.DMA((len(parts),))],
        compiler_params=pltpu.CompilerParams(vmem_limit_bytes=4 * MIB),
        name="join",
    )(here, *parts)


def exchange(value):
    return lax.all_to_all(value, "dap", split_axis=0, concat_axis=0, tiled=True)


def per_device(
    alignment,
    pair_state,
    row_norm_gain,
    row_norm_bias,
    pair_norm_gain,
    pair_weight,
    row_query,
    row_key,
    row_value,
    row_gate,
    row_gate_bias,
    row_output,
    row_output_bias,
    column_norm_gain,
    column_norm_bias,
    column_query,
    column_key,
    column_value,
    column_gate,
    column_gate_bias,
    column_output,
    column_output_bias,
):
    seqs, res, width = alignment.shape
    own = res // DAP
    me = lax.axis_index("dap")
    here = jnp.stack([me // (NX * NY), me // NY % NX, me % NY]).astype(jnp.int32)
    local = pair_bias(pair_state, pair_norm_gain, pair_weight)[None]
    pair = join(here, 2, local, fetch(local, y=1))
    near = [fetch(pair, x=step) for step in (1, 2, 3)]
    far_pair = fetch(pair, z=2)
    pair, inputs = lax.optimization_barrier((pair, alignment))
    projected = row_project(
        inputs, row_norm_gain, row_norm_bias, row_query, row_key, row_value, row_gate, row_gate_bias,
        (column_query, column_key, column_value, column_gate, column_output),
    )
    near, (*projected, weights) = lax.optimization_barrier((near, projected))
    own_plane = join(here, 1, pair, *near)
    far_pair, own_plane = lax.optimization_barrier((far_pair, own_plane))
    ahead, behind = fetch(own_plane, z=1), fetch(own_plane, z=3)
    far_plane = join(here, 1, far_pair, *(fetch(far_pair, x=step) for step in (1, 2, 3)))

    def attend(blocks, biases, *held):
        return row_attention(
            blocks, here, *projected, alignment, biases, row_output, row_output_bias, held
        )

    after = attend(((0, 0, 0), (0, 1, 0)), [own_plane])
    after = attend(((2, 0, 0), (2, 1, 0)), [far_plane], *after)
    first = attend(((1, 0, 0), (3, 0, 1)), [ahead, behind], after[0])[0]
    second = attend(((1, 1, 0), (3, 1, 1)), [ahead, behind], after[1])[0]
    first, second = lax.optimization_barrier((exchange(first), second))
    items = own // HALVES
    columns = ()
    for half, part in enumerate((first, exchange(second))):
        columns = column_attention(
            items,
            half,
            columns,
            part,
            column_norm_gain,
            column_norm_bias,
            weights,
            column_gate_bias,
            column_output_bias,
        )
    back = exchange(columns[0]).reshape(DAP, HALVES, seqs, items, width)
    return back.transpose(2, 0, 1, 3, 4).reshape(alignment.shape)


def solution(mesh):
    split = P(("batch", "dap"), None, None)
    return jax.shard_map(
        per_device,
        mesh=mesh,
        in_specs=(split, split) + (P(),) * 20,
        out_specs=split,
        check_vma=False,
    )
```

```python
import functools

import jax
import jax.numpy as jnp
from jax import lax
from jax.experimental import pallas as pl
from jax.experimental.pallas import tpu as pltpu
from jax.sharding import PartitionSpec as P

H = 8
HEAD = 32
C = 256
LANES = 128
GROUP = LANES // HEAD
EPS = 1e-05
MIB = 1024 * 1024
HALVES = 2
HALF_ROWS = 8
NZ, NX, NY = 4, 4, 2
DAP = NZ * NX * NY
NT = (((1,), (1,)), ((), ()))


def norm(x, gain, bias, center=None):
    if center is None:
        center = jnp.mean(x, axis=-1, keepdims=True)
    moved = x - center
    spread = jnp.mean(moved * moved, axis=-1, keepdims=True)
    return moved * lax.rsqrt(spread + EPS) * gain + bias


def lanes_of(part):
    return slice(part * LANES, (part + 1) * LANES)


def dot(a, b):
    return jnp.dot(a, b, preferred_element_type=jnp.float32)


def softmax_rounded(scores):
    top = jnp.max(scores, axis=-1, keepdims=True)
    e = jnp.exp(scores - top)
    total = jnp.sum(e, axis=-1, keepdims=True)
    return (e * (1.0 / total)).astype(jnp.bfloat16)


def head_of_lane():
    return lax.broadcasted_iota(jnp.int32, (1, LANES), 1) // HEAD


def stacked(q):
    head = head_of_lane()
    masks = [(head == i).astype(jnp.float32).astype(jnp.bfloat16) for i in range(GROUP)]
    return jnp.concatenate([q * mask for mask in masks], axis=0)


def own_lanes(mixed):
    head = head_of_lane()
    rows = mixed.shape[0] // GROUP
    total = mixed[:rows]
    for i in range(1, GROUP):
        total = jnp.where(head == i, mixed[i * rows : (i + 1) * rows], total)
    return total


def pipelined(count, score, soften, average):
    scores, weights = {0: score(0)}, {}
    for n in range(count + 1):
        if n + 1 < count:
            scores[n + 1] = score(n + 1)
        if n < count:
            weights[n] = soften(n, scores.pop(n))
        if n >= 1:
            average(n - 1, weights.pop(n - 1))


def project(normed, at_queries, q_w, k_w, v_w, g_w, g_b):
    q = (dot(at_queries, q_w[...]) * HEAD ** (-0.5)).astype(jnp.bfloat16)
    k_t = dot(normed, k_w[...]).T.astype(jnp.bfloat16)
    v = dot(normed, v_w[...]).astype(jnp.bfloat16)
    g = jax.nn.sigmoid(dot(at_queries, g_w[...]) + g_b[...])
    return q, k_t, v, g


def pair_kernel(x_ref, gain_ref, w_ref, out_ref, held):
    step = pl.program_id(0)
    rows, _, cz = x_ref.shape
    mean = jnp.full((cz, cz), 1.0 / cz, jnp.bfloat16)
    for i in range(rows):
        x = x_ref[i]
        normed = norm(x.astype(jnp.float32), gain_ref[...], 0.0, dot(x, mean)).astype(jnp.bfloat16)
        bias = lax.dot_general(w_ref[...], normed, NT, preferred_element_type=jnp.float32)
        for part in range(held.shape[0]):
            low = step * rows // HALF_ROWS * (H * HALF_ROWS) + lax.rem(step * rows, HALF_ROWS) + i
            held[part, pl.ds(low, H, stride=HALF_ROWS), :] = bias[:, lanes_of(part)]

    @pl.when(step == pl.num_programs(0) - 1)
    def _():
        for part in range(held.shape[0]):
            out_ref[:, :, lanes_of(part)] = (
                held[part].astype(jnp.bfloat16).reshape(out_ref.shape[:2] + (LANES,))
            )


def pair_bias(pair_state, gain, weight):
    count, res, cz = pair_state.shape
    rows = 4
    return pl.pallas_call(
        pair_kernel,
        grid=(count // rows,),
        out_shape=jax.ShapeDtypeStruct((H, count, res), jnp.bfloat16),
        in_specs=[
            pl.BlockSpec((rows, res, cz), lambda i: (i, 0, 0)),
            pl.BlockSpec((1, cz), lambda i: (0, 0)),
            pl.BlockSpec((H, cz), lambda i: (0, 0)),
        ],
        out_specs=pl.BlockSpec((H, count, res), lambda i: (0, 0, 0)),
        scratch_shapes=[pltpu.VMEM((res // LANES, H * count, LANES), jnp.float32)],
        compiler_params=pltpu.CompilerParams(vmem_limit_bytes=56 * MIB),
        name="pair_bias",
    )(pair_state, gain.reshape(1, cz), weight.T)


def project_kernel(x_ref, gain, bias, q_w, k_w, v_w, g_w, g_b, q_ref, k_ref, v_ref, g_ref):
    count, res, width = x_ref.shape
    x = x_ref[...].reshape(count * res, width).astype(jnp.float32)
    normed = norm(x, gain[...], bias[...])
    split = normed.reshape(count, DAP, HALVES, HALF_ROWS, width)
    halves = [split[:, :, half].reshape(count, res // HALVES, width) for half in range(HALVES)]
    at_queries = jnp.concatenate(halves, axis=1).reshape(count * res, width)
    q, k_t, v, g = project(
        normed.astype(jnp.bfloat16), at_queries.astype(jnp.bfloat16), q_w, k_w, v_w, g_w, g_b
    )
    for out_ref, value in ((q_ref, q), (v_ref, v), (g_ref, g)):
        out_ref[...] = value.reshape(count, res, width)
    for n in range(count):
        k_ref[n] = k_t[:, n * res : (n + 1) * res]


def row_project(x, gain, bias, q_w, k_w, v_w, g_w, g_b):
    seqs, res, width = x.shape
    count = 2
    block = pl.BlockSpec((count, res, width), lambda s: (s, 0, 0))
    turned = pl.BlockSpec((count, width, res), lambda s: (s, 0, 0))
    vector = pl.BlockSpec((1, width), lambda s: (0, 0))
    weight = pl.BlockSpec((width, width), lambda s: (0, 0))
    shape = jax.ShapeDtypeStruct
    return pl.pallas_call(
        project_kernel,
        grid=(seqs // count,),
        out_shape=[
            shape((seqs, res, width), jnp.bfloat16),
            shape((seqs, width, res), jnp.bfloat16),
            shape((seqs, res, width), jnp.bfloat16),
            shape((seqs, res, width), jnp.float32),
        ],
        in_specs=[block, vector, vector] + [weight] * 4 + [vector],
        out_specs=[block, turned, block, block],
        compiler_params=pltpu.CompilerParams(vmem_limit_bytes=24 * MIB),
        cost_estimate=pl.CostEstimate(
            flops=2 * seqs * res * width * width * 4,
            bytes_accessed=x.size * 12,
            transcendentals=x.size * 2,
        ),
        name="row_project",
    )(x, gain.reshape(1, -1), bias.reshape(1, -1), q_w, k_w, v_w, g_w, g_b.reshape(1, -1))


def stack_kernel(*refs):
    for n, ref in enumerate(refs[:-1]):
        refs[-1][n] = ref[...]


def stack(*weights):
    return pl.pallas_call(
        stack_kernel,
        out_shape=jax.ShapeDtypeStruct((len(weights),) + weights[0].shape, weights[0].dtype),
        compiler_params=pltpu.CompilerParams(vmem_limit_bytes=56 * MIB),
        name="stack",
    )(*weights)


def row_kernel(blocks, here_ref, *refs):
    count = len(blocks)
    planes = 1 + max(which for _, _, which in blocks)
    q_refs, g_refs, x_refs, (k_ref, v_ref) = refs[:2], refs[2:4], refs[4:6], refs[6:8]
    bias_refs, (o_w, o_b) = refs[8 : 8 + planes], refs[8 + planes : 10 + planes]
    held, weights, ready, sems = refs[-4:]
    halves = sorted({half for _, half, _ in blocks})
    outs = dict(zip(halves, refs[-4 - len(halves) : -4]))
    step, last = pl.program_id(0), pl.num_programs(0) - 1
    seqs, part_rows, width = q_refs[0].shape
    tile = count * part_rows
    owners = part_rows // HALF_ROWS
    groups = H // GROUP

    def place(n):
        return n // groups, n % groups, lanes_of(n % groups)

    def both(pick):
        return jnp.concatenate([pick(n) for n in range(count)], axis=0)

    def score(n):
        seq, _, lanes = place(n)
        q = both(lambda b: q_refs[b][seq, :, lanes])
        held[n % 2] = dot(stacked(q), k_ref[seq, lanes, :])

    def slot(x, y):
        return lax.rem(x - here_ref[1] + NX, NX) * NY + lax.rem(y - here_ref[2] + NY, NY)

    slots = [slot(x, y) for x in range(NX) for y in range(NY)]
    taken = 2

    def soften(n, _):
        _, group, _ = place(n)
        for b, (_, half, which) in enumerate(blocks):
            for two in range(0, GROUP, 2):
                for first in range(0, owners, taken):
                    piece = (half * H + group * GROUP + two) // 2
                    bias = [
                        bias_refs[which][slots[o], piece].astype(jnp.float32)
                        for o in range(first, first + taken)
                    ]
                    for i in range(2):
                        low = (two + i) * tile + b * part_rows + first * HALF_ROWS
                        rows = slice(low, low + taken * HALF_ROWS)
                        mine = [value[i * HALF_ROWS : (i + 1) * HALF_ROWS] for value in bias]
                        weights[n % 2, rows] = softmax_rounded(
                            held[n % 2, rows] + jnp.concatenate(mine, axis=0)
                        )

    gated, done = {}, []

    def average(n, _):
        seq, group, lanes = place(n)
        mixed = own_lanes(dot(weights[n % 2], v_ref[seq, :, lanes]))
        gated[group] = (mixed * both(lambda b: g_refs[b][seq, :, lanes])).astype(jnp.bfloat16)
        if len(gated) == groups:
            whole = jnp.concatenate([gated.pop(part) for part in range(groups)], axis=1)
            update = dot(whole, o_w[...]) + o_b[...]
            after = []
            for b, (_, half, _) in enumerate(blocks):
                x = x_refs[b][seq].astype(jnp.float32).reshape(owners, HALVES, HALF_ROWS, width)
                own = update[b * part_rows : (b + 1) * part_rows].reshape(owners, HALF_ROWS, width)
                after.append(x[:, half] + own)
            done.append(after)
            if len(done) == 2:
                low = (seq - 1) * HALF_ROWS
                for b in range(count):
                    rows = jnp.concatenate([value[b] for value in done], axis=1)
                    ready[step, b, :, low : low + 2 * HALF_ROWS] = rows.astype(jnp.bfloat16)
                done.clear()

    pipelined(seqs * groups, score, soften, average)

    def copies(step):
        for b, (plane, half, _) in enumerate(blocks):
            first = pl.multiple_of(lax.rem(here_ref[0] + plane, NZ) * owners, owners)
            rows = pl.ds(pl.multiple_of(step * seqs * HALF_ROWS, seqs * HALF_ROWS), seqs * HALF_ROWS)
            yield pltpu.make_async_copy(
                ready.at[step, b], outs[half].at[pl.ds(first, owners), rows], sems.at[step, b]
            )

    for copy in copies(step):
        copy.start()

    @pl.when(step == last)
    def _():
        for n in range(ready.shape[0]):
            for copy in copies(n):
                copy.wait()


def row_attention(grant, blocks, here, q, k, v, g, x, biases, o_w, o_b, held):
    seqs, res, width = x.shape
    own = res // DAP
    part_rows = DAP // NZ * HALF_ROWS
    once = 4
    halves = sorted({half for _, half, _ in blocks})

    def which(here, plane):
        return lax.rem(here[0] + plane, NZ)

    queries = [
        pl.BlockSpec(
            (once, part_rows, width),
            lambda s, here, plane=plane, half=half: (s, half * NZ + which(here, plane), 0),
        )
        for plane, half, _ in blocks
    ]
    residual = [
        pl.BlockSpec((once, res // NZ, width), lambda s, here, plane=plane: (s, which(here, plane), 0))
        for plane, _, _ in blocks
    ]
    args = [q, q, g, g, x, x, k, v, *biases, o_w, o_b.reshape(1, -1), *held]
    return pl.pallas_call(
        functools.partial(row_kernel, blocks),
        out_shape=[jax.ShapeDtypeStruct((DAP, seqs * HALF_ROWS, width), jnp.bfloat16)] * len(halves),
        grid_spec=pltpu.PrefetchScalarGridSpec(
            num_scalar_prefetch=1,
            grid=(seqs // once,),
            in_specs=queries
            + queries
            + residual
            + [
                pl.BlockSpec((once, width, res), lambda s, here: (s, 0, 0)),
                pl.BlockSpec((once, res, width), lambda s, here: (s, 0, 0)),
            ]
            + [pl.BlockSpec(bias.shape, lambda s, here: (0, 0, 0, 0)) for bias in biases]
            + [
                pl.BlockSpec((width, width), lambda s, here: (0, 0)),
                pl.BlockSpec((1, width), lambda s, here: (0, 0)),
            ]
            + [pl.BlockSpec(memory_space=pl.ANY)] * len(held),
            out_specs=[pl.BlockSpec(memory_space=pl.ANY)] * len(halves),
            scratch_shapes=[
                pltpu.VMEM((2, GROUP * part_rows * len(blocks), res), jnp.float32),
                pltpu.VMEM((2, GROUP * part_rows * len(blocks), res), jnp.bfloat16),
                pltpu.VMEM(
                    (seqs // once, len(blocks), DAP // NZ, once * HALF_ROWS, width), jnp.bfloat16
                ),
                pltpu.SemaphoreType.DMA((seqs // once, len(blocks))),
            ],
        ),
        input_output_aliases={len(args) + 1 - len(held) + n: n for n in range(len(held))},
        compiler_params=pltpu.CompilerParams(vmem_limit_bytes=grant * MIB),
        cost_estimate=pl.CostEstimate(
            flops=seqs * H * part_rows * len(blocks) * res * 256 * 16,
            bytes_accessed=8 * 1024 * 1024,
            transcendentals=seqs * H * part_rows * len(blocks) * res,
        ),
        name="row_attention",
    )(here, *args)


def column_kernel(at_once, x_ref, gain, bias, w_ref, g_b, o_b, *refs):
    q_w, k_w, v_w, g_w, o_w = (w_ref.at[n] for n in range(5))
    out_ref, held, scores, weights = refs[-4:]
    step = pl.program_id(0)
    owners, per, width = x_ref.shape
    items = pl.num_programs(0) * at_once
    seqs = owners * per // items
    parts = width // LANES

    @pl.when(step == 0)
    def _():
        for part in range(parts):
            held[part] = x_ref[:, :, lanes_of(part)].astype(jnp.float32).reshape(-1, LANES)

    mine = [pl.ds(step * at_once + n, seqs, stride=items) for n in range(at_once)]
    x = jnp.concatenate(
        [jnp.concatenate([held[part, rows, :] for rows in mine], axis=0) for part in range(parts)], axis=1
    )
    normed = norm(x, gain[...], bias[...]).astype(jnp.bfloat16)
    q, k_t, v, g = project(normed, normed, q_w, k_w, v_w, g_w, g_b)
    gated = {}

    def place(n):
        return slice(n // parts * seqs, (n // parts + 1) * seqs), lanes_of(n % parts)

    def score(n):
        rows, lanes = place(n)
        scores[n % 2] = dot(stacked(q[rows, lanes]), k_t[lanes, rows])

    def soften(n, _):
        for low in range(0, GROUP * seqs, 32):
            weights[n % 2, low : low + 32] = softmax_rounded(scores[n % 2, low : low + 32])

    def average(n, _):
        rows, lanes = place(n)
        mixed = own_lanes(dot(weights[n % 2], v[rows, lanes]))
        gated[n] = (mixed * g[rows, lanes]).astype(jnp.bfloat16)

    pipelined(at_once * parts, score, soften, average)
    gated = [
        jnp.concatenate([gated[n * parts + part] for part in range(parts)], axis=1)
        for n in range(at_once)
    ]
    after = x + (dot(jnp.concatenate(gated, axis=0), o_w[...]) + o_b[...])
    for n, rows in enumerate(mine):
        for part in range(parts):
            held[part, rows, :] = after[n * seqs : (n + 1) * seqs, lanes_of(part)]

    @pl.when(step == pl.num_programs(0) - 1)
    def _():
        for part in range(parts):
            out_ref[:, :, lanes_of(part)] = (
                held[part].reshape(owners, per, LANES).astype(jnp.bfloat16)
            )


def column_attention(items, half, before, x, gain, bias, weights, g_b, o_b):
    width = x.shape[2]
    seqs = x.size // (items * width)
    at_once = 4
    whole = pl.BlockSpec(x.shape, lambda r: (0, 0, 0))
    vector = pl.BlockSpec((1, width), lambda r: (0, 0))
    weight = pl.BlockSpec((5, width, width), lambda r: (0, 0, 0))
    return pl.pallas_call(
        functools.partial(column_kernel, at_once),
        grid=(items // at_once,),
        out_shape=[jax.ShapeDtypeStruct((DAP, HALVES * x.shape[1], width), jnp.bfloat16)],
        in_specs=[whole, vector, vector, weight, vector, vector]
        + [pl.BlockSpec(memory_space=pl.ANY)] * len(before),
        out_specs=[pl.BlockSpec(x.shape, lambda r: (0, half, 0))],
        input_output_aliases={6: 0} if before else {},
        scratch_shapes=[
            pltpu.VMEM((width // LANES, seqs * items, LANES), jnp.float32),
            pltpu.VMEM((2, GROUP * seqs, seqs), jnp.float32),
            pltpu.VMEM((2, GROUP * seqs, seqs), jnp.bfloat16),
        ],
        compiler_params=pltpu.CompilerParams(vmem_limit_bytes=44 * MIB),
        name="column_attention",
    )(
        x, gain.reshape(1, -1), bias.reshape(1, -1), weights, g_b.reshape(1, -1), o_b.reshape(1, -1), *before
    )


def fetch(value, z=0, x=0, y=0):
    pairs = []
    for dz in range(NZ):
        for dx in range(NX):
            for dy in range(NY):
                src = ((dz + z) % NZ * NX + (dx + x) % NX) * NY + (dy + y) % NY
                pairs.append((src, (dz * NX + dx) * NY + dy))
    return lax.ppermute(value, "dap", pairs)


def join_kernel(*refs):
    count = len(refs) - 2
    parts, out_ref, sems = refs[:count], refs[count], refs[count + 1]
    place, copies = 0, []
    for n, part in enumerate(parts):
        size = part.shape[0]
        copies.append(pltpu.make_async_copy(part, out_ref.at[pl.ds(place, size)], sems.at[n]))
        place += size
    for copy in copies:
        copy.start()
    for copy in copies:
        copy.wait()


def join(*parts):
    total = sum(part.shape[0] for part in parts)
    return pl.pallas_call(
        join_kernel,
        out_shape=jax.ShapeDtypeStruct((total,) + parts[0].shape[1:], parts[0].dtype),
        in_specs=[pl.BlockSpec(memory_space=pl.ANY)] * len(parts),
        out_specs=pl.BlockSpec(memory_space=pl.ANY),
        scratch_shapes=[pltpu.SemaphoreType.DMA((len(parts),))],
        compiler_params=pltpu.CompilerParams(vmem_limit_bytes=4 * MIB),
        name="join",
    )(*parts)


def exchange(value):
    return lax.all_to_all(value, "dap", split_axis=0, concat_axis=0, tiled=True)


def per_device(
    alignment,
    pair_state,
    row_norm_gain,
    row_norm_bias,
    pair_norm_gain,
    pair_weight,
    row_query,
    row_key,
    row_value,
    row_gate,
    row_gate_bias,
    row_output,
    row_output_bias,
    column_norm_gain,
    column_norm_bias,
    column_query,
    column_key,
    column_value,
    column_gate,
    column_gate_bias,
    column_output,
    column_output_bias,
):
    seqs, res, width = alignment.shape
    own = res // DAP
    me = lax.axis_index("dap")
    here = jnp.stack([me // (NX * NY), me // NY % NX, me % NY]).astype(jnp.int32)
    local = pair_bias(pair_state, pair_norm_gain, pair_weight)[None]
    pair = join(local, fetch(local, y=1))
    near = [fetch(pair, x=step) for step in (1, 2, 3)]
    far_pair = fetch(pair, z=2)
    weights = stack(column_query, column_key, column_value, column_gate, column_output)
    near, weights = lax.optimization_barrier((near, weights))
    own_plane = join(pair, *near)
    own_plane, far_pair, inputs = lax.optimization_barrier((own_plane, far_pair, alignment))
    ahead, behind = fetch(own_plane, z=1), fetch(own_plane, z=3)
    far_plane = join(far_pair, *(fetch(far_pair, x=step) for step in (1, 2, 3)))
    projected = row_project(
        inputs, row_norm_gain, row_norm_bias, row_query, row_key, row_value, row_gate, row_gate_bias
    )

    def attend(blocks, biases, *held, grant=24):
        return row_attention(
            grant, blocks, here, *projected, alignment, biases, row_output, row_output_bias, held
        )

    after = attend(((0, 0, 0), (0, 1, 0)), [own_plane])
    after = attend(((2, 0, 0), (2, 1, 0)), [far_plane], *after)
    first = attend(((1, 0, 0), (3, 0, 1)), [ahead, behind], after[0])[0]
    second = attend(((1, 1, 0), (3, 1, 1)), [ahead, behind], after[1], grant=56)[0]
    first, second = lax.optimization_barrier((exchange(first), second))
    items = own // HALVES
    columns = ()
    for half, part in enumerate((first, exchange(second))):
        columns = column_attention(
            items,
            half,
            columns,
            part,
            column_norm_gain,
            column_norm_bias,
            weights,
            column_gate_bias,
            column_output_bias,
        )
    back = exchange(columns[0]).reshape(DAP, HALVES, seqs, items, width)
    return back.transpose(2, 0, 1, 3, 4).reshape(alignment.shape)


def solution(mesh):
    split = P(("batch", "dap"), None, None)
    return jax.shard_map(
        per_device,
        mesh=mesh,
        in_specs=(split, split) + (P(),) * 20,
        out_specs=split,
        check_vma=False,
    )
```

```python
import functools

import jax
import jax.numpy as jnp
from jax import lax
from jax.experimental import pallas as pl
from jax.experimental.pallas import tpu as pltpu
from jax.sharding import PartitionSpec as P

H = 8
HEAD = 32
C = 256
LANES = 128
GROUP = LANES // HEAD
EPS = 1e-05
MIB = 1024 * 1024
HALVES = 2
HALF_ROWS = 8
NZ, NX, NY = 4, 4, 2
DAP = NZ * NX * NY
NT = (((1,), (1,)), ((), ()))


def norm(x, gain, bias, center=None):
    if center is None:
        center = jnp.mean(x, axis=-1, keepdims=True)
    moved = x - center
    spread = jnp.mean(moved * moved, axis=-1, keepdims=True)
    return moved * lax.rsqrt(spread + EPS) * gain + bias


def lanes_of(part):
    return slice(part * LANES, (part + 1) * LANES)


def dot(a, b):
    return jnp.dot(a, b, preferred_element_type=jnp.float32)


def softmax_rounded(scores):
    top = jnp.max(scores, axis=-1, keepdims=True)
    e = jnp.exp(scores - top)
    total = jnp.sum(e, axis=-1, keepdims=True)
    return (e * (1.0 / total)).astype(jnp.bfloat16)


def head_of_lane():
    return lax.broadcasted_iota(jnp.int32, (1, LANES), 1) // HEAD


def stacked(q):
    head = head_of_lane()
    masks = [(head == i).astype(jnp.float32).astype(jnp.bfloat16) for i in range(GROUP)]
    return jnp.concatenate([q * mask for mask in masks], axis=0)


def own_lanes(mixed):
    head = head_of_lane()
    rows = mixed.shape[0] // GROUP
    total = mixed[:rows]
    for i in range(1, GROUP):
        total = jnp.where(head == i, mixed[i * rows : (i + 1) * rows], total)
    return total


def pipelined(count, score, soften, average):
    scores, weights = {0: score(0)}, {}
    for n in range(count + 1):
        if n + 1 < count:
            scores[n + 1] = score(n + 1)
        if n < count:
            weights[n] = soften(n, scores.pop(n))
        if n >= 1:
            average(n - 1, weights.pop(n - 1))


def project(normed, at_queries, q_w, k_w, v_w, g_w, g_b):
    q = (dot(at_queries, q_w[...]) * HEAD ** (-0.5)).astype(jnp.bfloat16)
    k_t = dot(normed, k_w[...]).T.astype(jnp.bfloat16)
    v = dot(normed, v_w[...]).astype(jnp.bfloat16)
    g = jax.nn.sigmoid(dot(at_queries, g_w[...]) + g_b[...])
    return q, k_t, v, g


def pair_kernel(x_ref, gain_ref, w_ref, out_ref, held):
    step = pl.program_id(0)
    rows, _, cz = x_ref.shape
    mean = jnp.full((cz, cz), 1.0 / cz, jnp.bfloat16)
    for i in range(rows):
        x = x_ref[i]
        normed = norm(x.astype(jnp.float32), gain_ref[...], 0.0, dot(x, mean)).astype(jnp.bfloat16)
        bias = lax.dot_general(w_ref[...], normed, NT, preferred_element_type=jnp.float32)
        for part in range(held.shape[0]):
            low = step * rows // HALF_ROWS * (H * HALF_ROWS) + lax.rem(step * rows, HALF_ROWS) + i
            held[part, pl.ds(low, H, stride=HALF_ROWS), :] = bias[:, lanes_of(part)]

    @pl.when(step == pl.num_programs(0) - 1)
    def _():
        for part in range(held.shape[0]):
            out_ref[:, :, lanes_of(part)] = (
                held[part].astype(jnp.bfloat16).reshape(out_ref.shape[:2] + (LANES,))
            )


def pair_bias(pair_state, gain, weight):
    count, res, cz = pair_state.shape
    rows = 4
    return pl.pallas_call(
        pair_kernel,
        grid=(count // rows,),
        out_shape=jax.ShapeDtypeStruct((H, count, res), jnp.bfloat16),
        in_specs=[
            pl.BlockSpec((rows, res, cz), lambda i: (i, 0, 0)),
            pl.BlockSpec((1, cz), lambda i: (0, 0)),
            pl.BlockSpec((H, cz), lambda i: (0, 0)),
        ],
        out_specs=pl.BlockSpec((H, count, res), lambda i: (0, 0, 0)),
        scratch_shapes=[pltpu.VMEM((res // LANES, H * count, LANES), jnp.float32)],
        compiler_params=pltpu.CompilerParams(vmem_limit_bytes=56 * MIB),
        name="pair_bias",
    )(pair_state, gain.reshape(1, cz), weight.T)


def project_kernel(x_ref, gain, bias, q_w, k_w, v_w, g_w, g_b, q_ref, k_ref, v_ref, g_ref):
    count, res, width = x_ref.shape
    x = x_ref[...].reshape(count * res, width).astype(jnp.float32)
    normed = norm(x, gain[...], bias[...])
    split = normed.reshape(count, DAP, HALVES, HALF_ROWS, width)
    halves = [split[:, :, half].reshape(count, res // HALVES, width) for half in range(HALVES)]
    at_queries = jnp.concatenate(halves, axis=1).reshape(count * res, width)
    q, k_t, v, g = project(
        normed.astype(jnp.bfloat16), at_queries.astype(jnp.bfloat16), q_w, k_w, v_w, g_w, g_b
    )
    for out_ref, value in ((q_ref, q), (v_ref, v), (g_ref, g)):
        out_ref[...] = value.reshape(count, res, width)
    for n in range(count):
        k_ref[n] = k_t[:, n * res : (n + 1) * res]


def row_project(x, gain, bias, q_w, k_w, v_w, g_w, g_b):
    seqs, res, width = x.shape
    count = 2
    block = pl.BlockSpec((count, res, width), lambda s: (s, 0, 0))
    turned = pl.BlockSpec((count, width, res), lambda s: (s, 0, 0))
    vector = pl.BlockSpec((1, width), lambda s: (0, 0))
    weight = pl.BlockSpec((width, width), lambda s: (0, 0))
    shape = jax.ShapeDtypeStruct
    return pl.pallas_call(
        project_kernel,
        grid=(seqs // count,),
        out_shape=[
            shape((seqs, res, width), jnp.bfloat16),
            shape((seqs, width, res), jnp.bfloat16),
            shape((seqs, res, width), jnp.bfloat16),
            shape((seqs, res, width), jnp.float32),
        ],
        in_specs=[block, vector, vector] + [weight] * 4 + [vector],
        out_specs=[block, turned, block, block],
        compiler_params=pltpu.CompilerParams(vmem_limit_bytes=24 * MIB),
        cost_estimate=pl.CostEstimate(
            flops=2 * seqs * res * width * width * 4,
            bytes_accessed=x.size * 12,
            transcendentals=x.size * 2,
        ),
        name="row_project",
    )(x, gain.reshape(1, -1), bias.reshape(1, -1), q_w, k_w, v_w, g_w, g_b.reshape(1, -1))


def stack_kernel(*refs):
    for n, ref in enumerate(refs[:-1]):
        refs[-1][n] = ref[...]


def stack(*weights):
    return pl.pallas_call(
        stack_kernel,
        out_shape=jax.ShapeDtypeStruct((len(weights),) + weights[0].shape, weights[0].dtype),
        compiler_params=pltpu.CompilerParams(vmem_limit_bytes=16 * MIB),
        name="stack",
    )(*weights)


def row_kernel(blocks, here_ref, *refs):
    count = len(blocks)
    planes = 1 + max(which for _, _, which in blocks)
    q_refs, g_refs, x_refs, (k_ref, v_ref) = refs[:2], refs[2:4], refs[4:6], refs[6:8]
    bias_refs, (o_w, o_b) = refs[8 : 8 + planes], refs[8 + planes : 10 + planes]
    held, weights, ready, sems = refs[-4:]
    halves = sorted({half for _, half, _ in blocks})
    outs = dict(zip(halves, refs[-4 - len(halves) : -4]))
    step, last = pl.program_id(0), pl.num_programs(0) - 1
    seqs, part_rows, width = q_refs[0].shape
    tile = count * part_rows
    owners = part_rows // HALF_ROWS
    groups = H // GROUP

    def place(n):
        return n // groups, n % groups, lanes_of(n % groups)

    def both(pick):
        return jnp.concatenate([pick(n) for n in range(count)], axis=0)

    def score(n):
        seq, _, lanes = place(n)
        q = both(lambda b: q_refs[b][seq, :, lanes])
        held[n % 2] = dot(stacked(q), k_ref[seq, lanes, :])

    def slot(x, y):
        return lax.rem(x - here_ref[1] + NX, NX) * NY + lax.rem(y - here_ref[2] + NY, NY)

    slots = [slot(x, y) for x in range(NX) for y in range(NY)]
    taken = 2

    def soften(n, _):
        _, group, _ = place(n)
        for b, (_, half, which) in enumerate(blocks):
            for two in range(0, GROUP, 2):
                for first in range(0, owners, taken):
                    piece = (half * H + group * GROUP + two) // 2
                    bias = [
                        bias_refs[which][slots[o], piece].astype(jnp.float32)
                        for o in range(first, first + taken)
                    ]
                    for i in range(2):
                        low = (two + i) * tile + b * part_rows + first * HALF_ROWS
                        rows = slice(low, low + taken * HALF_ROWS)
                        mine = [value[i * HALF_ROWS : (i + 1) * HALF_ROWS] for value in bias]
                        weights[n % 2, rows] = softmax_rounded(
                            held[n % 2, rows] + jnp.concatenate(mine, axis=0)
                        )

    gated, done = {}, []

    def average(n, _):
        seq, group, lanes = place(n)
        mixed = own_lanes(dot(weights[n % 2], v_ref[seq, :, lanes]))
        gated[group] = (mixed * both(lambda b: g_refs[b][seq, :, lanes])).astype(jnp.bfloat16)
        if len(gated) == groups:
            whole = jnp.concatenate([gated.pop(part) for part in range(groups)], axis=1)
            update = dot(whole, o_w[...]) + o_b[...]
            after = []
            for b, (_, half, _) in enumerate(blocks):
                x = x_refs[b][seq].astype(jnp.float32).reshape(owners, HALVES, HALF_ROWS, width)
                own = update[b * part_rows : (b + 1) * part_rows].reshape(owners, HALF_ROWS, width)
                after.append(x[:, half] + own)
            done.append(after)
            if len(done) == 2:
                low = (seq - 1) * HALF_ROWS
                for b in range(count):
                    rows = jnp.concatenate([value[b] for value in done], axis=1)
                    ready[step, b, :, low : low + 2 * HALF_ROWS] = rows.astype(jnp.bfloat16)
                done.clear()

    pipelined(seqs * groups, score, soften, average)

    def copies(step):
        for b, (plane, half, _) in enumerate(blocks):
            first = pl.multiple_of(lax.rem(here_ref[0] + plane, NZ) * owners, owners)
            rows = pl.ds(pl.multiple_of(step * seqs * HALF_ROWS, seqs * HALF_ROWS), seqs * HALF_ROWS)
            yield pltpu.make_async_copy(
                ready.at[step, b], outs[half].at[pl.ds(first, owners), rows], sems.at[step, b]
            )

    for copy in copies(step):
        copy.start()

    @pl.when(step == last)
    def _():
        for n in range(ready.shape[0]):
            for copy in copies(n):
                copy.wait()


def row_attention(grant, blocks, here, q, k, v, g, x, biases, o_w, o_b, held):
    seqs, res, width = x.shape
    own = res // DAP
    part_rows = DAP // NZ * HALF_ROWS
    once = 8
    halves = sorted({half for _, half, _ in blocks})

    def which(here, plane):
        return lax.rem(here[0] + plane, NZ)

    queries = [
        pl.BlockSpec(
            (once, part_rows, width),
            lambda s, here, plane=plane, half=half: (s, half * NZ + which(here, plane), 0),
        )
        for plane, half, _ in blocks
    ]
    residual = [
        pl.BlockSpec((once, res // NZ, width), lambda s, here, plane=plane: (s, which(here, plane), 0))
        for plane, _, _ in blocks
    ]
    args = [q, q, g, g, x, x, k, v, *biases, o_w, o_b.reshape(1, -1), *held]
    return pl.pallas_call(
        functools.partial(row_kernel, blocks),
        out_shape=[jax.ShapeDtypeStruct((DAP, seqs * HALF_ROWS, width), jnp.bfloat16)] * len(halves),
        grid_spec=pltpu.PrefetchScalarGridSpec(
            num_scalar_prefetch=1,
            grid=(seqs // once,),
            in_specs=queries
            + queries
            + residual
            + [
                pl.BlockSpec((once, width, res), lambda s, here: (s, 0, 0)),
                pl.BlockSpec((once, res, width), lambda s, here: (s, 0, 0)),
            ]
            + [pl.BlockSpec(bias.shape, lambda s, here: (0, 0, 0, 0)) for bias in biases]
            + [
                pl.BlockSpec((width, width), lambda s, here: (0, 0)),
                pl.BlockSpec((1, width), lambda s, here: (0, 0)),
            ]
            + [pl.BlockSpec(memory_space=pl.ANY)] * len(held),
            out_specs=[pl.BlockSpec(memory_space=pl.ANY)] * len(halves),
            scratch_shapes=[
                pltpu.VMEM((2, GROUP * part_rows * len(blocks), res), jnp.float32),
                pltpu.VMEM((2, GROUP * part_rows * len(blocks), res), jnp.bfloat16),
                pltpu.VMEM(
                    (seqs // once, len(blocks), DAP // NZ, once * HALF_ROWS, width), jnp.bfloat16
                ),
                pltpu.SemaphoreType.DMA((seqs // once, len(blocks))),
            ],
        ),
        input_output_aliases={len(args) + 1 - len(held) + n: n for n in range(len(held))},
        compiler_params=pltpu.CompilerParams(vmem_limit_bytes=grant * MIB),
        cost_estimate=pl.CostEstimate(
            flops=seqs * H * part_rows * len(blocks) * res * 256 * 16,
            bytes_accessed=8 * 1024 * 1024,
            transcendentals=seqs * H * part_rows * len(blocks) * res,
        ),
        name="row_attention",
    )(here, *args)


def column_kernel(at_once, x_ref, gain, bias, w_ref, g_b, o_b, *refs):
    q_w, k_w, v_w, g_w, o_w = (w_ref.at[n] for n in range(5))
    out_ref, held, scores, weights = refs[-4:]
    step = pl.program_id(0)
    owners, per, width = x_ref.shape
    items = pl.num_programs(0) * at_once
    seqs = owners * per // items
    parts = width // LANES

    @pl.when(step == 0)
    def _():
        for part in range(parts):
            held[part] = x_ref[:, :, lanes_of(part)].astype(jnp.float32).reshape(-1, LANES)

    mine = [pl.ds(step * at_once + n, seqs, stride=items) for n in range(at_once)]
    x = jnp.concatenate(
        [jnp.concatenate([held[part, rows, :] for rows in mine], axis=0) for part in range(parts)], axis=1
    )
    normed = norm(x, gain[...], bias[...]).astype(jnp.bfloat16)
    q, k_t, v, g = project(normed, normed, q_w, k_w, v_w, g_w, g_b)
    gated = {}

    def place(n):
        return slice(n // parts * seqs, (n // parts + 1) * seqs), lanes_of(n % parts)

    def score(n):
        rows, lanes = place(n)
        scores[n % 2] = dot(stacked(q[rows, lanes]), k_t[lanes, rows])

    def soften(n, _):
        for low in range(0, GROUP * seqs, 32):
            weights[n % 2, low : low + 32] = softmax_rounded(scores[n % 2, low : low + 32])

    def average(n, _):
        rows, lanes = place(n)
        mixed = own_lanes(dot(weights[n % 2], v[rows, lanes]))
        gated[n] = (mixed * g[rows, lanes]).astype(jnp.bfloat16)

    pipelined(at_once * parts, score, soften, average)
    gated = [
        jnp.concatenate([gated[n * parts + part] for part in range(parts)], axis=1)
        for n in range(at_once)
    ]
    after = x + (dot(jnp.concatenate(gated, axis=0), o_w[...]) + o_b[...])
    for n, rows in enumerate(mine):
        for part in range(parts):
            held[part, rows, :] = after[n * seqs : (n + 1) * seqs, lanes_of(part)]

    @pl.when(step == pl.num_programs(0) - 1)
    def _():
        for part in range(parts):
            out_ref[:, :, lanes_of(part)] = (
                held[part].reshape(owners, per, LANES).astype(jnp.bfloat16)
            )


def column_attention(items, half, before, x, gain, bias, weights, g_b, o_b):
    width = x.shape[2]
    seqs = x.size // (items * width)
    at_once = 8
    whole = pl.BlockSpec(x.shape, lambda r: (0, 0, 0))
    vector = pl.BlockSpec((1, width), lambda r: (0, 0))
    weight = pl.BlockSpec((5, width, width), lambda r: (0, 0, 0))
    return pl.pallas_call(
        functools.partial(column_kernel, at_once),
        grid=(items // at_once,),
        out_shape=[jax.ShapeDtypeStruct((DAP, HALVES * x.shape[1], width), jnp.bfloat16)],
        in_specs=[whole, vector, vector, weight, vector, vector]
        + [pl.BlockSpec(memory_space=pl.ANY)] * len(before),
        out_specs=[pl.BlockSpec(x.shape, lambda r: (0, half, 0))],
        input_output_aliases={6: 0} if before else {},
        scratch_shapes=[
            pltpu.VMEM((width // LANES, seqs * items, LANES), jnp.float32),
            pltpu.VMEM((2, GROUP * seqs, seqs), jnp.float32),
            pltpu.VMEM((2, GROUP * seqs, seqs), jnp.bfloat16),
        ],
        compiler_params=pltpu.CompilerParams(vmem_limit_bytes=44 * MIB),
        name="column_attention",
    )(
        x, gain.reshape(1, -1), bias.reshape(1, -1), weights, g_b.reshape(1, -1), o_b.reshape(1, -1), *before
    )


def fetch(value, z=0, x=0, y=0):
    pairs = []
    for dz in range(NZ):
        for dx in range(NX):
            for dy in range(NY):
                src = ((dz + z) % NZ * NX + (dx + x) % NX) * NY + (dy + y) % NY
                pairs.append((src, (dz * NX + dx) * NY + dy))
    return lax.ppermute(value, "dap", pairs)


def join_kernel(*refs):
    count = len(refs) - 2
    parts, out_ref, sems = refs[:count], refs[count], refs[count + 1]
    place, copies = 0, []
    for n, part in enumerate(parts):
        size = part.shape[0]
        copies.append(pltpu.make_async_copy(part, out_ref.at[pl.ds(place, size)], sems.at[n]))
        place += size
    for copy in copies:
        copy.start()
    for copy in copies:
        copy.wait()


def join(*parts):
    total = sum(part.shape[0] for part in parts)
    return pl.pallas_call(
        join_kernel,
        out_shape=jax.ShapeDtypeStruct((total,) + parts[0].shape[1:], parts[0].dtype),
        in_specs=[pl.BlockSpec(memory_space=pl.ANY)] * len(parts),
        out_specs=pl.BlockSpec(memory_space=pl.ANY),
        scratch_shapes=[pltpu.SemaphoreType.DMA((len(parts),))],
        compiler_params=pltpu.CompilerParams(vmem_limit_bytes=4 * MIB),
        name="join",
    )(*parts)


def exchange(value):
    return lax.all_to_all(value, "dap", split_axis=0, concat_axis=0, tiled=True)


def per_device(
    alignment,
    pair_state,
    row_norm_gain,
    row_norm_bias,
    pair_norm_gain,
    pair_weight,
    row_query,
    row_key,
    row_value,
    row_gate,
    row_gate_bias,
    row_output,
    row_output_bias,
    column_norm_gain,
    column_norm_bias,
    column_query,
    column_key,
    column_value,
    column_gate,
    column_gate_bias,
    column_output,
    column_output_bias,
):
    seqs, res, width = alignment.shape
    own = res // DAP
    me = lax.axis_index("dap")
    here = jnp.stack([me // (NX * NY), me // NY % NX, me % NY]).astype(jnp.int32)
    local = pair_bias(pair_state, pair_norm_gain, pair_weight)[None]
    pair = join(local, fetch(local, y=1))
    near = [fetch(pair, x=step) for step in (1, 2, 3)]
    far_pair = fetch(pair, z=2)
    weights = stack(column_query, column_key, column_value, column_gate, column_output)
    near, weights = lax.optimization_barrier((near, weights))
    own_plane = join(pair, *near)
    own_plane, far_pair, gain = lax.optimization_barrier((own_plane, far_pair, row_norm_gain))
    ahead, behind = fetch(own_plane, z=1), fetch(own_plane, z=3)
    far_plane = join(far_pair, *(fetch(far_pair, x=step) for step in (1, 2, 3)))
    projected = row_project(
        alignment, gain, row_norm_bias, row_query, row_key, row_value, row_gate, row_gate_bias
    )

    def attend(blocks, biases, *held, grant=32):
        return row_attention(
            grant, blocks, here, *projected, alignment, biases, row_output, row_output_bias, held
        )

    after = attend(((0, 0, 0), (0, 1, 0)), [own_plane])
    after = attend(((2, 0, 0), (2, 1, 0)), [far_plane], *after)
    first = attend(((1, 0, 0), (3, 0, 1)), [ahead, behind], after[0])[0]
    second = attend(((1, 1, 0), (3, 1, 1)), [ahead, behind], after[1], grant=56)[0]
    first, second = lax.optimization_barrier((exchange(first), second))
    items = own // HALVES
    columns = ()
    for half, part in enumerate((first, exchange(second))):
        columns = column_attention(
            items,
            half,
            columns,
            part,
            column_norm_gain,
            column_norm_bias,
            weights,
            column_gate_bias,
            column_output_bias,
        )
    back = exchange(columns[0]).reshape(DAP, HALVES, seqs, items, width)
    return back.transpose(2, 0, 1, 3, 4).reshape(alignment.shape)


def solution(mesh):
    split = P(("batch", "dap"), None, None)
    return jax.shard_map(
        per_device,
        mesh=mesh,
        in_specs=(split, split) + (P(),) * 20,
        out_specs=split,
        check_vma=False,
    )
```

```python
import functools

import jax
import jax.numpy as jnp
from jax import lax
from jax.experimental import pallas as pl
from jax.experimental.pallas import tpu as pltpu
from jax.sharding import PartitionSpec as P

H = 8
HEAD = 32
C = 256
LANES = 128
GROUP = LANES // HEAD
EPS = 1e-05
MIB = 1024 * 1024
HALVES = 2
HALF_ROWS = 8
NZ, NX, NY = 4, 4, 2
DAP = NZ * NX * NY
NT = (((1,), (1,)), ((), ()))


def norm(x, gain, bias, center=None):
    if center is None:
        center = jnp.mean(x, axis=-1, keepdims=True)
    moved = x - center
    spread = jnp.mean(moved * moved, axis=-1, keepdims=True)
    return moved * lax.rsqrt(spread + EPS) * gain + bias


def lanes_of(part):
    return slice(part * LANES, (part + 1) * LANES)


def dot(a, b):
    return jnp.dot(a, b, preferred_element_type=jnp.float32)


def softmax_rounded(scores):
    top = jnp.max(scores, axis=-1, keepdims=True)
    e = jnp.exp(scores - top)
    total = jnp.sum(e, axis=-1, keepdims=True)
    return (e * (1.0 / total)).astype(jnp.bfloat16)


def head_of_lane():
    return lax.broadcasted_iota(jnp.int32, (1, LANES), 1) // HEAD


def stacked(q):
    head = head_of_lane()
    masks = [(head == i).astype(jnp.float32).astype(jnp.bfloat16) for i in range(GROUP)]
    return jnp.concatenate([q * mask for mask in masks], axis=0)


def own_lanes(mixed):
    head = head_of_lane()
    rows = mixed.shape[0] // GROUP
    total = mixed[:rows]
    for i in range(1, GROUP):
        total = jnp.where(head == i, mixed[i * rows : (i + 1) * rows], total)
    return total


def pipelined(count, score, soften, average):
    scores, weights = {0: score(0)}, {}
    for n in range(count + 1):
        if n + 1 < count:
            scores[n + 1] = score(n + 1)
        if n < count:
            weights[n] = soften(n, scores.pop(n))
        if n >= 1:
            average(n - 1, weights.pop(n - 1))


def project(normed, at_queries, q_w, k_w, v_w, g_w, g_b):
    q = (dot(at_queries, q_w[...]) * HEAD ** (-0.5)).astype(jnp.bfloat16)
    k_t = dot(normed, k_w[...]).T.astype(jnp.bfloat16)
    v = dot(normed, v_w[...]).astype(jnp.bfloat16)
    g = jax.nn.sigmoid(dot(at_queries, g_w[...]) + g_b[...])
    return q, k_t, v, g


def pair_kernel(x_ref, gain_ref, w_ref, out_ref, held):
    step = pl.program_id(0)
    rows, _, cz = x_ref.shape
    mean = jnp.full((cz, cz), 1.0 / cz, jnp.bfloat16)
    for i in range(rows):
        x = x_ref[i]
        normed = norm(x.astype(jnp.float32), gain_ref[...], 0.0, dot(x, mean)).astype(jnp.bfloat16)
        bias = lax.dot_general(w_ref[...], normed, NT, preferred_element_type=jnp.float32)
        for part in range(held.shape[0]):
            low = step * rows // HALF_ROWS * (H * HALF_ROWS) + lax.rem(step * rows, HALF_ROWS) + i
            held[part, pl.ds(low, H, stride=HALF_ROWS), :] = bias[:, lanes_of(part)]

    @pl.when(step == pl.num_programs(0) - 1)
    def _():
        for part in range(held.shape[0]):
            out_ref[:, :, lanes_of(part)] = (
                held[part].astype(jnp.bfloat16).reshape(out_ref.shape[:2] + (LANES,))
            )


def pair_bias(pair_state, gain, weight):
    count, res, cz = pair_state.shape
    rows = 4
    return pl.pallas_call(
        pair_kernel,
        grid=(count // rows,),
        out_shape=jax.ShapeDtypeStruct((H, count, res), jnp.bfloat16),
        in_specs=[
            pl.BlockSpec((rows, res, cz), lambda i: (i, 0, 0)),
            pl.BlockSpec((1, cz), lambda i: (0, 0)),
            pl.BlockSpec((H, cz), lambda i: (0, 0)),
        ],
        out_specs=pl.BlockSpec((H, count, res), lambda i: (0, 0, 0)),
        scratch_shapes=[pltpu.VMEM((res // LANES, H * count, LANES), jnp.float32)],
        compiler_params=pltpu.CompilerParams(vmem_limit_bytes=56 * MIB),
        name="pair_bias",
    )(pair_state, gain.reshape(1, cz), weight.T)


def project_kernel(x_ref, gain, bias, q_w, k_w, v_w, g_w, g_b, q_ref, k_ref, v_ref, g_ref):
    count, res, width = x_ref.shape
    x = x_ref[...].reshape(count * res, width).astype(jnp.float32)
    normed = norm(x, gain[...], bias[...])
    split = normed.reshape(count, DAP, HALVES, HALF_ROWS, width)
    halves = [split[:, :, half].reshape(count, res // HALVES, width) for half in range(HALVES)]
    at_queries = jnp.concatenate(halves, axis=1).reshape(count * res, width)
    q, k_t, v, g = project(
        normed.astype(jnp.bfloat16), at_queries.astype(jnp.bfloat16), q_w, k_w, v_w, g_w, g_b
    )
    for out_ref, value in ((q_ref, q), (v_ref, v), (g_ref, g)):
        out_ref[...] = value.reshape(count, res, width)
    for n in range(count):
        k_ref[n] = k_t[:, n * res : (n + 1) * res]


def row_project(x, gain, bias, q_w, k_w, v_w, g_w, g_b):
    seqs, res, width = x.shape
    count = 2
    block = pl.BlockSpec((count, res, width), lambda s: (s, 0, 0))
    turned = pl.BlockSpec((count, width, res), lambda s: (s, 0, 0))
    vector = pl.BlockSpec((1, width), lambda s: (0, 0))
    weight = pl.BlockSpec((width, width), lambda s: (0, 0))
    shape = jax.ShapeDtypeStruct
    return pl.pallas_call(
        project_kernel,
        grid=(seqs // count,),
        out_shape=[
            shape((seqs, res, width), jnp.bfloat16),
            shape((seqs, width, res), jnp.bfloat16),
            shape((seqs, res, width), jnp.bfloat16),
            shape((seqs, res, width), jnp.float32),
        ],
        in_specs=[block, vector, vector] + [weight] * 4 + [vector],
        out_specs=[block, turned, block, block],
        compiler_params=pltpu.CompilerParams(vmem_limit_bytes=24 * MIB),
        cost_estimate=pl.CostEstimate(
            flops=2 * seqs * res * width * width * 4,
            bytes_accessed=x.size * 12,
            transcendentals=x.size * 2,
        ),
        name="row_project",
    )(x, gain.reshape(1, -1), bias.reshape(1, -1), q_w, k_w, v_w, g_w, g_b.reshape(1, -1))


def stack_kernel(*refs):
    for n, ref in enumerate(refs[:-1]):
        refs[-1][n] = ref[...]


def stack(*weights):
    return pl.pallas_call(
        stack_kernel,
        out_shape=jax.ShapeDtypeStruct((len(weights),) + weights[0].shape, weights[0].dtype),
        compiler_params=pltpu.CompilerParams(vmem_limit_bytes=16 * MIB),
        name="stack",
    )(*weights)


def row_kernel(blocks, here_ref, *refs):
    count = len(blocks)
    planes = 1 + max(which for _, _, which in blocks)
    q_refs, g_refs, x_refs, (k_ref, v_ref) = refs[:2], refs[2:4], refs[4:6], refs[6:8]
    bias_refs, (o_w, o_b) = refs[8 : 8 + planes], refs[8 + planes : 10 + planes]
    held, weights, ready, sems = refs[-4:]
    halves = sorted({half for _, half, _ in blocks})
    outs = dict(zip(halves, refs[-4 - len(halves) : -4]))
    step, last = pl.program_id(0), pl.num_programs(0) - 1
    seqs, part_rows, width = q_refs[0].shape
    tile = count * part_rows
    owners = part_rows // HALF_ROWS
    groups = H // GROUP

    def place(n):
        return n // groups, n % groups, lanes_of(n % groups)

    def both(pick):
        return jnp.concatenate([pick(n) for n in range(count)], axis=0)

    def score(n):
        seq, _, lanes = place(n)
        q = both(lambda b: q_refs[b][seq, :, lanes])
        held[n % 2] = dot(stacked(q), k_ref[seq, lanes, :])

    def slot(x, y):
        return lax.rem(x - here_ref[1] + NX, NX) * NY + lax.rem(y - here_ref[2] + NY, NY)

    slots = [slot(x, y) for x in range(NX) for y in range(NY)]
    taken = 2

    def soften(n, _):
        _, group, _ = place(n)
        for b, (_, half, which) in enumerate(blocks):
            for two in range(0, GROUP, 2):
                for first in range(0, owners, taken):
                    piece = (half * H + group * GROUP + two) // 2
                    bias = [
                        bias_refs[which][slots[o], piece].astype(jnp.float32)
                        for o in range(first, first + taken)
                    ]
                    for i in range(2):
                        low = (two + i) * tile + b * part_rows + first * HALF_ROWS
                        rows = slice(low, low + taken * HALF_ROWS)
                        mine = [value[i * HALF_ROWS : (i + 1) * HALF_ROWS] for value in bias]
                        weights[n % 2, rows] = softmax_rounded(
                            held[n % 2, rows] + jnp.concatenate(mine, axis=0)
                        )

    gated, done = {}, []

    def average(n, _):
        seq, group, lanes = place(n)
        mixed = own_lanes(dot(weights[n % 2], v_ref[seq, :, lanes]))
        gated[group] = (mixed * both(lambda b: g_refs[b][seq, :, lanes])).astype(jnp.bfloat16)
        if len(gated) == groups:
            whole = jnp.concatenate([gated.pop(part) for part in range(groups)], axis=1)
            update = dot(whole, o_w[...]) + o_b[...]
            after = []
            for b, (_, half, _) in enumerate(blocks):
                x = x_refs[b][seq].astype(jnp.float32).reshape(owners, HALVES, HALF_ROWS, width)
                own = update[b * part_rows : (b + 1) * part_rows].reshape(owners, HALF_ROWS, width)
                after.append(x[:, half] + own)
            done.append(after)
            if len(done) == 2:
                low = (seq - 1) * HALF_ROWS
                for b in range(count):
                    rows = jnp.concatenate([value[b] for value in done], axis=1)
                    ready[step, b, :, low : low + 2 * HALF_ROWS] = rows.astype(jnp.bfloat16)
                done.clear()

    pipelined(seqs * groups, score, soften, average)

    def copies(step):
        for b, (plane, half, _) in enumerate(blocks):
            first = pl.multiple_of(lax.rem(here_ref[0] + plane, NZ) * owners, owners)
            rows = pl.ds(pl.multiple_of(step * seqs * HALF_ROWS, seqs * HALF_ROWS), seqs * HALF_ROWS)
            yield pltpu.make_async_copy(
                ready.at[step, b], outs[half].at[pl.ds(first, owners), rows], sems.at[step, b]
            )

    for copy in copies(step):
        copy.start()

    @pl.when(step == last)
    def _():
        for n in range(ready.shape[0]):
            for copy in copies(n):
                copy.wait()


def row_attention(grant, blocks, here, q, k, v, g, x, biases, o_w, o_b, held):
    seqs, res, width = x.shape
    own = res // DAP
    part_rows = DAP // NZ * HALF_ROWS
    once = 8 if grant < 56 else 4
    halves = sorted({half for _, half, _ in blocks})

    def which(here, plane):
        return lax.rem(here[0] + plane, NZ)

    queries = [
        pl.BlockSpec(
            (once, part_rows, width),
            lambda s, here, plane=plane, half=half: (s, half * NZ + which(here, plane), 0),
        )
        for plane, half, _ in blocks
    ]
    residual = [
        pl.BlockSpec((once, res // NZ, width), lambda s, here, plane=plane: (s, which(here, plane), 0))
        for plane, _, _ in blocks
    ]
    args = [q, q, g, g, x, x, k, v, *biases, o_w, o_b.reshape(1, -1), *held]
    return pl.pallas_call(
        functools.partial(row_kernel, blocks),
        out_shape=[jax.ShapeDtypeStruct((DAP, seqs * HALF_ROWS, width), jnp.bfloat16)] * len(halves),
        grid_spec=pltpu.PrefetchScalarGridSpec(
            num_scalar_prefetch=1,
            grid=(seqs // once,),
            in_specs=queries
            + queries
            + residual
            + [
                pl.BlockSpec((once, width, res), lambda s, here: (s, 0, 0)),
                pl.BlockSpec((once, res, width), lambda s, here: (s, 0, 0)),
            ]
            + [pl.BlockSpec(bias.shape, lambda s, here: (0, 0, 0, 0)) for bias in biases]
            + [
                pl.BlockSpec((width, width), lambda s, here: (0, 0)),
                pl.BlockSpec((1, width), lambda s, here: (0, 0)),
            ]
            + [pl.BlockSpec(memory_space=pl.ANY)] * len(held),
            out_specs=[pl.BlockSpec(memory_space=pl.ANY)] * len(halves),
            scratch_shapes=[
                pltpu.VMEM((2, GROUP * part_rows * len(blocks), res), jnp.float32),
                pltpu.VMEM((2, GROUP * part_rows * len(blocks), res), jnp.bfloat16),
                pltpu.VMEM(
                    (seqs // once, len(blocks), DAP // NZ, once * HALF_ROWS, width), jnp.bfloat16
                ),
                pltpu.SemaphoreType.DMA((seqs // once, len(blocks))),
            ],
        ),
        input_output_aliases={len(args) + 1 - len(held) + n: n for n in range(len(held))},
        compiler_params=pltpu.CompilerParams(vmem_limit_bytes=grant * MIB),
        cost_estimate=pl.CostEstimate(
            flops=seqs * H * part_rows * len(blocks) * res * 256 * 16,
            bytes_accessed=8 * 1024 * 1024,
            transcendentals=seqs * H * part_rows * len(blocks) * res,
        ),
        name="row_attention",
    )(here, *args)


def column_kernel(at_once, x_ref, gain, bias, w_ref, g_b, o_b, *refs):
    q_w, k_w, v_w, g_w, o_w = (w_ref.at[n] for n in range(5))
    out_ref, held, scores, weights = refs[-4:]
    step = pl.program_id(0)
    owners, per, width = x_ref.shape
    items = pl.num_programs(0) * at_once
    seqs = owners * per // items
    parts = width // LANES

    @pl.when(step == 0)
    def _():
        for part in range(parts):
            held[part] = x_ref[:, :, lanes_of(part)].astype(jnp.float32).reshape(-1, LANES)

    mine = [pl.ds(step * at_once + n, seqs, stride=items) for n in range(at_once)]
    x = jnp.concatenate(
        [jnp.concatenate([held[part, rows, :] for rows in mine], axis=0) for part in range(parts)], axis=1
    )
    normed = norm(x, gain[...], bias[...]).astype(jnp.bfloat16)
    q, k_t, v, g = project(normed, normed, q_w, k_w, v_w, g_w, g_b)
    gated = {}

    def place(n):
        return slice(n // parts * seqs, (n // parts + 1) * seqs), lanes_of(n % parts)

    def score(n):
        rows, lanes = place(n)
        scores[n % 2] = dot(stacked(q[rows, lanes]), k_t[lanes, rows])

    def soften(n, _):
        for low in range(0, GROUP * seqs, 32):
            weights[n % 2, low : low + 32] = softmax_rounded(scores[n % 2, low : low + 32])

    def average(n, _):
        rows, lanes = place(n)
        mixed = own_lanes(dot(weights[n % 2], v[rows, lanes]))
        gated[n] = (mixed * g[rows, lanes]).astype(jnp.bfloat16)

    pipelined(at_once * parts, score, soften, average)
    gated = [
        jnp.concatenate([gated[n * parts + part] for part in range(parts)], axis=1)
        for n in range(at_once)
    ]
    after = x + (dot(jnp.concatenate(gated, axis=0), o_w[...]) + o_b[...])
    for n, rows in enumerate(mine):
        for part in range(parts):
            held[part, rows, :] = after[n * seqs : (n + 1) * seqs, lanes_of(part)]

    @pl.when(step == pl.num_programs(0) - 1)
    def _():
        for part in range(parts):
            out_ref[:, :, lanes_of(part)] = (
                held[part].reshape(owners, per, LANES).astype(jnp.bfloat16)
            )


def column_attention(items, half, before, x, gain, bias, weights, g_b, o_b):
    width = x.shape[2]
    seqs = x.size // (items * width)
    at_once = 4
    whole = pl.BlockSpec(x.shape, lambda r: (0, 0, 0))
    vector = pl.BlockSpec((1, width), lambda r: (0, 0))
    weight = pl.BlockSpec((5, width, width), lambda r: (0, 0, 0))
    return pl.pallas_call(
        functools.partial(column_kernel, at_once),
        grid=(items // at_once,),
        out_shape=[jax.ShapeDtypeStruct((DAP, HALVES * x.shape[1], width), jnp.bfloat16)],
        in_specs=[whole, vector, vector, weight, vector, vector]
        + [pl.BlockSpec(memory_space=pl.ANY)] * len(before),
        out_specs=[pl.BlockSpec(x.shape, lambda r: (0, half, 0))],
        input_output_aliases={6: 0} if before else {},
        scratch_shapes=[
            pltpu.VMEM((width // LANES, seqs * items, LANES), jnp.float32),
            pltpu.VMEM((2, GROUP * seqs, seqs), jnp.float32),
            pltpu.VMEM((2, GROUP * seqs, seqs), jnp.bfloat16),
        ],
        compiler_params=pltpu.CompilerParams(vmem_limit_bytes=44 * MIB),
        name="column_attention",
    )(
        x, gain.reshape(1, -1), bias.reshape(1, -1), weights, g_b.reshape(1, -1), o_b.reshape(1, -1), *before
    )


def fetch(value, z=0, x=0, y=0):
    pairs = []
    for dz in range(NZ):
        for dx in range(NX):
            for dy in range(NY):
                src = ((dz + z) % NZ * NX + (dx + x) % NX) * NY + (dy + y) % NY
                pairs.append((src, (dz * NX + dx) * NY + dy))
    return lax.ppermute(value, "dap", pairs)


def join_kernel(*refs):
    count = len(refs) - 2
    parts, out_ref, sems = refs[:count], refs[count], refs[count + 1]
    place, copies = 0, []
    for n, part in enumerate(parts):
        size = part.shape[0]
        copies.append(pltpu.make_async_copy(part, out_ref.at[pl.ds(place, size)], sems.at[n]))
        place += size
    for copy in copies:
        copy.start()
    for copy in copies:
        copy.wait()


def join(*parts):
    total = sum(part.shape[0] for part in parts)
    return pl.pallas_call(
        join_kernel,
        out_shape=jax.ShapeDtypeStruct((total,) + parts[0].shape[1:], parts[0].dtype),
        in_specs=[pl.BlockSpec(memory_space=pl.ANY)] * len(parts),
        out_specs=pl.BlockSpec(memory_space=pl.ANY),
        scratch_shapes=[pltpu.SemaphoreType.DMA((len(parts),))],
        compiler_params=pltpu.CompilerParams(vmem_limit_bytes=4 * MIB),
        name="join",
    )(*parts)


def exchange(value):
    return lax.all_to_all(value, "dap", split_axis=0, concat_axis=0, tiled=True)


def per_device(
    alignment,
    pair_state,
    row_norm_gain,
    row_norm_bias,
    pair_norm_gain,
    pair_weight,
    row_query,
    row_key,
    row_value,
    row_gate,
    row_gate_bias,
    row_output,
    row_output_bias,
    column_norm_gain,
    column_norm_bias,
    column_query,
    column_key,
    column_value,
    column_gate,
    column_gate_bias,
    column_output,
    column_output_bias,
):
    seqs, res, width = alignment.shape
    own = res // DAP
    me = lax.axis_index("dap")
    here = jnp.stack([me // (NX * NY), me // NY % NX, me % NY]).astype(jnp.int32)
    local = pair_bias(pair_state, pair_norm_gain, pair_weight)[None]
    pair = join(local, fetch(local, y=1))
    near = [fetch(pair, x=step) for step in (1, 2, 3)]
    far_pair = fetch(pair, z=2)
    weights = stack(column_query, column_key, column_value, column_gate, column_output)
    near, weights = lax.optimization_barrier((near, weights))
    own_plane = join(pair, *near)
    own_plane, far_pair, gain = lax.optimization_barrier((own_plane, far_pair, row_norm_gain))
    ahead, behind = fetch(own_plane, z=1), fetch(own_plane, z=3)
    far_plane = join(far_pair, *(fetch(far_pair, x=step) for step in (1, 2, 3)))
    projected = row_project(
        alignment, gain, row_norm_bias, row_query, row_key, row_value, row_gate, row_gate_bias
    )

    def attend(blocks, biases, *held, grant=32):
        return row_attention(
            grant, blocks, here, *projected, alignment, biases, row_output, row_output_bias, held
        )

    after = attend(((0, 0, 0), (0, 1, 0)), [own_plane])
    after = attend(((2, 0, 0), (2, 1, 0)), [far_plane], *after)
    first = attend(((1, 0, 0), (3, 0, 1)), [ahead, behind], after[0])[0]
    second = attend(((1, 1, 0), (3, 1, 1)), [ahead, behind], after[1], grant=56)[0]
    first, second = lax.optimization_barrier((exchange(first), second))
    items = own // HALVES
    columns = ()
    for half, part in enumerate((first, exchange(second))):
        columns = column_attention(
            items,
            half,
            columns,
            part,
            column_norm_gain,
            column_norm_bias,
            weights,
            column_gate_bias,
            column_output_bias,
        )
    back = exchange(columns[0]).reshape(DAP, HALVES, seqs, items, width)
    return back.transpose(2, 0, 1, 3, 4).reshape(alignment.shape)


def solution(mesh):
    split = P(("batch", "dap"), None, None)
    return jax.shard_map(
        per_device,
        mesh=mesh,
        in_specs=(split, split) + (P(),) * 20,
        out_specs=split,
        check_vma=False,
    )
```
